128 devices in a mesh: dp: 16 (over z, y), ctx: 8 (over x, core).
Axes of the slice: x: 4, y: 4, z: 4, core: 2. Of those that a mesh axis runs over, the one named last changes fastest.
Arguments:
- tokens: bfloat16 [16384, 2048], P(('dp', 'ctx')), may hold values from -6 to 6
- cotangent: bfloat16 [16384, 2048], P(('dp', 'ctx')), may hold values from -6 to 6
- lengths: int32 [16, 4], P('dp'), may hold values from 0 to 1024, as said below
- spans: int32 [16, 8, 2], P('dp'), may hold values from 0 to 15, as said below
- gain_attn: bfloat16 [2048], P(('dp', 'ctx')), may hold values from 0.25 to 1.75
- w_query: bfloat16 [2048, 2048], P(('dp', 'ctx')), may hold values from -0.125 to 0.125
- w_key: bfloat16 [2048, 256], P(('dp', 'ctx')), may hold values from -0.125 to 0.125
- w_value: bfloat16 [2048, 256], P(('dp', 'ctx')), may hold values from -0.125 to 0.125
- w_out: bfloat16 [2048, 2048], P(('dp', 'ctx')), may hold values from -1.5 to 1.5
- gain_mlp: bfloat16 [2048], P(('dp', 'ctx')), may hold values from 0.25 to 1.75
- w_gate: bfloat16 [2048, 5632], P(('dp', 'ctx')), may hold values from -0.125 to 0.125
- w_up: bfloat16 [2048, 5632], P(('dp', 'ctx')), may hold values from -0.125 to 0.125
- w_down: bfloat16 [5632, 2048], P(('dp', 'ctx')), may hold values from -0.078125 to 0.078125
Outputs:
- block_out: bfloat16 [16384, 2048], P(('dp', 'ctx'))
- input_grad: float32 [16384, 2048], P(('dp', 'ctx'))
- grad_gain_attn: float32 [2048], P(('dp', 'ctx'))
- grad_query: float32 [2048, 2048], P(('dp', 'ctx'))
- grad_key: float32 [2048, 256], P(('dp', 'ctx'))
- grad_value: float32 [2048, 256], P(('dp', 'ctx'))
- grad_out: float32 [2048, 2048], P(('dp', 'ctx'))
- grad_gain_mlp: float32 [2048], P(('dp', 'ctx'))
- grad_gate: float32 [2048, 5632], P(('dp', 'ctx'))
- grad_up: float32 [2048, 5632], P(('dp', 'ctx'))
- grad_down: float32 [5632, 2048], P(('dp', 'ctx'))
The draws below stay inside these ranges and needn't reach their ends.
Inputs may be any that keep to these rules, and one draw needn't show every extreme that they name: Row g holds the lengths of group g's 4 packed sequences, which fill its 1024 places in order; the first or the last of them is 512 or longer, and some group holds one sequence of 1024. A group's 1024 places form 16 blocks of 64 in order; index r of ctx holds block spans[g, r, 0], of the first half, then block spans[g, r, 1], of the second half; each block is held once.
All inputs are finite; a program needn't handle non-finite values.
Results may differ from the reference program's by a relative error of at most 0.017.
Values may be sent and summed in bfloat16 or wider, within the bound.
A program may use at most 448 MiB of HBM per device.

```python
import jax
import jax.numpy as jnp
from jax import lax

D = 2048
HEADS = 32
KV_HEADS = 4
HEAD_DIM = 64
FF = 5632
TOK_DEV = 128
CAP = 1024
HALF = 512
TOKENS = 16384
N_DP = 16
N_CTX = 8


def draw_lengths(key, part):
    key = jax.random.fold_in(key, 11)
    keys_all = jax.random.split(key, 5)
    chosen = jax.random.randint(keys_all[0], (), 0, N_DP)
    longest = jax.random.randint(keys_all[1], (N_DP,), HALF, CAP + 1)
    longest = jnp.where(jnp.arange(N_DP) == chosen, CAP, longest)
    remain = CAP - longest
    cut_one = jax.random.randint(keys_all[2], (N_DP,), 0, remain + 1)
    cut_two = jax.random.randint(keys_all[3], (N_DP,), cut_one, remain + 1)
    others = jnp.stack([cut_one, cut_two - cut_one, remain - cut_two], 1)
    placed_first = jax.random.randint(keys_all[4], (N_DP,), 0, 2)
    first_form = jnp.concatenate([longest[:, None], others], 1)
    last_form = jnp.concatenate([others, longest[:, None]], 1)
    return jnp.where(placed_first[:, None] == 1, first_form, last_form).astype(jnp.int32)


def draw_spans(key, part):
    key = jax.random.fold_in(key, 23)
    early_keys = jax.random.split(jax.random.fold_in(key, 1), N_DP)
    late_keys = jax.random.split(jax.random.fold_in(key, 2), N_DP)

    def shuffle(one_key):
        return jax.random.permutation(one_key, N_CTX)
    early = jax.vmap(shuffle)(early_keys)
    late = jax.vmap(shuffle)(late_keys) + N_CTX
    return jnp.stack([early, late], -1).astype(jnp.int32)


def block_levels(rng, extent, shards, least, top_value):
    gain, own = 1.0, jax.random.fold_in(rng, 6)
    for dim, blocks in shards:
        steps = jnp.exp(jax.random.uniform(jax.random.fold_in(own, dim), (blocks,), jnp.float32, least / len(shards), top_value / len(shards)))
        gain = gain * jnp.repeat(steps, extent[dim] // blocks).reshape([-1 if axis == dim else 1 for axis in range(len(extent))])
    return gain


def gaussian(own_key, dims, width, reach, cuts=(), kind=jnp.bfloat16):
    array = jax.random.normal(own_key, dims, jnp.float32) * width
    if len(cuts) > 0:
        array = block_levels(own_key, dims, cuts, -0.22, 0.18) * array
    return jnp.clip(array, min=-reach, max=reach).astype(kind)


def setup_inputs(seed: int = 0) -> dict:
    keys = jax.random.split(jax.random.key(seed), 14)
    tokens = gaussian(keys[0], (TOKENS, D), 1.0, 6.0, ((0, 128),))
    cotangent = gaussian(keys[1], (TOKENS, D), 1.0, 6.0, ((0, 128),))
    lengths = draw_lengths(jax.random.fold_in(keys[13], 71), 0)
    spans = draw_spans(jax.random.fold_in(keys[13], 71), 0)
    gain_attn = jnp.clip(1.0 + 0.15 * jax.random.normal(keys[4], (D,), jnp.float32), 0.25, 1.75).astype(jnp.bfloat16)
    w_query = gaussian(keys[5], (D, D), D ** -0.5, 0.125, ((0, 128),))
    w_key = gaussian(keys[6], (D, KV_HEADS * HEAD_DIM), D ** -0.5, 0.125, ((0, 128),))
    w_value = gaussian(keys[7], (D, KV_HEADS * HEAD_DIM), D ** -0.5, 0.125, ((0, 128),))
    w_out = gaussian(keys[8], (D, D), (max(D // 128, 1)) ** -0.5, 1.5, ((0, 128),))
    gain_mlp = jnp.clip(1.0 + 0.15 * jax.random.normal(keys[9], (D,), jnp.float32), 0.25, 1.75).astype(jnp.bfloat16)
    w_gate = gaussian(keys[10], (D, FF), D ** -0.5, 0.125, ((0, 128),))
    w_up = gaussian(keys[11], (D, FF), D ** -0.5, 0.125, ((0, 128),))
    w_down = gaussian(keys[12], (FF, D), FF ** -0.5, 0.078125, ((0, 128),))
    return dict(tokens=tokens, cotangent=cotangent, lengths=lengths, spans=spans, gain_attn=gain_attn, w_query=w_query, w_key=w_key, w_value=w_value, w_out=w_out, gain_mlp=gain_mlp, w_gate=w_gate, w_up=w_up, w_down=w_down)


@jax.custom_vjp
def low(v):
    return lax.optimization_barrier(v.astype(jnp.bfloat16)).astype(jnp.float32)

@jax.custom_vjp
def low_back(v):
    return v

def low_keep(v):
    return (low(v), None)

def low_pass(kept, grad):
    return (grad,)

def back_keep(v):
    return (v, None)

def back_low(kept, grad):
    return (low(grad),)
low.defvjp(low_keep, low_pass)
low_back.defvjp(back_keep, back_low)
EPSILON = 1e-05
NEG_LARGE = -1e+30
PRECISE = lax.Precision.HIGHEST

def matmul(left_op, right_op):
    return jnp.dot(left_op, right_op, precision=PRECISE, preferred_element_type=jnp.float32)

def rope_tables(position):
    inverse = jnp.power(jnp.float32(10000.0), -jnp.arange(0, HEAD_DIM, 2).astype(jnp.float32) / HEAD_DIM)
    angles = position.astype(jnp.float32)[:, None] * inverse[None, :]
    return (jnp.cos(angles)[:, None, :], jnp.sin(angles)[:, None, :])

def rotate(values, cos_table, sin_table):
    half_dim = values.shape[-1] // 2
    leading = values[..., :half_dim]
    trailing = values[..., half_dim:]
    return jnp.concatenate([leading * cos_table - trailing * sin_table, trailing * cos_table + leading * sin_table], -1)

def rms_scale(values):
    return lax.rsqrt(lax.optimization_barrier(jnp.mean(values * values, -1, keepdims=True)) + EPSILON)

def group_layout(length_row, span_row):
    row_ids = jnp.arange(CAP, dtype=jnp.int32)
    span_len = TOK_DEV // 2
    span_ids = span_row.reshape(-1)[row_ids // span_len]
    packed = span_ids * span_len + row_ids % span_len
    seq_ends = jnp.cumsum(length_row).astype(jnp.int32)
    before = seq_ends[None, :] <= packed[:, None]
    doc_ids = lax.optimization_barrier(jnp.sum(before.astype(jnp.int32), 1))
    starts = lax.optimization_barrier(jnp.sum(jnp.where(before, length_row[None, :], 0), 1)).astype(jnp.int32)
    return (packed, doc_ids, packed - starts)

def group_forward(tokens, gain_attn, w_query, w_key, w_value, w_out, gain_mlp, w_gate, w_up, w_down, packed, doc_ids, position):
    kv_groups = HEADS // KV_HEADS
    cos_table, sin_table = rope_tables(position)
    normed = low(tokens * rms_scale(tokens) * gain_attn)
    query_rows = low_back(matmul(normed, w_query)).reshape(CAP, HEADS, HEAD_DIM)
    key_rows = low_back(matmul(normed, w_key)).reshape(CAP, KV_HEADS, HEAD_DIM)
    value_rows = low_back(low(matmul(normed, w_value))).reshape(CAP, KV_HEADS, HEAD_DIM)
    query_rows = low(rotate(query_rows, cos_table, sin_table))
    key_rows = low(rotate(key_rows, cos_table, sin_table))
    allowed = (doc_ids[:, None] == doc_ids[None, :]) & (packed[None, :] <= packed[:, None])

    def one_head(operands):
        queries, key_block, values = operands
        scores = jnp.einsum('gqd,kd->gqk', queries, key_block, precision=PRECISE) * HEAD_DIM ** (-0.5)
        scores = low_back(jnp.where(allowed[None], scores, NEG_LARGE))
        weights = jax.nn.softmax(scores, axis=-1)
        return jnp.einsum('gqk,kd->gqd', low(weights), values, precision=PRECISE)
    queries = query_rows.reshape(CAP, KV_HEADS, kv_groups, HEAD_DIM).transpose(1, 2, 0, 3)
    key_heads = key_rows.transpose(1, 0, 2)
    value_heads = value_rows.transpose(1, 0, 2)
    attended = lax.map(jax.checkpoint(one_head), (queries, key_heads, value_heads))
    attended = low_back(low(attended.transpose(2, 0, 1, 3).reshape(CAP, D)))
    hidden = tokens + low_back(matmul(attended, w_out))
    normed_mlp = low(hidden * rms_scale(hidden) * gain_mlp)
    gate_act = low_back(matmul(normed_mlp, w_gate))
    up_act = low_back(matmul(normed_mlp, w_up))
    inner_act = low(jax.nn.silu(gate_act) * up_act)
    return hidden + low_back(matmul(inner_act, w_down))

def reference(tokens, cotangent, lengths, spans, gain_attn, w_query, w_key, w_value, w_out, gain_mlp, w_gate, w_up, w_down):
    params = tuple((array_in.astype(jnp.float32) for array_in in (gain_attn, w_query, w_key, w_value, w_out, gain_mlp, w_gate, w_up, w_down)))
    inputs = tokens.astype(jnp.float32).reshape(N_DP, CAP, D)
    seeds = cotangent.astype(jnp.float32).reshape(N_DP, CAP, D)

    def per_group(totals, operands):
        block_in, block_cot, length_row, span_row = operands
        packed, doc_ids, position = group_layout(length_row, span_row)

        def forward(block_tokens, *weights_all):
            return group_forward(block_tokens, *weights_all, packed, doc_ids, position)
        outputs, pullback = jax.vjp(forward, block_in, *params)
        gradients = pullback(block_cot)
        totals = tuple((running + gradient for running, gradient in zip(totals, gradients[1:])))
        return (totals, (outputs, gradients[0]))
    init = tuple((jnp.zeros_like(array_in) for array_in in params))
    totals, (outputs, input_grads) = lax.scan(per_group, init, (inputs, seeds, lengths, spans))
    return (outputs.reshape(TOKENS, D).astype(jnp.bfloat16), input_grads.reshape(TOKENS, D), totals[0], totals[1], totals[2], totals[3], totals[4], totals[5], totals[6], totals[7], totals[8])
```

```python
import jax
import jax.numpy as jnp
from jax import lax
from jax.experimental import pallas as pl
from jax.experimental.pallas import tpu as pltpu
from jax.sharding import PartitionSpec as P

D = 2048
HEADS = 32
KV_HEADS = 4
HEAD_DIM = 64
FF = 5632
N_CTX = 8
N_DP = 16
ROWS = 128
GROUP = 1024
Q_LOC = 256
QKV_LOC = 384
FF_PART = 44
FF_PAD = 48
FF_LOC = N_DP * FF_PAD
EPSILON = 1e-05
NEG_LARGE = -1e30
MESH = pl.DeviceIdType.MESH
BF = jnp.bfloat16
F32 = jnp.float32
ANY = pl.BlockSpec(memory_space=pl.ANY)
VM = pl.BlockSpec(memory_space=pltpu.VMEM)
ACROSS = (((1,), (1,)), ((), ()))
DOWNWARD = (((0,), (0,)), ((), ()))


class Place:
    def __init__(self):
        self.d = lax.axis_index("dp")
        self.c = lax.axis_index("ctx")
        self.z, self.y = lax.div(self.d, 4), lax.rem(self.d, 4)
        self.x, self.k = lax.div(self.c, 2), lax.rem(self.c, 2)

    def at_x(self, step):
        return lax.rem(self.x + step, 4)

    def on_x(self, step):
        return (self.d, self.at_x(step) * 2 + self.k)

    def sibling(self):
        return (self.d, self.x * 2 + 1 - self.k)

    def on_ctx(self, step):
        return (self.d, lax.rem(self.c + step, 8))

    def on_y(self, step):
        return (self.z * 4 + lax.rem(self.y + step, 4), self.c)

    def on_z(self, step):
        return (lax.rem(self.z + step, 4) * 4 + self.y, self.c)

    def moved_to(self):
        flat = self.d * 8 + self.c
        return (lax.rem(flat, 16), lax.div(flat, 16))

    def moved_from(self):
        flat = self.c * 16 + self.d
        return (lax.div(flat, 8), lax.rem(flat, 8))

    def moves(self):
        return self.d * 8 + self.c != self.c * 16 + self.d


class Copies:
    def __init__(self, send_sems, recv_sems):
        self.send_sems, self.recv_sems, self.used, self.started = send_sems, recv_sems, 0, []

    def make(self, src, dst, device):
        i = self.used
        self.used += 1
        return pltpu.make_async_remote_copy(
            src_ref=src,
            dst_ref=dst,
            send_sem=self.send_sems.at[i],
            recv_sem=self.recv_sems.at[i],
            device_id=device,
            device_id_type=MESH,
        )

    def send(self, src, dst, device):
        copy = self.make(src, dst, device)
        copy.start()
        self.started.append(copy)
        return copy

    def finish(self):
        for copy in self.started:
            copy.wait_send()


def greet(peers, extra=None, extra_on=None):
    barrier = pltpu.get_barrier_semaphore()
    for peer in peers:
        pl.semaphore_signal(barrier, 1, device_id=peer, device_id_type=MESH)
    count = len(peers)
    if extra is not None:

        @pl.when(extra_on)
        def _():
            pl.semaphore_signal(barrier, 1, device_id=extra, device_id_type=MESH)

        count = jnp.where(extra_on, count + 1, count)
    pl.semaphore_wait(barrier, count)


def yz_peers(me):
    return [me.on_y(s) for s in (1, 2, 3)] + [me.on_z(s) for s in (1, 2, 3)]


def ctx_peers(me):
    return [me.on_ctx(s) for s in range(1, 8)]


def x_peers(me):
    return [me.on_x(1), me.on_x(3), me.sibling()]


def round_robin(*flows):
    flows = list(flows)
    while flows:
        flows = [f for f in flows if next(f, "end") != "end"]


def ctx_gather(me, copies, src, full, local_sem):
    own, left, right, far = (me.at_x(s) * 2 + me.k for s in (0, 3, 1, 2))
    to_right, to_left, to_sib = me.on_x(1), me.on_x(3), me.sibling()
    top, low = pl.ds(0, 64), pl.ds(64, 64)
    r1 = copies.send(src.at[top], full.at[own, top], to_right)
    l1 = copies.send(src.at[low], full.at[own, low], to_left)
    s0 = copies.send(src, full.at[own], to_sib)
    r2 = copies.send(src.at[low], full.at[own, low], to_right)
    l2 = copies.send(src.at[top], full.at[own, top], to_left)
    mine = pltpu.make_async_copy(src, full.at[own], local_sem)
    mine.start()
    yield
    r1.wait_recv()
    r3 = copies.send(full.at[left, top], full.at[left, top], to_right)
    l1.wait_recv()
    l3 = copies.send(full.at[right, low], full.at[right, low], to_left)
    yield
    r2.wait_recv()
    s1 = copies.send(full.at[left], full.at[left], to_sib)
    l2.wait_recv()
    s2 = copies.send(full.at[right], full.at[right], to_sib)
    yield
    r3.wait_recv()
    s3 = copies.send(full.at[far, top], full.at[far, top], to_sib)
    l3.wait_recv()
    s4 = copies.send(full.at[far, low], full.at[far, low], to_sib)
    yield
    for s in (s0, s1, s2, s3, s4):
        s.wait_recv()
    mine.wait()


def add_rows(dst, rows, *terms):
    def step(i, carry):
        at = pl.ds(pl.multiple_of(i * 16, 16), 16)
        total = terms[0](at).astype(F32)
        for term in terms[1:]:
            total += term(at).astype(F32)
        dst[at, :] = total.astype(dst.dtype)
        return carry

    lax.fori_loop(0, rows // 16, step, 0)


def ctx_scatter(me, copies, part, pair, half_left, half_right, from_left, from_right):
    to_right, to_left, to_sib = me.on_x(1), me.on_x(3), me.sibling()
    top, low = pl.ds(0, 64), pl.ds(64, 64)
    arriving = {}
    for s in (2, 1, 3, 0):
        arriving[s] = copies.send(part.at[me.at_x(s) * 2 + 1 - me.k], pair.at[s], to_sib)
    yield

    def merge(s):
        arriving[s].wait_recv()
        block = me.at_x(s) * 2 + me.k
        add_rows(pair.at[s], 128, lambda at: part[block, at, :], lambda at: pair[s, at, :])

    merge(2)
    a = copies.send(pair.at[2, top], half_left, to_right)
    b = copies.send(pair.at[2, low], half_right, to_left)
    merge(1)
    r1 = copies.send(pair.at[1, low], from_left.at[low], to_right)
    merge(3)
    l1 = copies.send(pair.at[3, top], from_right.at[top], to_left)
    merge(0)
    yield
    a.wait_recv()
    add_rows(half_left, 64, lambda at: half_left[at, :], lambda at: pair[1, at, :])
    r2 = copies.send(half_left, from_left.at[top], to_right)
    b.wait_recv()
    add_rows(
        half_right,
        64,
        lambda at: half_right[at, :],
        lambda at: pair.at[3, low][at, :],
    )
    l2 = copies.send(half_right, from_right.at[low], to_left)
    yield
    for copy in (r1, l1, r2, l2):
        copy.wait_recv()


SCATTER_SCRATCH = [
    pltpu.VMEM((4, 128, D), BF),
    pltpu.VMEM((64, D), BF),
    pltpu.VMEM((64, D), BF),
    pltpu.VMEM((128, D), BF),
    pltpu.VMEM((128, D), BF),
]


def scattered(at, pair, from_left, from_right):
    return (
        pair[0, at, :].astype(F32) + from_left[at, :].astype(F32) + from_right[at, :].astype(F32)
    )


def halves(ref, half, by_rows):
    shape = ref.shape
    if by_rows:
        n = shape[-3]
        return ref.at[(*(slice(None),) * (len(shape) - 3), pl.ds(half * (n // 2), n // 2))]
    columns = shape[-1]
    return ref.at[
        (*(slice(None),) * (len(shape) - 1), pl.ds(half * (columns // 2), columns // 2))
    ]


def dp_axes(me, half):
    z = (me.z, me.on_z)
    y = (me.y, me.on_y)
    return (y, z) if half else (z, y)


def dp_gather(me, copies, full, half, by_rows):
    view = halves(full, half, by_rows)
    (p2, dev2), (p1, dev1) = dp_axes(me, half)

    def group(i2, j1):
        return view.at[j1, i2] if half else view.at[i2, j1]

    own = group(p2, p1)
    first = [copies.send(own, own, dev1(s)) for s in (1, 3, 2)]
    yield
    for copy in first:
        copy.wait_recv()
    every, lo, hi = pl.ds(0, 4), pl.ds(0, 2), pl.ds(2, 2)
    mine = group(p2, every)
    up = copies.send(mine, mine, dev2(1))
    down = copies.send(mine, mine, dev2(3))
    yield
    up.wait_recv()
    passed = group(lax.rem(p2 + 3, 4), lo)
    up2 = copies.send(passed, passed, dev2(1))
    down.wait_recv()
    passed = group(lax.rem(p2 + 1, 4), hi)
    down2 = copies.send(passed, passed, dev2(3))
    yield
    up2.wait_recv()
    down2.wait_recv()


def add_blocks(dst, *terms):
    lead = dst.shape[:-2]
    if not lead:
        total = terms[0][...].astype(F32)
        for term in terms[1:]:
            total += term[...].astype(F32)
        dst[...] = total.astype(dst.dtype)
        return

    def step(i, carry):
        at = (lax.div(i, lead[1]), lax.rem(i, lead[1])) if len(lead) == 2 else (i,)
        total = terms[0][at].astype(F32)
        for term in terms[1:]:
            total += term[at].astype(F32)
        dst[at] = total.astype(dst.dtype)
        return carry

    lax.fori_loop(0, lead[0] * (lead[1] if len(lead) == 2 else 1), step, 0)


def dp_scatter(me, copies, part, half, by_rows, out, pass_up, pass_down, from_up, from_down, last):
    view = halves(part, half, by_rows)
    (p1, dev1), (p2, dev2) = dp_axes(me, half)

    def group(i1, j2):
        return view.at[j2, i1] if half else view.at[i1, j2]

    every, lo, hi = pl.ds(0, 4), pl.ds(0, 2), pl.ds(2, 2)
    nxt, far, prv = (lax.rem(p1 + s, 4) for s in (1, 2, 3))
    a = copies.send(group(far, lo), pass_up, dev1(1))
    b = copies.send(group(far, hi), pass_down, dev1(3))
    e1 = copies.send(group(nxt, hi), from_up.at[hi], dev1(1))
    e2 = copies.send(group(prv, lo), from_down.at[lo], dev1(3))
    yield
    a.wait_recv()
    add_blocks(pass_up, pass_up, group(nxt, lo))
    f1 = copies.send(pass_up, from_up.at[lo], dev1(1))
    b.wait_recv()
    add_blocks(pass_down, pass_down, group(prv, hi))
    f2 = copies.send(pass_down, from_down.at[hi], dev1(3))
    yield
    for copy in (e1, e2, f1, f2):
        copy.wait_recv()
    add_blocks(from_up, from_up, from_down, group(p1, every))
    sent = [
        copies.send(from_up.at[lax.rem(p2 + s, 4)], last.at[s - 1], dev2(s)) for s in (1, 2, 3)
    ]
    yield
    for copy in sent:
        copy.wait_recv()
    add_blocks(halves(out, half, by_rows), from_up.at[p2], last.at[0], last.at[1], last.at[2])


def dp_scatter_scratch(block, by_rows):
    block = (block[0] // 2, *block[1:]) if by_rows else (*block[:-1], block[-1] // 2)
    return [pltpu.VMEM((lead, *block), BF) for lead in (2, 2, 4, 4, 3)] * 2


def start_kernel(
    qkv_src, gu_src, out_src, dn_src, n1, n1_full, w_qkv, w_out, gu_own, dn_own, ss, rs, ls
):
    me = Place()
    greet(ctx_peers(me) + yz_peers(me), me.moved_from(), me.moves())
    copies = Copies(ss, rs)
    home = w_qkv.at[me.z, me.y]
    qkv_in = [
        copies.send(qkv_src.at[lax.rem(me.c + s, 8)], home.at[me.c], me.on_ctx(s))
        for s in range(1, 8)
    ]
    qkv_mine = pltpu.make_async_copy(qkv_src.at[me.c], home.at[me.c], ls.at[0])
    qkv_mine.start()
    out_home = w_out.at[me.z, me.y]
    there = me.moved_to()
    move_out = copies.make(out_src, w_out.at[lax.div(there[0], 4), lax.rem(there[0], 4)], there)
    move_dn = copies.make(dn_src, dn_own, there)
    keep_out = pltpu.make_async_copy(out_src, out_home, ls.at[1])
    keep_dn = pltpu.make_async_copy(dn_src, dn_own, ls.at[2])

    @pl.when(me.moves())
    def _():
        move_out.start()
        move_dn.start()

    @pl.when(jnp.logical_not(me.moves()))
    def _():
        keep_out.start()
        keep_dn.start()

    rows = ctx_gather(me, copies, n1, n1_full, ls.at[3])
    next(rows)
    gu_in = [
        copies.send(gu_src.at[lax.rem(me.c + s, 8)], gu_own.at[me.c], me.on_ctx(s))
        for s in range(1, 8)
    ]
    gu_mine = pltpu.make_async_copy(gu_src.at[me.c], gu_own.at[me.c], ls.at[4])
    gu_mine.start()
    for copy in qkv_in:
        copy.wait_recv()
    qkv_mine.wait()
    flows = [dp_gather(me, copies, w_qkv, h, True) for h in (0, 1)]
    for flow in flows:
        next(flow)

    @pl.when(me.moves())
    def _():
        move_out.wait()
        move_dn.wait()

    @pl.when(jnp.logical_not(me.moves()))
    def _():
        keep_out.wait()
        keep_dn.wait()

    flows += [dp_gather(me, copies, w_out, h, False) for h in (0, 1)]
    round_robin(*flows, rows)
    for copy in gu_in:
        copy.wait_recv()
    gu_mine.wait()
    copies.finish()


def middle_kernel(
    part, tokens, cot, gu_own, dn_own, h1, n2_full, cot_full, w_gu, w_dn,
    n2, pair, half_left, half_right, from_left, from_right, ss, rs, ls,
):
    me = Place()
    greet(x_peers(me) + yz_peers(me))
    copies = Copies(ss, rs)
    keep_gu = pltpu.make_async_copy(gu_own, w_gu.at[me.z, me.y], ls.at[0])
    keep_dn = pltpu.make_async_copy(dn_own, w_dn.at[me.z, me.y], ls.at[1])
    keep_gu.start()
    keep_dn.start()
    rows = ctx_scatter(me, copies, part, pair, half_left, half_right, from_left, from_right)
    next(rows)
    keep_gu.wait()
    keep_dn.wait()
    flows = [dp_gather(me, copies, w_gu, h, True) for h in (0, 1)]
    for flow in flows:
        next(flow)
    next(rows)
    flows += [dp_gather(me, copies, w_dn, h, False) for h in (0, 1)]
    for flow in flows[2:]:
        next(flow)
    seeds = ctx_gather(me, copies, cot, cot_full, ls.at[2])
    next(seeds)
    next(rows)
    for flow in flows:
        next(flow)
    for _ in rows:
        pass

    def norm(i, carry):
        at = pl.ds(pl.multiple_of(i * 16, 16), 16)
        hidden = tokens[at, :].astype(F32) + scattered(at, pair, from_left, from_right)
        scale = lax.rsqrt(jnp.mean(hidden * hidden, -1, keepdims=True) + EPSILON)
        h1[at, :] = hidden
        n2[at, :] = (hidden * scale).astype(BF)
        return carry

    lax.fori_loop(0, 8, norm, 0)
    normed = ctx_gather(me, copies, n2, n2_full, ls.at[3])
    next(normed)
    round_robin(seeds, normed, *flows)
    copies.finish()


def back_kernel(
    part_u, part_y, h1, cot, g_gu, g_dn, out, dh1, da_full, ret_gu, ret_dn,
    da, own_gu, own_dn, *rest,
):
    ss, rs, ls = rest[-3:]
    scr_u, scr_y = rest[0:5], rest[5:10]
    scr_gu, scr_dn = rest[10:20], rest[20:30]
    me = Place()
    greet(ctx_peers(me) + yz_peers(me), me.moved_to(), me.moves())
    copies = Copies(ss, rs)
    rows_u = ctx_scatter(me, copies, part_u, *scr_u)
    next(rows_u)
    flows = [
        dp_scatter(me, copies, g_gu, h, True, own_gu, *scr_gu[h * 5 : h * 5 + 5]) for h in (0, 1)
    ]
    for flow in flows:
        next(flow)
    next(rows_u)
    flows_dn = [
        dp_scatter(me, copies, g_dn, h, False, own_dn, *scr_dn[h * 5 : h * 5 + 5]) for h in (0, 1)
    ]
    for flow in flows_dn:
        next(flow)
    next(rows_u)
    rows_y = ctx_scatter(me, copies, part_y, *scr_y)
    next(rows_y)
    for flow in flows:
        next(flow)
    for _ in rows_u:
        pass

    def norm_back(i, carry):
        at = pl.ds(pl.multiple_of(i * 16, 16), 16)
        hidden = h1[at, :]
        scale = lax.rsqrt(jnp.mean(hidden * hidden, -1, keepdims=True) + EPSILON)
        u = scattered(at, scr_u[0], scr_u[3], scr_u[4])
        grad = (
            cot[at, :].astype(F32)
            + scale * u
            - hidden * (scale * scale * scale * jnp.mean(u * hidden, -1, keepdims=True))
        )
        dh1[at, :] = grad
        da[at, :] = grad.astype(BF)
        return carry

    lax.fori_loop(0, 8, norm_back, 0)
    rows_da = ctx_gather(me, copies, da, da_full, ls.at[0])
    next(rows_da)
    round_robin(rows_y, rows_da, *flows, *flows_dn)
    gu_in = [
        copies.send(own_gu.at[lax.rem(me.c + s, 8)], ret_gu.at[me.c], me.on_ctx(s))
        for s in range(1, 8)
    ]
    gu_mine = pltpu.make_async_copy(own_gu.at[me.c], ret_gu.at[me.c], ls.at[1])
    gu_mine.start()
    move_dn = copies.make(own_dn, ret_dn, me.moved_from())
    keep_dn = pltpu.make_async_copy(own_dn, ret_dn, ls.at[2])

    @pl.when(me.moves())
    def _():
        move_dn.start()

    @pl.when(jnp.logical_not(me.moves()))
    def _():
        keep_dn.start()

    def finish(i, carry):
        at = pl.ds(pl.multiple_of(i * 16, 16), 16)
        out[at, :] = (h1[at, :] + scattered(at, scr_y[0], scr_y[3], scr_y[4])).astype(BF)
        return carry

    lax.fori_loop(0, 8, finish, 0)
    for copy in gu_in:
        copy.wait_recv()
    gu_mine.wait()

    @pl.when(me.moves())
    def _():
        move_dn.wait()

    @pl.when(jnp.logical_not(me.moves()))
    def _():
        keep_dn.wait()

    copies.finish()


def end_kernel(
    part, tokens, dh1, g_qkv, g_out, grad, ret_qkv, ret_out, own_qkv, own_out, *rest
):
    ss, rs, ls = rest[-3:]
    scr, scr_qkv, scr_out = rest[0:5], rest[5:15], rest[15:25]
    me = Place()
    greet(ctx_peers(me) + yz_peers(me), me.moved_to(), me.moves())
    copies = Copies(ss, rs)
    rows = ctx_scatter(me, copies, part, *scr)
    next(rows)
    flows = [
        dp_scatter(me, copies, g_qkv, h, True, own_qkv, *scr_qkv[h * 5 : h * 5 + 5]) for h in (0, 1)
    ] + [
        dp_scatter(me, copies, g_out, h, False, own_out, *scr_out[h * 5 : h * 5 + 5])
        for h in (0, 1)
    ]
    round_robin(rows, *flows)
    qkv_in = [
        copies.send(own_qkv.at[lax.rem(me.c + s, 8)], ret_qkv.at[me.c], me.on_ctx(s))
        for s in range(1, 8)
    ]
    qkv_mine = pltpu.make_async_copy(own_qkv.at[me.c], ret_qkv.at[me.c], ls.at[0])
    qkv_mine.start()
    move_out = copies.make(own_out, ret_out, me.moved_from())
    keep_out = pltpu.make_async_copy(own_out, ret_out, ls.at[1])

    @pl.when(me.moves())
    def _():
        move_out.start()

    @pl.when(jnp.logical_not(me.moves()))
    def _():
        keep_out.start()

    def finish(i, carry):
        at = pl.ds(pl.multiple_of(i * 16, 16), 16)
        x = tokens[at, :].astype(F32)
        scale = lax.rsqrt(jnp.mean(x * x, -1, keepdims=True) + EPSILON)
        u = scattered(at, scr[0], scr[3], scr[4])
        grad[at, :] = (
            dh1[at, :]
            + scale * u
            - x * (scale * scale * scale * jnp.mean(u * x, -1, keepdims=True))
        )
        return carry

    lax.fori_loop(0, 8, finish, 0)
    for copy in qkv_in:
        copy.wait_recv()
    qkv_mine.wait()

    @pl.when(me.moves())
    def _():
        move_out.wait()

    @pl.when(jnp.logical_not(me.moves()))
    def _():
        keep_out.wait()

    copies.finish()


def call(kernel, number, ins, in_specs, outs, out_specs, scratch, n_copies, n_local):
    return pl.pallas_call(
        kernel,
        out_shape=[jax.ShapeDtypeStruct(*o) for o in outs],
        in_specs=in_specs,
        out_specs=out_specs,
        scratch_shapes=[
            *scratch,
            pltpu.SemaphoreType.DMA((n_copies,)),
            pltpu.SemaphoreType.DMA((n_copies,)),
            pltpu.SemaphoreType.DMA((n_local,)),
        ],
        compiler_params=pltpu.CompilerParams(
            collective_id=number, has_side_effects=True, vmem_limit_bytes=56 << 20
        ),
        name=kernel.__name__,
    )(*ins)


def rope_tables(position):
    inverse = jnp.power(F32(10000.0), -jnp.arange(0, HEAD_DIM, 2).astype(F32) / HEAD_DIM)
    angles = position.astype(F32)[:, None] * inverse[None, :]
    return (jnp.cos(angles)[:, None, :], jnp.sin(angles)[:, None, :])


def rotate(values, cos_table, sin_table):
    half_dim = values.shape[-1] // 2
    leading = values[..., :half_dim]
    trailing = values[..., half_dim:]
    return jnp.concatenate(
        [leading * cos_table - trailing * sin_table, trailing * cos_table + leading * sin_table], -1
    )


def contract(left_op, right_op, dims_pair):
    return lax.dot_general(left_op, right_op, dims_pair, preferred_element_type=F32)


def spread():
    place = jnp.arange(FF // N_CTX, dtype=jnp.int32)
    place = FF_PAD * (place // FF_PART) + place % FF_PART
    return place[:, None] == jnp.arange(FF_LOC, dtype=jnp.int32)[None, :]


def per_device(
    tokens, cotangent, lengths, spans, gain_attn, w_query, w_key, w_value, w_out, gain_mlp,
    w_gate, w_up, w_down,
):
    row_ids = jnp.arange(GROUP, dtype=jnp.int32)
    slot_ids = jnp.arange(2 * N_CTX, dtype=jnp.int32)
    table = spans.reshape(-1)
    span_ids = jnp.sum(
        jnp.where((row_ids // 64)[:, None] == slot_ids[None, :], table[None, :], 0), 1
    )
    packed = span_ids * 64 + row_ids % 64
    length_row = lengths[0]
    seq_ends = jnp.cumsum(length_row)
    before = seq_ends[None, :] <= packed[:, None]
    doc_ids = jnp.sum(before.astype(jnp.int32), 1)
    position = packed - jnp.sum(jnp.where(before, length_row[None, :], 0), 1)
    allowed = (doc_ids[:, None] == doc_ids[None, :]) & (packed[None, :] <= packed[:, None])
    cos_table, sin_table = rope_tables(position)

    gain_a = gain_attn.astype(F32)[:, None]
    gain_m = gain_mlp.astype(F32)[:, None]
    hot = spread()

    def scaled(w, gain):
        return (w.astype(F32) * gain).astype(BF)

    by_index = lambda w, n: w.reshape(16, n, -1).transpose(1, 0, 2)
    twice = lambda w: jnp.repeat(by_index(w, 4), 2, axis=0)
    qkv_src = jnp.concatenate(
        [
            by_index(scaled(w_query, gain_a), 8),
            twice(scaled(w_key, gain_a)),
            twice(scaled(w_value, gain_a)),
        ],
        -1,
    )

    def padded(w):
        cut = by_index(scaled(w, gain_m), 8)
        return contract(cut.reshape(128, -1), hot.astype(BF), (((1,), (0,)), ((), ()))).astype(
            BF
        ).reshape(8, 16, FF_LOC)

    gu_src = jnp.concatenate([padded(w_gate), padded(w_up)], -1)
    dn_src = jnp.pad(w_down, ((0, FF_PAD - FF_PART), (0, 0))).reshape(3, 16, D)
    tokens_f = tokens.astype(F32)
    scale_attn = lax.rsqrt(jnp.mean(tokens_f * tokens_f, -1, keepdims=True) + EPSILON)
    n1_own = (tokens_f * scale_attn).astype(BF)

    n1, wf_qkv, wf_out, gu_own, dn_own = call(
        start_kernel, 1,
        (qkv_src, gu_src, w_out, dn_src, n1_own), [ANY] * 5,
        [((8, 128, D), BF), ((4, 4, 8, 16, QKV_LOC), BF), ((4, 4, 16, D), BF),
         ((8, 16, 2 * FF_LOC), BF), ((3, 16, D), BF)],
        [ANY] * 5, [], 64, 5,
    )
    n1 = n1.reshape(GROUP, D)
    wf_qkv = wf_qkv.reshape(D, QKV_LOC)
    wf_out = wf_out.reshape(Q_LOC, D)

    heads = HEADS // N_CTX
    score_scale = HEAD_DIM ** (-0.5)
    qkv = jnp.dot(n1, wf_qkv, preferred_element_type=F32)
    q = rotate(qkv[:, :Q_LOC].reshape(GROUP, heads, HEAD_DIM), cos_table, sin_table).astype(BF)
    k = rotate(qkv[:, Q_LOC : Q_LOC + 64].reshape(GROUP, 1, HEAD_DIM), cos_table, sin_table)
    k = k.astype(BF)[:, 0]
    v = qkv[:, Q_LOC + 64 :].astype(BF)

    def scores_of():
        raw = jnp.einsum("qgd,nd->gqn", q, k, preferred_element_type=F32) * score_scale
        return jnp.where(allowed[None], raw, NEG_LARGE)

    scores = scores_of()
    peak = jnp.max(scores, -1, keepdims=True)
    expo = jnp.exp(scores - peak)
    denom = jnp.sum(expo, -1, keepdims=True)
    log_total = peak + jnp.log(denom)
    probs_low = (expo / denom).astype(BF)
    o = jnp.einsum("gqn,nd->qgd", probs_low, v, preferred_element_type=F32)
    o = o.astype(BF).reshape(GROUP, Q_LOC)
    branch_part = jnp.dot(o, wf_out, preferred_element_type=F32).astype(BF)

    h1, n2, cot_full, wf_gu, wf_dn = call(
        middle_kernel, 2,
        (branch_part.reshape(8, 128, D), tokens, cotangent, gu_own, dn_own),
        [VM, VM, ANY, ANY, ANY],
        [((128, D), F32), ((8, 128, D), BF), ((8, 128, D), BF),
         ((4, 4, 8, 16, 2 * FF_LOC), BF), ((4, 4, 3, 16, D), BF)],
        [VM, ANY, ANY, ANY, ANY],
        [pltpu.VMEM((128, D), BF), *SCATTER_SCRATCH], 64, 4,
    )
    n2 = n2.reshape(GROUP, D)
    cot_full = cot_full.reshape(GROUP, D)
    wf_gu = wf_gu.reshape(D, 2 * FF_LOC)
    wf_dn = wf_dn.reshape(FF_LOC, D)

    gu = jnp.dot(n2, wf_gu, preferred_element_type=F32)
    gate_act, up_act = gu[:, :FF_LOC], gu[:, FF_LOC:]
    gate_sig = jax.nn.sigmoid(gate_act)
    silu_act = gate_act * gate_sig
    hm = (silu_act * up_act).astype(BF)
    y_part = jnp.dot(hm, wf_dn, preferred_element_type=F32).astype(BF)
    inner_grad = contract(cot_full, wf_dn, ACROSS)
    gate_grad = inner_grad * up_act * gate_sig * (1.0 + gate_act * (1.0 - gate_sig))
    both_grads = jnp.concatenate([gate_grad, inner_grad * silu_act], 1).astype(BF)
    u_part = contract(both_grads, wf_gu, ACROSS).astype(BF)
    g_gu = contract(n2, both_grads, DOWNWARD).astype(BF)
    g_dn = contract(hm, cot_full, DOWNWARD).astype(BF)

    block_out, dh1, da, ret_gu, ret_dn = call(
        back_kernel, 3,
        (u_part.reshape(8, 128, D), y_part.reshape(8, 128, D), h1, cotangent,
         g_gu.reshape(4, 4, 8, 16, 2 * FF_LOC), g_dn.reshape(4, 4, 3, 16, D)),
        [VM] * 6,
        [((128, D), BF), ((128, D), F32), ((8, 128, D), BF),
         ((8, 16, 2 * FF_LOC), BF), ((3, 16, D), BF)],
        [VM, VM, ANY, ANY, ANY],
        [pltpu.VMEM((128, D), BF), pltpu.VMEM((8, 16, 2 * FF_LOC), BF), pltpu.VMEM((3, 16, D), BF),
         *SCATTER_SCRATCH, *SCATTER_SCRATCH,
         *dp_scatter_scratch((8, 16, 2 * FF_LOC), True), *dp_scatter_scratch((3, 16, D), False)],
        96, 3,
    )
    da = da.reshape(GROUP, D)

    do = contract(da, wf_out, ACROSS).astype(BF).reshape(GROUP, heads, HEAD_DIM)
    g_out = contract(o, da, DOWNWARD).astype(BF)
    probs = jnp.exp(scores_of() - log_total)
    probs_low = probs.astype(BF)
    prob_grad = jnp.einsum("qgd,nd->gqn", do, v, preferred_element_type=F32)
    delta = jnp.sum(probs * prob_grad, -1, keepdims=True)
    score_grad = (probs * (prob_grad - delta)).astype(BF)
    dq = jnp.einsum("gqn,nd->qgd", score_grad, k, preferred_element_type=F32) * score_scale
    dk = jnp.einsum("gqn,qgd->nd", score_grad, q, preferred_element_type=F32) * score_scale
    dv = jnp.einsum("gqn,qgd->nd", probs_low, do, preferred_element_type=F32)
    dq = rotate(dq, cos_table, -sin_table).reshape(GROUP, Q_LOC)
    dk = rotate(dk[:, None], cos_table, -sin_table)[:, 0]
    dqkv = jnp.concatenate([dq, dk, dv], 1).astype(BF)
    u1_part = contract(dqkv, wf_qkv, ACROSS).astype(BF)
    g_qkv = contract(n1, dqkv, DOWNWARD).astype(BF)

    input_grad, ret_qkv, ret_out = call(
        end_kernel, 4,
        (u1_part.reshape(8, 128, D), tokens, dh1,
         g_qkv.reshape(4, 4, 8, 16, QKV_LOC), g_out.reshape(4, 4, 16, D)),
        [VM] * 5,
        [((128, D), F32), ((8, 16, QKV_LOC), BF), ((16, D), BF)],
        [VM, ANY, ANY],
        [pltpu.VMEM((8, 16, QKV_LOC), BF), pltpu.VMEM((16, D), BF),
         *SCATTER_SCRATCH,
         *dp_scatter_scratch((8, 16, QKV_LOC), True), *dp_scatter_scratch((16, D), False)],
        64, 2,
    )

    ret_gu = ret_gu.astype(F32)
    ret_qkv = ret_qkv.astype(F32)
    back = lambda r: r.transpose(1, 0, 2).reshape(16, -1)
    raw_q = back(ret_qkv[:, :, :Q_LOC])
    pairs = ret_qkv[:, :, Q_LOC:].reshape(4, 2, 16, 128).sum(1)
    raw_k, raw_v = back(pairs[:, :, :64]), back(pairs[:, :, 64:])

    def unpadded(r):
        cut = lax.dot_general(
            r.reshape(128, FF_LOC).astype(BF),
            hot.astype(BF),
            ACROSS,
            preferred_element_type=F32,
        )
        return back(cut.reshape(8, 16, FF // N_CTX))

    raw_gate, raw_up = unpadded(ret_gu[:, :, :FF_LOC]), unpadded(ret_gu[:, :, FF_LOC:])

    def gain_grad(*pairs_of):
        return sum(jnp.sum(w.astype(F32) * raw, 1) for w, raw in pairs_of)

    return (
        block_out,
        input_grad,
        gain_grad((w_query, raw_q), (w_key, raw_k), (w_value, raw_v)),
        gain_a * raw_q,
        gain_a * raw_k,
        gain_a * raw_v,
        ret_out.astype(F32),
        gain_grad((w_gate, raw_gate), (w_up, raw_up)),
        gain_m * raw_gate,
        gain_m * raw_up,
        ret_dn.reshape(FF_PAD, D)[:FF_PART].astype(F32),
    )


def solution(mesh):
    flat = P(("dp", "ctx"), None)
    in_specs = (
        flat, flat, P("dp", None), P("dp", None, None), P(("dp", "ctx")), flat, flat, flat, flat,
        P(("dp", "ctx")), flat, flat, flat,
    )
    out_specs = (
        flat, flat, P(("dp", "ctx")), flat, flat, flat, flat, P(("dp", "ctx")), flat, flat, flat,
    )
    return jax.shard_map(
        per_device, mesh=mesh, in_specs=in_specs, out_specs=out_specs, check_vma=False
    )
```

```python
import jax
import jax.numpy as jnp
from jax import lax
from jax.experimental import pallas as pl
from jax.experimental.pallas import tpu as pltpu
from jax.sharding import PartitionSpec as P

D = 2048
HEADS = 32
KV_HEADS = 4
HEAD_DIM = 64
FF = 5632
N_CTX = 8
N_DP = 16
ROWS = 128
GROUP = 1024
Q_LOC = 256
QKV_LOC = 384
FF_PART = 44
FF_PAD = 48
FF_LOC = N_DP * FF_PAD
EPSILON = 1e-05
NEG_LARGE = -1e30
MESH = pl.DeviceIdType.MESH
BF = jnp.bfloat16
F32 = jnp.float32
ANY = pl.BlockSpec(memory_space=pl.ANY)
VM = pl.BlockSpec(memory_space=pltpu.VMEM)
ACROSS = (((1,), (1,)), ((), ()))
DOWNWARD = (((0,), (0,)), ((), ()))
PLAIN = (((1,), (0,)), ((), ()))


class Place:
    def __init__(self):
        self.d = lax.axis_index("dp")
        self.c = lax.axis_index("ctx")
        self.z, self.y = lax.div(self.d, 4), lax.rem(self.d, 4)
        self.x, self.k = lax.div(self.c, 2), lax.rem(self.c, 2)

    def at_x(self, step):
        return lax.rem(self.x + step, 4)

    def on_x(self, step):
        return (self.d, self.at_x(step) * 2 + self.k)

    def sibling(self):
        return (self.d, self.x * 2 + 1 - self.k)

    def on_ctx(self, step):
        return (self.d, lax.rem(self.c + step, 8))

    def on_y(self, step):
        return (self.z * 4 + lax.rem(self.y + step, 4), self.c)

    def on_z(self, step):
        return (lax.rem(self.z + step, 4) * 4 + self.y, self.c)

    def spread_to(self):
        return (lax.rem(self.d + 2 * self.c, 16), self.c)

    def spread_from(self):
        return (lax.rem(self.d + 16 - 2 * self.c, 16), self.c)

    def spreads(self):
        return self.c != 0

    def turn_to(self):
        return (self.d, lax.rem(lax.div(self.d, 2) + 8 - self.c, 8))

    def turns(self):
        return self.turn_to()[1] != self.c


def block_of(position, index):
    return 8 * (position % 2) + (position // 2 + 8 - index) % 8


class Copies:
    def __init__(self, send_sems, recv_sems):
        self.send_sems, self.recv_sems, self.used, self.started = send_sems, recv_sems, 0, []

    def make(self, src, dst, device):
        i = self.used
        self.used += 1
        return pltpu.make_async_remote_copy(
            src_ref=src,
            dst_ref=dst,
            send_sem=self.send_sems.at[i],
            recv_sem=self.recv_sems.at[i],
            device_id=device,
            device_id_type=MESH,
        )

    def send(self, src, dst, device):
        copy = self.make(src, dst, device)
        copy.start()
        self.started.append(copy)
        return copy

    def sent(self, copy):
        copy.wait_send()
        self.started = [other for other in self.started if other is not copy]

    def finish(self):
        for copy in self.started:
            copy.wait_send()


def greet(peers, extra=None, extra_on=None):
    barrier = pltpu.get_barrier_semaphore()
    for peer in peers:
        pl.semaphore_signal(barrier, 1, device_id=peer, device_id_type=MESH)
    count = len(peers)
    if extra is not None:

        @pl.when(extra_on)
        def _():
            pl.semaphore_signal(barrier, 1, device_id=extra, device_id_type=MESH)

        count = jnp.where(extra_on, count + 1, count)
    pl.semaphore_wait(barrier, count)


def hop(copies, keep, src, dst, device, far):
    sent, kept = copies.make(src, dst, device), keep(src, dst)

    def start():
        pl.when(far)(sent.start)
        pl.when(jnp.logical_not(far))(kept.start)

    def wait():
        pl.when(far)(sent.wait)
        pl.when(jnp.logical_not(far))(kept.wait)

    return start, wait


def keeper(sems):
    used = []

    def keep(src, dst):
        used.append(src)
        return pltpu.make_async_copy(src, dst, sems.at[len(used) - 1])

    return keep


def yz_peers(me):
    return [me.on_y(s) for s in (1, 2, 3)] + [me.on_z(s) for s in (1, 2, 3)]


def ctx_peers(me):
    return [me.on_ctx(s) for s in range(1, 8)]


def x_peers(me):
    return [me.on_x(1), me.on_x(3), me.sibling()]


def round_robin(*flows):
    flows = list(flows)
    while flows:
        flows = [f for f in flows if next(f, "end") != "end"]


def ctx_gather(me, copies, src, full, keep):
    own, left, right, far = (me.at_x(s) * 2 + me.k for s in (0, 3, 1, 2))
    to_right, to_left, to_sib = me.on_x(1), me.on_x(3), me.sibling()
    top, low = pl.ds(0, 64), pl.ds(64, 64)
    r1 = copies.send(src.at[top], full.at[own, top], to_right)
    l1 = copies.send(src.at[low], full.at[own, low], to_left)
    s0 = copies.send(src, full.at[own], to_sib)
    r2 = copies.send(src.at[low], full.at[own, low], to_right)
    l2 = copies.send(src.at[top], full.at[own, top], to_left)
    mine = keep(src, full.at[own])
    mine.start()
    yield
    r1.wait_recv()
    r3 = copies.send(full.at[left, top], full.at[left, top], to_right)
    l1.wait_recv()
    l3 = copies.send(full.at[right, low], full.at[right, low], to_left)
    yield
    r2.wait_recv()
    s1 = copies.send(full.at[left], full.at[left], to_sib)
    l2.wait_recv()
    s2 = copies.send(full.at[right], full.at[right], to_sib)
    yield
    r3.wait_recv()
    s3 = copies.send(full.at[far, top], full.at[far, top], to_sib)
    l3.wait_recv()
    s4 = copies.send(full.at[far, low], full.at[far, low], to_sib)
    yield
    for s in (s0, s1, s2, s3, s4):
        s.wait_recv()
    mine.wait()


def add_rows(dst, rows, *terms):
    def step(i, carry):
        at = pl.ds(pl.multiple_of(i * 16, 16), 16)
        total = terms[0](at).astype(F32)
        for term in terms[1:]:
            total += term(at).astype(F32)
        dst[at, :] = total.astype(dst.dtype)
        return carry

    lax.fori_loop(0, rows // 16, step, 0)


class CtxScatter:
    def __init__(self, me, copies, part, pair, half_left, half_right, from_left, from_right):
        self.me, self.copies, self.part, self.pair = me, copies, part, pair
        self.half_left, self.half_right = half_left, half_right
        self.from_left, self.from_right = from_left, from_right
        self.to_right, self.to_left, self.to_sib = me.on_x(1), me.on_x(3), me.sibling()
        self.arriving = {}

    def give(self, s):
        block = self.me.at_x(s) * 2 + 1 - self.me.k
        self.arriving[s] = self.copies.send(self.part.at[block], self.pair.at[s], self.to_sib)

    def merge(self, s):
        top, low = pl.ds(0, 64), pl.ds(64, 64)
        self.arriving[s].wait_recv()
        block, pair, part = self.me.at_x(s) * 2 + self.me.k, self.pair, self.part
        add_rows(pair.at[s], 128, lambda at: part[block, at, :], lambda at: pair[s, at, :])
        send = self.copies.send
        if s == 2:
            self.a = send(pair.at[2, top], self.half_left, self.to_right)
            self.b = send(pair.at[2, low], self.half_right, self.to_left)
        if s == 1:
            self.r1 = send(pair.at[1, low], self.from_left.at[low], self.to_right)
        if s == 3:
            self.l1 = send(pair.at[3, top], self.from_right.at[top], self.to_left)

    def relay_right(self):
        half, pair = self.half_left, self.pair
        self.a.wait_recv()
        add_rows(half, 64, lambda at: half[at, :], lambda at: pair[1, at, :])
        self.r2 = self.copies.send(half, self.from_left.at[pl.ds(0, 64)], self.to_right)

    def relay_left(self):
        half, pair = self.half_right, self.pair
        self.b.wait_recv()
        add_rows(half, 64, lambda at: half[at, :], lambda at: pair.at[3, pl.ds(64, 64)][at, :])
        self.l2 = self.copies.send(half, self.from_right.at[pl.ds(64, 64)], self.to_left)

    def finish(self):
        for copy in (self.r1, self.l1, self.r2, self.l2):
            copy.wait_recv()


def ctx_scatter(*args):
    job = CtxScatter(*args)
    for s in (2, 1, 3, 0):
        job.give(s)
    yield
    for s in (2, 1, 3, 0):
        job.merge(s)
    yield
    job.relay_right()
    job.relay_left()
    yield
    job.finish()


SCATTER_SCRATCH = [
    pltpu.VMEM((4, 128, D), BF),
    pltpu.VMEM((64, D), BF),
    pltpu.VMEM((64, D), BF),
    pltpu.VMEM((128, D), BF),
    pltpu.VMEM((128, D), BF),
]


def scattered(at, pair, from_left, from_right):
    return (
        pair[0, at, :].astype(F32) + from_left[at, :].astype(F32) + from_right[at, :].astype(F32)
    )


def halves(ref, half, by_rows):
    shape = ref.shape
    if by_rows:
        n = shape[-3]
        return ref.at[(*(slice(None),) * (len(shape) - 3), pl.ds(half * (n // 2), n // 2))]
    columns = shape[-1]
    return ref.at[
        (*(slice(None),) * (len(shape) - 1), pl.ds(half * (columns // 2), columns // 2))
    ]


def dp_axes(me, half):
    z = (me.z, me.on_z)
    y = (me.y, me.on_y)
    return (y, z) if half else (z, y)


def dp_gather(me, copies, full, half, by_rows):
    view = halves(full, half, by_rows)
    (p2, dev2), (p1, dev1) = dp_axes(me, half)

    def group(i2, j1):
        return view.at[j1, i2] if half else view.at[i2, j1]

    own = group(p2, p1)
    first = [copies.send(own, own, dev1(s)) for s in (1, 3, 2)]
    yield
    for copy in first:
        copy.wait_recv()
    every, lo, hi = pl.ds(0, 4), pl.ds(0, 2), pl.ds(2, 2)
    mine = group(p2, every)
    up = copies.send(mine, mine, dev2(1))
    down = copies.send(mine, mine, dev2(3))
    yield
    up.wait_recv()
    passed = group(lax.rem(p2 + 3, 4), lo)
    up2 = copies.send(passed, passed, dev2(1))
    down.wait_recv()
    passed = group(lax.rem(p2 + 1, 4), hi)
    down2 = copies.send(passed, passed, dev2(3))
    yield
    up2.wait_recv()
    down2.wait_recv()


def add_blocks(dst, *terms):
    lead = dst.shape[:-2]
    if not lead:
        total = terms[0][...].astype(F32)
        for term in terms[1:]:
            total += term[...].astype(F32)
        dst[...] = total.astype(dst.dtype)
        return

    def step(i, carry):
        at = (lax.div(i, lead[1]), lax.rem(i, lead[1])) if len(lead) == 2 else (i,)
        total = terms[0][at].astype(F32)
        for term in terms[1:]:
            total += term[at].astype(F32)
        dst[at] = total.astype(dst.dtype)
        return carry

    lax.fori_loop(0, lead[0] * (lead[1] if len(lead) == 2 else 1), step, 0)


def dp_scatter(me, copies, part, half, by_rows, out, pass_up, pass_down, from_up, from_down, last):
    view = halves(part, half, by_rows)
    (p1, dev1), (p2, dev2) = dp_axes(me, half)

    def group(i1, j2):
        return view.at[j2, i1] if half else view.at[i1, j2]

    every, lo, hi = pl.ds(0, 4), pl.ds(0, 2), pl.ds(2, 2)
    nxt, far, prv = (lax.rem(p1 + s, 4) for s in (1, 2, 3))
    a = copies.send(group(far, lo), pass_up, dev1(1))
    b = copies.send(group(far, hi), pass_down, dev1(3))
    e1 = copies.send(group(nxt, hi), from_up.at[hi], dev1(1))
    e2 = copies.send(group(prv, lo), from_down.at[lo], dev1(3))
    yield
    a.wait_recv()
    add_blocks(pass_up, pass_up, group(nxt, lo))
    f1 = copies.send(pass_up, from_up.at[lo], dev1(1))
    b.wait_recv()
    add_blocks(pass_down, pass_down, group(prv, hi))
    f2 = copies.send(pass_down, from_down.at[hi], dev1(3))
    yield
    for copy in (e1, e2, f1, f2):
        copy.wait_recv()
    add_blocks(from_up, from_up, from_down, group(p1, every))
    sent = [
        copies.send(from_up.at[lax.rem(p2 + s, 4)], last.at[s - 1], dev2(s)) for s in (1, 2, 3)
    ]
    yield
    for copy in sent:
        copy.wait_recv()
    add_blocks(halves(out, half, by_rows), from_up.at[p2], last.at[0], last.at[1], last.at[2])


def dp_scatter_scratch(block, by_rows):
    block = (block[0] // 2, *block[1:]) if by_rows else (*block[:-1], block[-1] // 2)
    return [pltpu.VMEM((lead, *block), BF) for lead in (2, 2, 4, 4, 3)] * 2


def turn(values, cos_of, sin_of):
    lane = lax.broadcasted_iota(jnp.int32, values.shape, 1)
    other = jnp.where(
        lax.rem(lane, 64) < 32, pltpu.roll(values, 96, 1), pltpu.roll(values, 32, 1)
    )
    return values * cos_of + other * sin_of


def keys_only(cos_of, sin_of):
    lane = lax.broadcasted_iota(jnp.int32, cos_of.shape, 1)
    return jnp.where(lane < 64, cos_of, 1.0), jnp.where(lane < 64, sin_of, 0.0)


def mask_bias(bias, at, packed, first, places):
    places = places[...]
    allowed = (places <= packed[at, :]) & (places >= first[at, :])
    bias[...] = jnp.where(allowed, 0.0, NEG_LARGE).astype(F32)


def attend(at, q, kv, bias, o, log_sums):
    k, v = kv[:, :64], kv[:, 64:]
    outs, logs = [], []
    for h in range(HEADS // N_CTX):
        scores = contract(q[at, h * 64 : h * 64 + 64], k, ACROSS) + bias[...]
        peak = jnp.max(scores, -1, keepdims=True)
        expo = jnp.exp(scores - peak)
        total = jnp.sum(expo, -1, keepdims=True)
        outs.append(contract(expo.astype(BF), v, PLAIN) / total)
        logs.append(peak + jnp.log(total))
    o[at, :] = jnp.concatenate(outs, 1).astype(BF)
    log_sums[at, :] = jnp.concatenate(logs, 1)


def forward_kernel(
    qkv_src, gu_src, od_src, n1_own, cot, tokens, cos_of, sin_of, packed, first, places,
    n1_out, w_qkv_out, w_out_out, w_gu, w_dn, cot_full, n2_full, h1, q, kv, o, log_sums,
    n1, w_qkv, od_mid, w_od, w_out, bias, part, n2, pair, half_left, half_right, from_left, from_right,
    ss, rs, ls,
):
    me = Place()
    greet(ctx_peers(me) + yz_peers(me), me.spread_from(), me.spreads())
    copies = Copies(ss, rs)
    keep = keeper(ls)

    def to_indices(src, home):
        sent = [
            copies.send(src.at[lax.rem(me.c + s, 8)], home.at[me.c], me.on_ctx(s))
            for s in range(1, 8)
        ]
        mine = keep(src.at[me.c], home.at[me.c])
        mine.start()

        def wait():
            for copy in sent:
                copy.wait_recv()
            mine.wait()

        return wait

    qkv_there = to_indices(qkv_src, w_qkv.at[me.z, me.y])
    spread_start, spread_there = hop(copies, keep, od_src, od_mid, me.spread_to(), me.spreads())
    turns = [
        hop(copies, keep, od_mid.at[0], w_od.at[me.z, me.y], me.turn_to(), me.turns()),
        hop(copies, keep, od_mid.at[pl.ds(1, 3)], w_dn.at[me.z, me.y], me.turn_to(), me.turns()),
    ]
    spread_start()
    rows = ctx_gather(me, copies, n1_own, n1, keep)
    next(rows)

    def steps(flows):
        for flow in flows:
            next(flow, None)

    f_qkv = [dp_gather(me, copies, w_qkv, h, True) for h in (0, 1)]
    f_out = [dp_gather(me, copies, w_od, h, False) for h in (0, 1)]
    f_gu = [dp_gather(me, copies, w_gu, h, True) for h in (0, 1)]
    f_dn = [dp_gather(me, copies, w_dn, h, False) for h in (0, 1)]
    seeds = ctx_gather(me, copies, cot, cot_full, keep)
    qkv_there()
    steps(f_qkv)
    spread_there()
    for start, _ in turns:
        start()
    next(rows)
    steps(f_qkv)
    turns[0][1]()
    steps(f_out)
    next(rows)
    gu_there = to_indices(gu_src, w_gu.at[me.z, me.y])
    turns[1][1]()
    steps(f_qkv)
    steps(f_out)
    steps(f_dn)
    next(rows)
    gu_there()
    steps(f_gu)
    next(seeds)
    steps(f_qkv)
    steps(f_out)
    steps(f_dn)
    next(rows, None)
    keeps = [keep(n1, n1_out), keep(w_qkv, w_qkv_out)]
    for copy in keeps:
        copy.start()

    def project(b, carry):
        at = pl.ds(pl.multiple_of(b * 128, 128), 128)
        qkv = contract(n1[b], w_qkv[...].reshape(D, QKV_LOC), PLAIN)
        cos_b, sin_b = cos_of[at, :], sin_of[at, :]
        for j in (0, 1):
            turned = turn(qkv[:, j * 128 : j * 128 + 128], cos_b, sin_b)
            q[at, j * 128 : j * 128 + 128] = (turned * HEAD_DIM ** (-0.5)).astype(BF)
        kv[at, :] = turn(qkv[:, Q_LOC:], *keys_only(cos_b, sin_b)).astype(BF)
        return carry

    lax.fori_loop(0, 8, project, 0)
    steps(f_out)
    steps(f_gu)

    def place(i, carry):
        block = 8 * lax.rem(i, 2) + lax.rem(lax.div(i, 2) + 8 - me.c, 8)
        w_out[block] = w_od[lax.div(i, 4), lax.rem(i, 4)]
        return carry

    lax.fori_loop(0, 16, place, 0)
    keeps.append(keep(w_out, w_out_out))
    keeps[-1].start()
    sums = CtxScatter(
        me, copies, part, pair, half_left, half_right, from_left, from_right
    )

    def heads_of(s):
        at = pl.ds(pl.multiple_of(me.at_x(s) * 256, 256), 256)
        mask_bias(bias, at, packed, first, places)
        attend(at, q, kv, bias, o, log_sums)
        for j in (1 - me.k, me.k):
            block = me.at_x(s) * 2 + j
            rows_at = pl.ds(pl.multiple_of(block * 128, 128), 128)
            part[block] = contract(o[rows_at, :], w_out[...].reshape(Q_LOC, D), PLAIN).astype(BF)
        sums.give(s)

    heads_of(2)
    next(seeds)
    heads_of(1)
    sums.merge(2)
    sums.merge(1)
    next(seeds)
    steps(f_dn)
    heads_of(3)
    sums.merge(3)
    sums.relay_right()
    sums.relay_left()
    next(seeds)
    steps(f_gu)
    heads_of(0)
    sums.merge(0)
    sums.finish()

    def norm(i, carry):
        at = pl.ds(pl.multiple_of(i * 16, 16), 16)
        hidden = tokens[at, :].astype(F32) + scattered(at, pair, from_left, from_right)
        scale = lax.rsqrt(jnp.mean(hidden * hidden, -1, keepdims=True) + EPSILON)
        h1[at, :] = hidden
        n2[at, :] = (hidden * scale).astype(BF)
        return carry

    lax.fori_loop(0, 8, norm, 0)
    normed = ctx_gather(me, copies, n2, n2_full, keep)
    next(normed)
    round_robin(normed, seeds, *f_dn, *f_gu)
    for copy in keeps:
        copy.wait()
    copies.finish()


def ffn_kernel(
    n2_in, cot_in, w_gu_in, w_dn_in, h1, cot, dh1, da_full, part_y, g_gu, ret_dn,
    n2, cot_full, w_gu, w_dn, hm, dgu, part, part_out, g_gu_own, g_dn, da, own_dn, mid_dn, *rest,
):
    ss, rs, ls = rest[-3:]
    scr, scr_dn = rest[0:5], rest[5:15]
    me = Place()
    copies, keep = Copies(ss, rs), keeper(ls)
    loads = {}

    def load(name, src, dst):
        loads[name] = keep(src, dst)
        loads[name].start()

    def two(s):
        return pl.ds(me.at_x(s) * 2, 2)

    load("n2", n2_in.at[two(2)], n2.at[two(2)])
    load("gu", w_gu_in, w_gu)
    load("cot", cot_in.at[two(2)], cot_full.at[two(2)])
    load("dn", w_dn_in, w_dn)
    for s in (1, 3, 0):
        load(("n2", s), n2_in.at[two(s)], n2.at[two(s)])
        load(("cot", s), cot_in.at[two(s)], cot_full.at[two(s)])
    greet(x_peers(me) + yz_peers(me) + [me.turn_to()], me.spread_to(), me.spreads())
    sums = CtxScatter(me, copies, part, *scr)

    def gate_up(s):
        at = pl.ds(pl.multiple_of(me.at_x(s) * 256, 256), 256)
        x = n2[two(s)].reshape(256, D)
        gate = contract(x, w_gu[..., :FF_LOC].reshape(D, FF_LOC), PLAIN)
        up = contract(x, w_gu[..., FF_LOC:].reshape(D, FF_LOC), PLAIN)
        sig = jax.nn.sigmoid(gate)
        silu = gate * sig
        hm[at, :] = (silu * up).astype(BF)
        inner = contract(cot_full[two(s)].reshape(256, D), w_dn[...].reshape(FF_LOC, D), ACROSS)
        dgu[at, :FF_LOC] = (inner * up * (sig + silu * (1.0 - sig))).astype(BF)
        dgu[at, FF_LOC:] = (inner * silu).astype(BF)
        for j in (1 - me.k, me.k):
            block = me.at_x(s) * 2 + j
            rows_at = pl.ds(pl.multiple_of(block * 128, 128), 128)
            part[block] = contract(
                dgu[rows_at, :], w_gu[...].reshape(D, 2 * FF_LOC), ACROSS
            ).astype(BF)
        sums.give(s)

    loads["n2"].wait()
    loads["gu"].wait()
    loads["cot"].wait()
    loads["dn"].wait()
    gate_up(2)
    loads["n2", 1].wait()
    loads["cot", 1].wait()
    gate_up(1)
    sums.merge(2)
    sums.merge(1)
    loads["n2", 3].wait()
    loads["cot", 3].wait()
    gate_up(3)
    sums.merge(3)
    sums.relay_right()
    sums.relay_left()
    loads["n2", 0].wait()
    loads["cot", 0].wait()
    gate_up(0)

    def down(i, carry):
        at = pl.ds(pl.multiple_of(i * 256, 256), 256)
        y = contract(hm[at, :], w_dn[...].reshape(FF_LOC, D), PLAIN).astype(BF)
        part_out[pl.ds(2 * i, 2)] = y.reshape(2, 128, D)
        return carry

    lax.fori_loop(0, 4, down, 0)
    kept = [keep(part_out, part_y)]
    kept[0].start()
    sums.merge(0)
    sums.finish()

    def norm_back(i, carry):
        at = pl.ds(pl.multiple_of(i * 16, 16), 16)
        hidden = h1[at, :]
        scale = lax.rsqrt(jnp.mean(hidden * hidden, -1, keepdims=True) + EPSILON)
        u = scattered(at, scr[0], scr[3], scr[4])
        grad = (
            cot[at, :].astype(F32)
            + scale * u
            - hidden * (scale * scale * scale * jnp.mean(u * hidden, -1, keepdims=True))
        )
        dh1[at, :] = grad
        da[at, :] = grad.astype(BF)
        return carry

    lax.fori_loop(0, 8, norm_back, 0)
    rows_da = ctx_gather(me, copies, da, da_full, keep)
    next(rows_da)
    for j in (0, 1):
        for i in (0, 1):
            cols = slice(1024 * i, 1024 * i + 1024)
            term = contract(
                hm[:, 384 * j : 384 * j + 384], cot_full[:, :, cols].reshape(GROUP, 1024), DOWNWARD
            )
            g_dn[2 * j : 2 * j + 2, :, :, :, cols] = term.astype(BF).reshape(2, 4, 3, 16, 1024)
    flows = [
        dp_scatter(me, copies, g_dn, h, False, own_dn, *scr_dn[h * 5 : h * 5 + 5]) for h in (0, 1)
    ]
    for flow in flows:
        next(flow)

    def outer(j):
        at = pl.ds(256 * j, 256)
        term = contract(n2[:, :, at].reshape(GROUP, 256), dgu[...], DOWNWARD)
        where = (j // 2, pl.ds(2 * (j % 2), 2))
        g_gu_own[where] = term.astype(BF).reshape(2, 8, 16, 2 * FF_LOC)
        kept.append(keep(g_gu_own.at[where], g_gu.at[where]))
        kept[-1].start()

    outer(0)
    next(rows_da)
    outer(1)
    outer(2)
    next(rows_da)
    outer(3)
    for flow in flows:
        next(flow)
    outer(4)
    next(rows_da)
    outer(5)
    outer(6)
    for flow in flows:
        next(flow)
    outer(7)
    round_robin(rows_da, *flows)
    turn_dn = hop(copies, keep, own_dn, mid_dn, me.turn_to(), me.turns())
    home_dn = hop(copies, keep, mid_dn, ret_dn, me.spread_from(), me.spreads())
    turn_dn[0]()
    turn_dn[1]()
    home_dn[0]()
    home_dn[1]()
    for copy in kept:
        copy.wait()
    copies.finish()


def attend_back(at, q, kv, o, do, log_sums, bias, dqkv, dk, dv):
    k, v = kv[:, :64], kv[:, 64:]
    outs = []
    for h in range(HEADS // N_CTX):
        lanes = slice(h * 64, h * 64 + 64)
        queries, grads = q[at, lanes], do[at, lanes]
        probs = jnp.exp(contract(queries, k, ACROSS) + bias[...] - log_sums[at, h : h + 1])
        delta = jnp.sum(grads.astype(F32) * o[at, lanes].astype(F32), -1, keepdims=True)
        score_grad = (probs * (contract(grads, v, ACROSS) - delta)).astype(BF)
        outs.append(contract(score_grad, k, PLAIN) * HEAD_DIM ** (-0.5))
        dk[...] += contract(score_grad, queries, DOWNWARD)
        dv[...] += contract(probs.astype(BF), grads, DOWNWARD)
    dqkv[at, :Q_LOC] = jnp.concatenate(outs, 1)


def end_kernel(
    da_in, part_y_in, g_gu_in, n1_in, w_qkv_in, w_out_in,
    q, kv, o, log_sums, cos_of, sin_of, packed, first, places, h1, dh1, tokens,
    block_out, grad, ret_gu, ret_qkv, ret_out,
    da, part_y, g_gu, n1, w_qkv, w_out, do, dqkv, dqkv_low, dk, dv, bias,
    g_qkv, g_nat, g_out, own_gu, own_qkv, own_out, mid_out, *rest,
):
    ss, rs, ls = rest[-3:]
    scr_y, scr = rest[0:5], rest[5:10]
    scr_gu, scr_qkv, scr_out = rest[10:20], rest[20:30], rest[30:40]
    me = Place()
    copies, keep = Copies(ss, rs), keeper(ls)

    def load(src, dst):
        copy = keep(src, dst)
        copy.start()
        return copy

    load_y = load(part_y_in, part_y)
    load_out = load(w_out_in, w_out)
    load_da = load(da_in, da)
    load_gu = load(g_gu_in, g_gu)
    load_qkv = load(w_qkv_in, w_qkv)
    load_n1 = load(n1_in, n1)
    greet(ctx_peers(me) + yz_peers(me), me.spread_to(), me.spreads())
    load_y.wait()
    sums_y = CtxScatter(me, copies, part_y, *scr_y)
    for s in (2, 1, 3, 0):
        sums_y.give(s)
    load_out.wait()
    load_da.wait()
    load_gu.wait()

    def scatter(g, scratch, own, by_rows):
        return [
            dp_scatter(me, copies, g, h, by_rows, own, *scratch[h * 5 : h * 5 + 5]) for h in (0, 1)
        ]

    def steps(flows):
        for flow in flows:
            next(flow, None)

    f_gu = scatter(g_gu, scr_gu, own_gu, True)
    steps(f_gu)

    def attended_grad(i, carry):
        at = pl.ds(pl.multiple_of(i * 256, 256), 256)
        x = da[pl.ds(2 * i, 2)].reshape(256, D)
        do[at, :] = contract(x, w_out[...].reshape(Q_LOC, D), ACROSS).astype(BF)
        return carry

    lax.fori_loop(0, 4, attended_grad, 0)
    sums_y.merge(2)
    sums_y.merge(1)
    sums_y.merge(3)
    for i in (0, 1):
        cols = slice(1024 * i, 1024 * i + 1024)
        term = contract(o[...], da[:, :, cols].reshape(GROUP, 1024), DOWNWARD)
        g_nat[:, :, cols] = term.astype(BF).reshape(16, 16, 1024)

    def place(i, carry):
        block = 8 * lax.rem(i, 2) + lax.rem(lax.div(i, 2) + 8 - me.c, 8)
        g_out[lax.div(i, 4), lax.rem(i, 4)] = g_nat[block]
        return carry

    lax.fori_loop(0, 16, place, 0)
    dk[...] = jnp.zeros_like(dk)
    dv[...] = jnp.zeros_like(dv)

    def heads_of(i):
        at = pl.ds(256 * i, 256)
        mask_bias(bias, at, packed, first, places)
        attend_back(at, q, kv, o, do, log_sums, bias, dqkv, dk, dv)

    heads_of(0)
    sums_y.relay_right()
    sums_y.relay_left()
    sums_y.merge(0)
    heads_of(1)
    sums_y.finish()

    def finish_y(i, carry):
        at = pl.ds(pl.multiple_of(i * 16, 16), 16)
        block_out[at, :] = (h1[at, :] + scattered(at, scr_y[0], scr_y[3], scr_y[4])).astype(BF)
        return carry

    lax.fori_loop(0, 8, finish_y, 0)
    steps(f_gu)
    f_out = scatter(g_out, scr_out, own_out, False)
    steps(f_out)
    heads_of(2)
    steps(f_gu)
    steps(f_out)
    heads_of(3)
    steps(f_out)
    load_qkv.wait()
    dqkv[:, Q_LOC : Q_LOC + 64] = dk[...]
    dqkv[:, Q_LOC + 64 :] = dv[...]

    def turn_back(i, carry):
        at = pl.ds(pl.multiple_of(i * 128, 128), 128)
        cos_b, sin_b = cos_of[at, :], -sin_of[at, :]
        for j in (0, 1):
            lanes = slice(j * 128, j * 128 + 128)
            dqkv_low[at, lanes] = turn(dqkv[at, lanes], cos_b, sin_b).astype(BF)
        cos_b, sin_b = keys_only(cos_b, sin_b)
        dqkv_low[at, Q_LOC:] = turn(dqkv[at, Q_LOC:], cos_b, sin_b).astype(BF)
        return carry

    lax.fori_loop(0, 8, turn_back, 0)
    part = part_y
    for s in (2, 1, 3, 0):
        copies.sent(sums_y.arriving[s])
    sums = CtxScatter(me, copies, part, *scr)

    def rows_of(s):
        for j in (1 - me.k, me.k):
            block = me.at_x(s) * 2 + j
            at = pl.ds(pl.multiple_of(block * 128, 128), 128)
            part[block] = contract(
                dqkv_low[at, :], w_qkv[...].reshape(D, QKV_LOC), ACROSS
            ).astype(BF)
        sums.give(s)

    rows_of(2)
    rows_of(1)
    sums.merge(2)
    rows_of(3)
    sums.merge(1)
    sums.merge(3)
    rows_of(0)
    load_n1.wait()

    def outer(j, carry):
        at = pl.ds(pl.multiple_of(256 * j, 256), 256)
        term = contract(n1[:, :, at].reshape(GROUP, 256), dqkv_low[...], DOWNWARD)
        where = (lax.div(j, 2), pl.ds(2 * lax.rem(j, 2), 2))
        g_qkv[where] = term.astype(BF).reshape(2, 8, 16, QKV_LOC)
        return carry

    lax.fori_loop(0, 8, outer, 0)
    f_qkv = scatter(g_qkv, scr_qkv, own_qkv, True)
    steps(f_qkv)
    sums.relay_right()
    sums.relay_left()
    sums.merge(0)
    steps(f_gu)
    steps(f_out)
    steps(f_gu)
    steps(f_qkv)

    def to_indices(own, back):
        sent = [
            copies.send(own.at[lax.rem(me.c + s, 8)], back.at[me.c], me.on_ctx(s))
            for s in range(1, 8)
        ]
        mine = keep(own.at[me.c], back.at[me.c])
        mine.start()

        def wait():
            for copy in sent:
                copy.wait_recv()
            mine.wait()

        return wait

    gu_back = to_indices(own_gu, ret_gu)
    steps(f_out)
    turn_out = hop(copies, keep, own_out, mid_out, me.turn_to(), me.turns())
    home_out = hop(copies, keep, mid_out, ret_out, me.spread_from(), me.spreads())
    turn_out[0]()
    steps(f_qkv)
    turn_out[1]()
    home_out[0]()
    sums.finish()

    def finish(i, carry):
        at = pl.ds(pl.multiple_of(i * 16, 16), 16)
        x = tokens[at, :].astype(F32)
        scale = lax.rsqrt(jnp.mean(x * x, -1, keepdims=True) + EPSILON)
        u = scattered(at, scr[0], scr[3], scr[4])
        grad[at, :] = (
            dh1[at, :]
            + scale * u
            - x * (scale * scale * scale * jnp.mean(u * x, -1, keepdims=True))
        )
        return carry

    lax.fori_loop(0, 8, finish, 0)
    steps(f_qkv)
    steps(f_qkv)
    qkv_back = to_indices(own_qkv, ret_qkv)
    gu_back()
    home_out[1]()
    qkv_back()
    copies.finish()


def call(kernel, number, ins, in_specs, outs, out_specs, scratch, n_copies, n_local):
    return pl.pallas_call(
        kernel,
        out_shape=[jax.ShapeDtypeStruct(*o) for o in outs],
        in_specs=in_specs,
        out_specs=out_specs,
        scratch_shapes=[
            *scratch,
            pltpu.SemaphoreType.DMA((n_copies,)),
            pltpu.SemaphoreType.DMA((n_copies,)),
            pltpu.SemaphoreType.DMA((n_local,)),
        ],
        compiler_params=pltpu.CompilerParams(
            collective_id=number, has_side_effects=True, vmem_limit_bytes=60 << 20
        ),
        name=kernel.__name__,
    )(*ins)


def rope_tables(position):
    inverse = jnp.power(F32(10000.0), -jnp.arange(0, HEAD_DIM, 2).astype(F32) / HEAD_DIM)
    angles = position.astype(F32)[:, None] * inverse[None, :]
    return (jnp.cos(angles)[:, None, :], jnp.sin(angles)[:, None, :])


def rotate(values, cos_table, sin_table):
    half_dim = values.shape[-1] // 2
    leading = values[..., :half_dim]
    trailing = values[..., half_dim:]
    return jnp.concatenate(
        [leading * cos_table - trailing * sin_table, trailing * cos_table + leading * sin_table], -1
    )


def contract(left_op, right_op, dims_pair):
    return lax.dot_general(left_op, right_op, dims_pair, preferred_element_type=F32)


def spread():
    index = jnp.arange(N_CTX, dtype=jnp.int32)[:, None, None]
    column = jnp.arange(FF_LOC, dtype=jnp.int32)[None, None, :]
    here = FF_PART * block_of(column // FF_PAD, index) + column % FF_PAD
    held = (column % FF_PAD) < FF_PART
    return held & (jnp.arange(FF // N_CTX, dtype=jnp.int32)[None, :, None] == here)


def per_device(
    tokens, cotangent, lengths, spans, gain_attn, w_query, w_key, w_value, w_out, gain_mlp,
    w_gate, w_up, w_down,
):
    row_ids = jnp.arange(GROUP, dtype=jnp.int32)
    slot_ids = jnp.arange(2 * N_CTX, dtype=jnp.int32)
    table = spans.reshape(-1)
    span_ids = jnp.sum(
        jnp.where((row_ids // 64)[:, None] == slot_ids[None, :], table[None, :], 0), 1
    )
    packed = span_ids * 64 + row_ids % 64
    length_row = lengths[0]
    seq_ends = jnp.cumsum(length_row)
    before = seq_ends[None, :] <= packed[:, None]
    position = packed - jnp.sum(jnp.where(before, length_row[None, :], 0), 1)
    cos_table, sin_table = rope_tables(position)
    cos_of = jnp.tile(cos_table[:, 0], (1, 4))
    sin_of = jnp.tile(jnp.concatenate([-sin_table[:, 0], sin_table[:, 0]], 1), (1, 2))

    gain_a = gain_attn.astype(F32)[:, None]
    gain_m = gain_mlp.astype(F32)[:, None]
    hot = spread().astype(BF)

    def scaled(w, gain):
        return (w.astype(F32) * gain).astype(BF)

    by_index = lambda w, n: w.reshape(16, n, -1).transpose(1, 0, 2)
    twice = lambda w: jnp.repeat(by_index(w, 4), 2, axis=0)
    qkv_src = jnp.concatenate(
        [
            by_index(scaled(w_query, gain_a), 8),
            twice(scaled(w_key, gain_a)),
            twice(scaled(w_value, gain_a)),
        ],
        -1,
    )

    def padded(w):
        return lax.dot_general(
            by_index(scaled(w, gain_m), 8), hot, (((2,), (1,)), ((0,), (0,)))
        )

    gu_src = jnp.concatenate([padded(w_gate), padded(w_up)], -1)
    od_src = jnp.concatenate([w_out, jnp.pad(w_down, ((0, FF_PAD - FF_PART), (0, 0)))])
    od_src = od_src.reshape(4, 16, D)
    tokens_f = tokens.astype(F32)
    scale_attn = lax.rsqrt(jnp.mean(tokens_f * tokens_f, -1, keepdims=True) + EPSILON)
    n1_own = (tokens_f * scale_attn).astype(BF)

    n1, wf_qkv, wf_out, wf_gu, wf_dn, cot_full, n2, h1, q, kv, o, log_sums = call(
        forward_kernel, 1,
        (qkv_src, gu_src, od_src, n1_own, cotangent, tokens, cos_of, sin_of,
         packed[:, None], (packed - position)[:, None], packed[None, :]),
        [ANY] * 5 + [VM] * 6,
        [((8, 128, D), BF), ((4, 4, 8, 16, QKV_LOC), BF), ((16, 16, D), BF),
         ((4, 4, 8, 16, 2 * FF_LOC), BF), ((4, 4, 3, 16, D), BF), ((8, 128, D), BF),
         ((8, 128, D), BF), ((128, D), F32), ((GROUP, Q_LOC), BF), ((GROUP, 128), BF),
         ((GROUP, Q_LOC), BF), ((GROUP, 4), F32)],
        [ANY] * 7 + [VM] * 5,
        [pltpu.VMEM((8, 128, D), BF), pltpu.VMEM((4, 4, 8, 16, QKV_LOC), BF),
         pltpu.VMEM((4, 16, D), BF), pltpu.VMEM((4, 4, 16, D), BF), pltpu.VMEM((16, 16, D), BF),
         pltpu.VMEM((256, GROUP), F32),
         pltpu.VMEM((8, 128, D), BF), pltpu.VMEM((128, D), BF), *SCATTER_SCRATCH], 128, 16,
    )
    dh1, da, part_y, g_gu, ret_dn = call(
        ffn_kernel, 2,
        (n2, cot_full, wf_gu, wf_dn, h1, cotangent), [ANY] * 4 + [VM] * 2,
        [((128, D), F32), ((8, 128, D), BF), ((8, 128, D), BF), ((4, 4, 8, 16, 2 * FF_LOC), BF),
         ((3, 16, D), BF)],
        [VM] + [ANY] * 4,
        [pltpu.VMEM((8, 128, D), BF), pltpu.VMEM((8, 128, D), BF),
         pltpu.VMEM((4, 4, 8, 16, 2 * FF_LOC), BF), pltpu.VMEM((4, 4, 3, 16, D), BF),
         pltpu.VMEM((GROUP, FF_LOC), BF), pltpu.VMEM((GROUP, 2 * FF_LOC), BF),
         pltpu.VMEM((8, 128, D), BF), pltpu.VMEM((8, 128, D), BF),
         pltpu.VMEM((4, 4, 8, 16, 2 * FF_LOC), BF), pltpu.VMEM((4, 4, 3, 16, D), BF),
         pltpu.VMEM((128, D), BF), pltpu.VMEM((3, 16, D), BF), pltpu.VMEM((3, 16, D), BF),
         *SCATTER_SCRATCH, *dp_scatter_scratch((3, 16, D), False)],
        64, 32,
    )

    block_out, input_grad, ret_gu, ret_qkv, ret_out = call(
        end_kernel, 3,
        (da, part_y, g_gu, n1, wf_qkv, wf_out, q, kv, o, log_sums, cos_of, sin_of,
         packed[:, None], (packed - position)[:, None], packed[None, :], h1, dh1, tokens),
        [ANY] * 6 + [VM] * 12,
        [((128, D), BF), ((128, D), F32), ((8, 16, 2 * FF_LOC), BF), ((8, 16, QKV_LOC), BF),
         ((16, D), BF)],
        [VM, VM, ANY, ANY, ANY],
        [pltpu.VMEM((8, 128, D), BF), pltpu.VMEM((8, 128, D), BF),
         pltpu.VMEM((4, 4, 8, 16, 2 * FF_LOC), BF), pltpu.VMEM((8, 128, D), BF),
         pltpu.VMEM((4, 4, 8, 16, QKV_LOC), BF), pltpu.VMEM((16, 16, D), BF),
         pltpu.VMEM((GROUP, Q_LOC), BF), pltpu.VMEM((GROUP, QKV_LOC), F32),
         pltpu.VMEM((GROUP, QKV_LOC), BF), pltpu.VMEM((GROUP, 64), F32),
         pltpu.VMEM((GROUP, 64), F32), pltpu.VMEM((256, GROUP), F32),
         pltpu.VMEM((4, 4, 8, 16, QKV_LOC), BF),
         pltpu.VMEM((16, 16, D), BF), pltpu.VMEM((4, 4, 16, D), BF),
         pltpu.VMEM((8, 16, 2 * FF_LOC), BF), pltpu.VMEM((8, 16, QKV_LOC), BF),
         pltpu.VMEM((16, D), BF), pltpu.VMEM((16, D), BF),
         *SCATTER_SCRATCH, *SCATTER_SCRATCH, *dp_scatter_scratch((8, 16, 2 * FF_LOC), True),
         *dp_scatter_scratch((8, 16, QKV_LOC), True), *dp_scatter_scratch((16, D), False)],
        112, 32,
    )

    ret_qkv = ret_qkv.astype(F32)
    back = lambda r: r.transpose(1, 0, 2).reshape(16, -1)
    raw_q = back(ret_qkv[:, :, :Q_LOC])
    pairs = ret_qkv[:, :, Q_LOC:].reshape(4, 2, 16, 128).sum(1)
    raw_k, raw_v = back(pairs[:, :, :64]), back(pairs[:, :, 64:])

    def unpadded(r):
        return back(
            lax.dot_general(
                r, hot, (((2,), (2,)), ((0,), (0,))), preferred_element_type=F32
            )
        )

    raw_gate, raw_up = unpadded(ret_gu[:, :, :FF_LOC]), unpadded(ret_gu[:, :, FF_LOC:])

    def gain_grad(*pairs_of):
        return sum(jnp.sum(w.astype(F32) * raw, 1) for w, raw in pairs_of)

    return (
        block_out,
        input_grad,
        gain_grad((w_query, raw_q), (w_key, raw_k), (w_value, raw_v)),
        gain_a * raw_q,
        gain_a * raw_k,
        gain_a * raw_v,
        ret_out.astype(F32),
        gain_grad((w_gate, raw_gate), (w_up, raw_up)),
        gain_m * raw_gate,
        gain_m * raw_up,
        ret_dn.reshape(FF_PAD, D)[:FF_PART].astype(F32),
    )


def solution(mesh):
    flat = P(("dp", "ctx"), None)
    in_specs = (
        flat, flat, P("dp", None), P("dp", None, None), P(("dp", "ctx")), flat, flat, flat, flat,
        P(("dp", "ctx")), flat, flat, flat,
    )
    out_specs = (
        flat, flat, P(("dp", "ctx")), flat, flat, flat, flat, P(("dp", "ctx")), flat, flat, flat,
    )
    return jax.shard_map(
        per_device, mesh=mesh, in_specs=in_specs, out_specs=out_specs, check_vma=False
    )
```

```python
import jax
import jax.numpy as jnp
import numpy as np
from jax import lax
from jax.experimental import pallas as pl
from jax.experimental.pallas import tpu as pltpu
from jax.sharding import PartitionSpec as P

D = 2048
HEADS = 32
KV_HEADS = 4
HEAD_DIM = 64
FF = 5632
N_CTX = 8
N_DP = 16
ROWS = 128
GROUP = 1024
Q_LOC = 256
QKV_LOC = 384
FF_PART = 44
FF_PAD = 48
FF_LOC = N_DP * FF_PAD
FF_CUT = FF // N_CTX
EPSILON = 1e-05
NEG_LARGE = -1e30
MESH = pl.DeviceIdType.MESH
BF = jnp.bfloat16
F32 = jnp.float32
ANY = pl.BlockSpec(memory_space=pl.ANY)
VM = pl.BlockSpec(memory_space=pltpu.VMEM)
SM = pl.BlockSpec(memory_space=pltpu.SMEM)
ACROSS = (((1,), (1,)), ((), ()))
DOWNWARD = (((0,), (0,)), ((), ()))
PLAIN = (((1,), (0,)), ((), ()))


def contract(left_op, right_op, dims_pair):
    return lax.dot_general(left_op, right_op, dims_pair, preferred_element_type=F32)


class Place:
    def __init__(self):
        self.d = lax.axis_index("dp")
        self.c = lax.axis_index("ctx")
        self.z, self.y = lax.div(self.d, 4), lax.rem(self.d, 4)
        self.x, self.k = lax.div(self.c, 2), lax.rem(self.c, 2)

    def at_x(self, step):
        return lax.rem(self.x + step, 4)

    def on_x(self, step):
        return (self.d, self.at_x(step) * 2 + self.k)

    def sibling(self):
        return (self.d, self.x * 2 + 1 - self.k)

    def on_ctx(self, step):
        return (self.d, lax.rem(self.c + step, 8))

    def on_y(self, step):
        return (self.z * 4 + lax.rem(self.y + step, 4), self.c)

    def on_z(self, step):
        return (lax.rem(self.z + step, 4) * 4 + self.y, self.c)

    def spread_to(self):
        return (lax.rem(self.d + 2 * self.c, 16), self.c)

    def spread_from(self):
        return (lax.rem(self.d + 16 - 2 * self.c, 16), self.c)

    def spreads(self):
        return self.c != 0

    def turn_to(self):
        return (self.d, lax.rem(lax.div(self.d, 2) + 8 - self.c, 8))

    def turns(self):
        return self.turn_to()[1] != self.c


def block_at(position, index):
    return 8 * lax.rem(position, 2) + lax.rem(lax.div(position, 2) + 8 - index, 8)


class Copies:
    def __init__(self, send_sems, recv_sems):
        self.send_sems, self.recv_sems, self.used, self.started = send_sems, recv_sems, 0, []

    def make(self, src, dst, device):
        i = self.used
        self.used += 1
        return pltpu.make_async_remote_copy(
            src_ref=src,
            dst_ref=dst,
            send_sem=self.send_sems.at[i],
            recv_sem=self.recv_sems.at[i],
            device_id=device,
            device_id_type=MESH,
        )

    def send(self, src, dst, device):
        copy = self.make(src, dst, device)
        copy.start()
        self.started.append(copy)
        return copy

    def sent(self, copy):
        copy.wait_send()
        self.started = [other for other in self.started if other is not copy]

    def finish(self):
        for copy in self.started:
            copy.wait_send()


def greet(peers, extra=None, extra_on=None, meanwhile=lambda: None):
    barrier = pltpu.get_barrier_semaphore()
    for peer in peers:
        pl.semaphore_signal(barrier, 1, device_id=peer, device_id_type=MESH)
    count = len(peers)
    if extra is not None:

        @pl.when(extra_on)
        def _():
            pl.semaphore_signal(barrier, 1, device_id=extra, device_id_type=MESH)

        count = jnp.where(extra_on, count + 1, count)
    meanwhile()
    pl.semaphore_wait(barrier, count)


def hop(copies, keep, src, dst, device, far):
    sent, kept = copies.make(src, dst, device), keep(src, dst)

    def start():
        pl.when(far)(sent.start)
        pl.when(jnp.logical_not(far))(kept.start)

    def wait():
        pl.when(far)(sent.wait)
        pl.when(jnp.logical_not(far))(kept.wait)

    return start, wait


def keeper(sems):
    used = []

    def keep(src, dst):
        used.append(src)
        return pltpu.make_async_copy(src, dst, sems.at[len(used) - 1])

    return keep


def yz_peers(me):
    return [me.on_y(s) for s in (1, 2, 3)] + [me.on_z(s) for s in (1, 2, 3)]


def ctx_peers(me):
    return [me.on_ctx(s) for s in range(1, 8)]


def x_peers(me):
    return [me.on_x(1), me.on_x(3), me.sibling()]


def round_robin(*flows):
    flows = list(flows)
    while flows:
        flows = [f for f in flows if next(f, "end") != "end"]


def ctx_gather(me, copies, src, full, keep):
    own, left, right, far = (me.at_x(s) * 2 + me.k for s in (0, 3, 1, 2))
    to_right, to_left, to_sib = me.on_x(1), me.on_x(3), me.sibling()
    top, low = pl.ds(0, 64), pl.ds(64, 64)
    r1 = copies.send(src.at[top], full.at[own, top], to_right)
    l1 = copies.send(src.at[low], full.at[own, low], to_left)
    s0 = copies.send(src, full.at[own], to_sib)
    r2 = copies.send(src.at[low], full.at[own, low], to_right)
    l2 = copies.send(src.at[top], full.at[own, top], to_left)
    mine = keep(src, full.at[own])
    mine.start()
    yield
    r1.wait_recv()
    r3 = copies.send(full.at[left, top], full.at[left, top], to_right)
    l1.wait_recv()
    l3 = copies.send(full.at[right, low], full.at[right, low], to_left)
    yield
    r2.wait_recv()
    s1 = copies.send(full.at[left], full.at[left], to_sib)
    l2.wait_recv()
    s2 = copies.send(full.at[right], full.at[right], to_sib)
    yield
    r3.wait_recv()
    s3 = copies.send(full.at[far, top], full.at[far, top], to_sib)
    l3.wait_recv()
    s4 = copies.send(full.at[far, low], full.at[far, low], to_sib)
    yield
    for s in (s0, s1, s2, s3, s4):
        s.wait_recv()
    mine.wait()


def add_rows(dst, rows, *terms):
    def step(i, carry):
        at = pl.ds(pl.multiple_of(i * 16, 16), 16)
        total = terms[0](at).astype(F32)
        for term in terms[1:]:
            total += term(at).astype(F32)
        dst[at, :] = total.astype(dst.dtype)
        return carry

    lax.fori_loop(0, rows // 16, step, 0)


class CtxScatter:
    def __init__(self, me, copies, part, pair, half_left, half_right, from_left, from_right):
        self.me, self.copies, self.part, self.pair = me, copies, part, pair
        self.half_left, self.half_right = half_left, half_right
        self.from_left, self.from_right = from_left, from_right
        self.to_right, self.to_left, self.to_sib = me.on_x(1), me.on_x(3), me.sibling()
        self.arriving = {}

    def give(self, s):
        block = self.me.at_x(s) * 2 + 1 - self.me.k
        self.arriving[s] = self.copies.send(self.part.at[block], self.pair.at[s], self.to_sib)

    def merge(self, s):
        top, low = pl.ds(0, 64), pl.ds(64, 64)
        self.arriving[s].wait_recv()
        block, pair, part = self.me.at_x(s) * 2 + self.me.k, self.pair, self.part
        add_rows(pair.at[s], 128, lambda at: part[block, at, :], lambda at: pair[s, at, :])
        send = self.copies.send
        if s == 2:
            self.a = send(pair.at[2, top], self.half_left, self.to_right)
            self.b = send(pair.at[2, low], self.half_right, self.to_left)
        if s == 1:
            self.r1 = send(pair.at[1, low], self.from_left.at[low], self.to_right)
        if s == 3:
            self.l1 = send(pair.at[3, top], self.from_right.at[top], self.to_left)

    def relay_right(self):
        half, pair = self.half_left, self.pair
        self.a.wait_recv()
        add_rows(half, 64, lambda at: half[at, :], lambda at: pair[1, at, :])
        self.r2 = self.copies.send(half, self.from_left.at[pl.ds(0, 64)], self.to_right)

    def relay_left(self):
        half, pair = self.half_right, self.pair
        self.b.wait_recv()
        add_rows(half, 64, lambda at: half[at, :], lambda at: pair.at[3, pl.ds(64, 64)][at, :])
        self.l2 = self.copies.send(half, self.from_right.at[pl.ds(64, 64)], self.to_left)

    def finish(self):
        for copy in (self.r1, self.l1, self.r2, self.l2):
            copy.wait_recv()


def ctx_scatter(*args):
    job = CtxScatter(*args)
    for s in (2, 1, 3, 0):
        job.give(s)
    yield
    for s in (2, 1, 3, 0):
        job.merge(s)
    yield
    job.relay_right()
    job.relay_left()
    yield
    job.finish()


SCATTER_SCRATCH = [
    pltpu.VMEM((4, 128, D), BF),
    pltpu.VMEM((64, D), BF),
    pltpu.VMEM((64, D), BF),
    pltpu.VMEM((128, D), BF),
    pltpu.VMEM((128, D), BF),
]


def scattered(at, pair, from_left, from_right):
    return (
        pair[0, at, :].astype(F32) + from_left[at, :].astype(F32) + from_right[at, :].astype(F32)
    )


def halves(ref, half, by_rows):
    shape = ref.shape
    if by_rows:
        n = shape[-3]
        return ref.at[(*(slice(None),) * (len(shape) - 3), pl.ds(half * (n // 2), n // 2))]
    columns = shape[-1]
    return ref.at[
        (*(slice(None),) * (len(shape) - 1), pl.ds(half * (columns // 2), columns // 2))
    ]


def dp_axes(me, half):
    z = (me.z, me.on_z)
    y = (me.y, me.on_y)
    return (y, z) if half else (z, y)


def dp_gather(me, copies, full, half, by_rows):
    view = halves(full, half, by_rows)
    (p2, dev2), (p1, dev1) = dp_axes(me, half)

    def group(i2, j1):
        return view.at[j1, i2] if half else view.at[i2, j1]

    own = group(p2, p1)
    first = [copies.send(own, own, dev1(s)) for s in (1, 3, 2)]
    yield
    for copy in first:
        copy.wait_recv()
    every, lo, hi = pl.ds(0, 4), pl.ds(0, 2), pl.ds(2, 2)
    mine = group(p2, every)
    up = copies.send(mine, mine, dev2(1))
    down = copies.send(mine, mine, dev2(3))
    yield
    up.wait_recv()
    passed = group(lax.rem(p2 + 3, 4), lo)
    up2 = copies.send(passed, passed, dev2(1))
    down.wait_recv()
    passed = group(lax.rem(p2 + 1, 4), hi)
    down2 = copies.send(passed, passed, dev2(3))
    yield
    up2.wait_recv()
    down2.wait_recv()


def add_blocks(dst, *terms):
    lead = dst.shape[:-2]
    if not lead:
        total = terms[0][...].astype(F32)
        for term in terms[1:]:
            total += term[...].astype(F32)
        dst[...] = total.astype(dst.dtype)
        return

    def step(i, carry):
        at = (lax.div(i, lead[1]), lax.rem(i, lead[1])) if len(lead) == 2 else (i,)
        total = terms[0][at].astype(F32)
        for term in terms[1:]:
            total += term[at].astype(F32)
        dst[at] = total.astype(dst.dtype)
        return carry

    lax.fori_loop(0, lead[0] * (lead[1] if len(lead) == 2 else 1), step, 0)


def dp_scatter(me, copies, part, half, by_rows, out, pass_up, pass_down, from_up, from_down, last):
    view = halves(part, half, by_rows)
    (p1, dev1), (p2, dev2) = dp_axes(me, half)

    def group(i1, j2):
        return view.at[j2, i1] if half else view.at[i1, j2]

    every, lo, hi = pl.ds(0, 4), pl.ds(0, 2), pl.ds(2, 2)
    nxt, far, prv = (lax.rem(p1 + s, 4) for s in (1, 2, 3))
    a = copies.send(group(far, lo), pass_up, dev1(1))
    b = copies.send(group(far, hi), pass_down, dev1(3))
    e1 = copies.send(group(nxt, hi), from_up.at[hi], dev1(1))
    e2 = copies.send(group(prv, lo), from_down.at[lo], dev1(3))
    yield
    a.wait_recv()
    add_blocks(pass_up, pass_up, group(nxt, lo))
    f1 = copies.send(pass_up, from_up.at[lo], dev1(1))
    b.wait_recv()
    add_blocks(pass_down, pass_down, group(prv, hi))
    f2 = copies.send(pass_down, from_down.at[hi], dev1(3))
    yield
    for copy in (e1, e2, f1, f2):
        copy.wait_recv()
    add_blocks(from_up, from_up, from_down, group(p1, every))
    sent = [
        copies.send(from_up.at[lax.rem(p2 + s, 4)], last.at[s - 1], dev2(s)) for s in (1, 2, 3)
    ]
    yield
    for copy in sent:
        copy.wait_recv()
    add_blocks(halves(out, half, by_rows), from_up.at[p2], last.at[0], last.at[1], last.at[2])


def dp_scatter_scratch(block, by_rows):
    block = (block[0] // 2, *block[1:]) if by_rows else (*block[:-1], block[-1] // 2)
    return [pltpu.VMEM((lead, *block), BF) for lead in (2, 2, 4, 4, 3)] * 2


def turn(values, cos_of, sin_of):
    lane = lax.broadcasted_iota(jnp.int32, values.shape, 1)
    other = jnp.where(
        lax.rem(lane, 64) < 32, pltpu.roll(values, 96, 1), pltpu.roll(values, 32, 1)
    )
    return values * cos_of + other * sin_of


def keys_only(cos_of, sin_of):
    lane = lax.broadcasted_iota(jnp.int32, cos_of.shape, 1)
    return jnp.where(lane < 64, cos_of, 1.0), jnp.where(lane < 64, sin_of, 0.0)


def split_halves(values):
    return (
        jnp.concatenate([values[0:64], values[128:192]], 0),
        jnp.concatenate([values[64:128], values[192:256]], 0),
    )


def half_rows(half, chip):
    return pl.ds(pl.multiple_of(half * 512 + chip * 128, 128), 128)


def of_both(ref, half, chips, lanes=slice(None)):
    pieces = [ref[half_rows(half, chip), lanes] for chip in chips]
    return jnp.concatenate(pieces, 0) if len(pieces) > 1 else pieces[0]


def to_both(ref, half, chips, lanes, values):
    for i, chip in enumerate(chips):
        ref[half_rows(half, chip), lanes] = values[128 * i : 128 * i + 128]


def group_rows(chip, core, half):
    return pl.ds(pl.multiple_of(chip * 256 + core * 128 + half * 64, 64), 64)


def lay_out(lengths, spans, inverse, meta, places, cos_of, sin_of):
    j = lax.broadcasted_iota(jnp.int32, (1, GROUP), 1)
    slot, packed = lax.div(j, 64), lax.rem(j, 64)
    for r in range(8):
        for half in range(2):
            packed = packed + jnp.where(slot == half * 8 + r, spans[0, 2 * r + half] * 64, 0)
    first, end = jnp.zeros_like(packed), 0
    for i in range(4):
        end = end + lengths[0, i]
        first = first + jnp.where(packed >= end, lengths[0, i], 0)
    places[...] = packed.astype(F32)
    row = lax.broadcasted_iota(jnp.int32, (8, GROUP), 0)
    meta[...] = jnp.transpose(
        jnp.where(row == 0, packed, jnp.where(row == 1, first, packed - first)).astype(F32)
    )

    def table(i, carry):
        at = pl.ds(pl.multiple_of(i * 128, 128), 128)
        angles = meta[at, 2:3] * inverse[...]
        lane = lax.broadcasted_iota(jnp.int32, angles.shape, 1)
        sines = jnp.sin(angles)
        cos_of[at, :] = jnp.cos(angles)
        sin_of[at, :] = jnp.where(lax.rem(lane, 64) < 32, -sines, sines)
        return carry

    lax.fori_loop(0, 8, table, 0)


def mask_bias(bias, half, chips, meta, places):
    keys = 512 * (half + 1)
    seen = places[:, :keys]
    here = of_both(meta, half, chips)
    allowed = (seen <= here[:, 0:1]) & (seen >= here[:, 1:2])
    bias[: 128 * len(chips), :keys] = jnp.where(allowed, 0.0, NEG_LARGE).astype(F32)


def attend(half, chips, q, kv, bias, o, log_sums):
    keys = 512 * (half + 1)
    k, v = kv[:keys, :64], kv[:keys, 64:]
    for h in range(HEADS // N_CTX):
        lanes = slice(h * 64, h * 64 + 64)
        scores = contract(of_both(q, half, chips, lanes), k, ACROSS) + bias[: 128 * len(chips), :keys]
        peak = jnp.max(scores, -1, keepdims=True)
        expo = jnp.exp(scores - peak)
        total = jnp.sum(expo, -1, keepdims=True)
        out = (contract(expo.astype(BF), v, PLAIN) / total).astype(BF)
        for i in range(2 * len(chips)):
            o[group_rows(chips[i // 2], i % 2, half), lanes] = out[64 * i : 64 * i + 64]
        to_both(log_sums, half, chips, slice(h, h + 1), peak + jnp.log(total))


def column(row):
    i = lax.broadcasted_iota(jnp.int32, (16, 16), 0)
    j = lax.broadcasted_iota(jnp.int32, (16, 16), 1)
    return jnp.sum(jnp.where(i == j, row[...].astype(F32), 0.0), 1, keepdims=True)


def spread():
    j = lax.broadcasted_iota(jnp.int32, (FF_CUT, FF_LOC), 0)
    to = lax.broadcasted_iota(jnp.int32, (FF_CUT, FF_LOC), 1)
    return jnp.where(FF_PAD * lax.div(j, FF_PART) + lax.rem(j, FF_PART) == to, 1.0, 0.0).astype(BF)


def forward_kernel(
    lengths, spans, inverse, gain_attn, gain_mlp, w_query, w_key, w_value, w_out_own, w_gate, w_up,
    w_down, tokens, cot,
    n1_out, w_qkv_out, w_out_out, w_gu, w_dn, cot_full, n2_full,
    h1, q, kv, o, log_sums, cos_of, sin_of, meta, places,
    n1_own, qkv_src, od_src, gu_src, stack, n1, w_qkv, od_mid, w_od, w_out, bias, part, n2, pair, half_left, half_right, from_left, from_right,
    ss, rs, ls,
):
    me = Place()

    def prepare():
        def norm(i, carry):
            at = pl.ds(pl.multiple_of(i * 16, 16), 16)
            x = tokens[at, :].astype(F32)
            scale = lax.rsqrt(jnp.mean(x * x, -1, keepdims=True) + EPSILON)
            n1_own[at, :] = (x * scale).astype(BF)
            return carry

        lax.fori_loop(0, 8, norm, 0)
        gain = column(gain_attn)
        for i in range(8):
            pair = slice(64 * (i // 2), 64 * (i // 2) + 64)
            scaled = w_query[:, Q_LOC * i : Q_LOC * i + Q_LOC].astype(F32) * gain
            qkv_src[i, :, :Q_LOC] = scaled.astype(BF)
            both = jnp.concatenate([w_key[:, pair], w_value[:, pair]], 1).astype(F32) * gain
            qkv_src[i, :, Q_LOC:] = both.astype(BF)
        od_src[0] = w_out_own[...]
        od_src[1] = w_down[0:16, :]
        od_src[2] = w_down[16:32, :]
        tail = jnp.concatenate([w_down[32:FF_PART, :].astype(F32), jnp.zeros((4, D), F32)], 0)
        od_src[3] = tail.astype(BF)

    greet(ctx_peers(me) + yz_peers(me), me.spread_from(), me.spreads(), prepare)
    copies = Copies(ss, rs)
    keep = keeper(ls)

    def to_indices(src, home):
        sent = [
            copies.send(src.at[lax.rem(me.c + s, 8)], home.at[me.c], me.on_ctx(s))
            for s in range(1, 8)
        ]
        mine = keep(src.at[me.c], home.at[me.c])
        mine.start()

        def wait():
            for copy in sent:
                copy.wait_recv()
            mine.wait()

        return wait

    qkv_there = to_indices(qkv_src, w_qkv.at[me.z, me.y])
    spread_start, spread_there = hop(copies, keep, od_src, od_mid, me.spread_to(), me.spreads())
    turns = [
        hop(copies, keep, od_mid.at[0], w_od.at[me.z, me.y], me.turn_to(), me.turns()),
        hop(copies, keep, od_mid.at[pl.ds(1, 3)], w_dn.at[me.z, me.y], me.turn_to(), me.turns()),
    ]
    spread_start()
    rows = ctx_gather(me, copies, n1_own, n1, keep)
    next(rows)

    def steps(flows):
        for flow in flows:
            next(flow, None)

    f_qkv = [dp_gather(me, copies, w_qkv, h, True) for h in (0, 1)]
    f_out = [dp_gather(me, copies, w_od, h, False) for h in (0, 1)]
    f_gu = [dp_gather(me, copies, w_gu, h, True) for h in (0, 1)]
    f_dn = [dp_gather(me, copies, w_dn, h, False) for h in (0, 1)]
    seeds = ctx_gather(me, copies, cot, cot_full, keep)
    qkv_there()
    steps(f_qkv)
    gain = column(gain_mlp)
    for j, w in enumerate((w_gate, w_up)):
        for i in range(8):
            scaled = w[:, FF_CUT * i : FF_CUT * i + FF_CUT].astype(F32) * gain
            stack[16 * i : 16 * i + 16, :] = scaled.astype(BF)
        placed = contract(stack[...], spread(), PLAIN).astype(BF)
        gu_src[:, :, FF_LOC * j : FF_LOC * j + FF_LOC] = placed.reshape(8, 16, FF_LOC)
    spread_there()
    turns[0][0]()
    steps(f_qkv)
    next(rows)
    turns[1][0]()
    gu_there = to_indices(gu_src, w_gu.at[me.z, me.y])
    turns[0][1]()
    steps(f_out)
    steps(f_qkv)
    steps(f_out)
    next(rows)
    lay_out(lengths, spans, inverse, meta, places, cos_of, sin_of)
    steps(f_out)
    steps(f_qkv)
    next(rows)
    turns[1][1]()
    steps(f_dn)
    gu_there()
    steps(f_gu)
    next(seeds)
    next(rows, None)
    keeps = [keep(n1, n1_out), keep(w_qkv, w_qkv_out)]
    for copy in keeps:
        copy.start()

    def project(chip, carry):
        x = n1[pl.ds(2 * chip, 2)].reshape(256, D)
        qkv = contract(x, w_qkv[...].reshape(D, QKV_LOC), PLAIN)
        for half, rows_of in enumerate(split_halves(qkv)):
            at = half_rows(half, chip)
            cos_b, sin_b = cos_of[at, :], sin_of[at, :]
            for j in (0, 1):
                turned = turn(rows_of[:, j * 128 : j * 128 + 128], cos_b, sin_b)
                q[at, j * 128 : j * 128 + 128] = (turned * HEAD_DIM ** (-0.5)).astype(BF)
            kv[at, :] = turn(rows_of[:, Q_LOC:], *keys_only(cos_b, sin_b)).astype(BF)
        return carry

    lax.fori_loop(0, 4, project, 0)
    steps(f_out)
    steps(f_dn)
    steps(f_gu)

    def place(i, carry):
        w_out[block_at(i, me.c)] = w_od[lax.div(i, 4), lax.rem(i, 4)]
        return carry

    lax.fori_loop(0, 16, place, 0)
    keeps.append(keep(w_out, w_out_out))
    keeps[-1].start()
    sums = CtxScatter(
        me, copies, part, pair, half_left, half_right, from_left, from_right
    )

    def heads_of(half, *steps_away):
        chips = [me.at_x(s) for s in steps_away]
        mask_bias(bias, half, chips, meta, places)
        attend(half, chips, q, kv, bias, o, log_sums)

    def out_of(s):
        at = pl.ds(pl.multiple_of(me.at_x(s) * 256, 256), 256)
        term = contract(o[at, :], w_out[...].reshape(Q_LOC, D), PLAIN).astype(BF)
        part[pl.ds(me.at_x(s) * 2, 2)] = term.reshape(2, 128, D)
        sums.give(s)

    heads_of(0, 2, 1)
    next(seeds)
    heads_of(1, 2, 1)
    out_of(2)
    out_of(1)
    steps(f_dn)
    heads_of(0, 3)
    sums.merge(2)
    sums.merge(1)
    next(seeds)
    heads_of(1, 3)
    out_of(3)
    sums.relay_right()
    steps(f_gu)
    heads_of(0, 0)
    sums.merge(3)
    sums.relay_left()
    next(seeds)
    heads_of(1, 0)
    out_of(0)
    sums.merge(0)
    sums.finish()

    def norm(i, carry):
        at = pl.ds(pl.multiple_of(i * 16, 16), 16)
        hidden = tokens[at, :].astype(F32) + scattered(at, pair, from_left, from_right)
        scale = lax.rsqrt(jnp.mean(hidden * hidden, -1, keepdims=True) + EPSILON)
        h1[at, :] = hidden
        n2[at, :] = (hidden * scale).astype(BF)
        return carry

    lax.fori_loop(0, 8, norm, 0)
    normed = ctx_gather(me, copies, n2, n2_full, keep)
    next(normed)
    round_robin(normed, seeds, *f_dn, *f_gu)
    for copy in keeps:
        copy.wait()
    copies.finish()


def ffn_kernel(
    n2_in, cot_in, w_gu_in, w_dn_in, h1, cot, dh1, da_full, part_y, g_gu, own_dn_out,
    n2, cot_full, w_gu, w_dn, hm, dgu, part, part_out, g_gu_own, g_nat, g_dn, da, own_dn, *rest,
):
    ss, rs, ls = rest[-3:]
    scr, scr_dn = rest[0:5], rest[5:15]
    me = Place()
    copies, keep = Copies(ss, rs), keeper(ls)
    loads = {}

    def load(name, src, dst):
        loads[name] = keep(src, dst)
        loads[name].start()

    def two(s):
        return pl.ds(me.at_x(s) * 2, 2)

    load("n2", n2_in.at[two(2)], n2.at[two(2)])
    load("gu", w_gu_in, w_gu)
    load("cot", cot_in.at[two(2)], cot_full.at[two(2)])
    for p in range(16):
        load(("dn", p), w_dn_in.at[p // 4, p % 4], w_dn.at[block_at(p, me.c)])
    for s in (1, 3, 0):
        load(("n2", s), n2_in.at[two(s)], n2.at[two(s)])
        load(("cot", s), cot_in.at[two(s)], cot_full.at[two(s)])
    greet(x_peers(me) + yz_peers(me))
    sums = CtxScatter(me, copies, part, *scr)

    def gate_up(s):
        at = pl.ds(pl.multiple_of(me.at_x(s) * 256, 256), 256)
        x = n2[two(s)].reshape(256, D)
        gate = contract(x, w_gu[..., :FF_LOC].reshape(D, FF_LOC), PLAIN)
        up = contract(x, w_gu[..., FF_LOC:].reshape(D, FF_LOC), PLAIN)
        sig = jax.nn.sigmoid(gate)
        silu = gate * sig
        hm[at, :] = (silu * up).astype(BF)
        inner = contract(cot_full[two(s)].reshape(256, D), w_dn[...].reshape(FF_LOC, D), ACROSS)
        dgu[at, :FF_LOC] = (inner * up * (sig + silu * (1.0 - sig))).astype(BF)
        dgu[at, FF_LOC:] = (inner * silu).astype(BF)
        term = contract(dgu[at, :], w_gu[...].reshape(D, 2 * FF_LOC), ACROSS).astype(BF)
        part[two(s)] = term.reshape(2, 128, D)
        sums.give(s)

    loads["n2"].wait()
    loads["gu"].wait()
    loads["cot"].wait()
    for p in range(16):
        loads["dn", p].wait()
    gate_up(2)
    loads["n2", 1].wait()
    loads["cot", 1].wait()
    gate_up(1)
    sums.merge(2)
    sums.merge(1)
    loads["n2", 3].wait()
    loads["cot", 3].wait()
    gate_up(3)
    sums.merge(3)
    sums.relay_right()
    sums.relay_left()
    loads["n2", 0].wait()
    loads["cot", 0].wait()
    gate_up(0)

    for j in (0, 1):
        for i in (0, 1):
            cols = slice(1024 * i, 1024 * i + 1024)
            term = contract(
                hm[:, 384 * j : 384 * j + 384], cot_full[:, :, cols].reshape(GROUP, 1024), DOWNWARD
            )
            g_nat[8 * j : 8 * j + 8, :, :, cols] = term.astype(BF).reshape(8, 3, 16, 1024)

    def place(i, carry):
        g_dn[lax.div(i, 4), lax.rem(i, 4)] = g_nat[block_at(i, me.c)]
        return carry

    lax.fori_loop(0, 16, place, 0)
    flows = [
        dp_scatter(me, copies, g_dn, h, False, own_dn, *scr_dn[h * 5 : h * 5 + 5]) for h in (0, 1)
    ]
    for flow in flows:
        next(flow)

    sums.merge(0)
    sums.finish()

    def norm_back(i, carry):
        at = pl.ds(pl.multiple_of(i * 16, 16), 16)
        hidden = h1[at, :]
        scale = lax.rsqrt(jnp.mean(hidden * hidden, -1, keepdims=True) + EPSILON)
        u = scattered(at, scr[0], scr[3], scr[4])
        grad = (
            cot[at, :].astype(F32)
            + scale * u
            - hidden * (scale * scale * scale * jnp.mean(u * hidden, -1, keepdims=True))
        )
        dh1[at, :] = grad
        da[at, :] = grad.astype(BF)
        return carry

    lax.fori_loop(0, 8, norm_back, 0)
    rows_da = ctx_gather(me, copies, da, da_full, keep)
    next(rows_da)
    kept = []

    def outer(j):
        at = pl.ds(256 * j, 256)
        term = contract(n2[:, :, at].reshape(GROUP, 256), dgu[...], DOWNWARD)
        where = (j // 2, pl.ds(2 * (j % 2), 2))
        g_gu_own[where] = term.astype(BF).reshape(2, 8, 16, 2 * FF_LOC)
        kept.append(keep(g_gu_own.at[where], g_gu.at[where]))
        kept[-1].start()

    def down(i, carry):
        at = pl.ds(pl.multiple_of(i * 256, 256), 256)
        y = contract(hm[at, :], w_dn[...].reshape(FF_LOC, D), PLAIN).astype(BF)
        part_out[pl.ds(2 * i, 2)] = y.reshape(2, 128, D)
        return carry

    lax.fori_loop(0, 4, down, 0)
    kept.append(keep(part_out, part_y))
    kept[-1].start()
    outer(0)
    next(rows_da)
    for flow in flows:
        next(flow)
    outer(1)
    outer(2)
    next(rows_da)
    outer(3)
    outer(4)
    next(rows_da)
    for flow in flows:
        next(flow)
    for j in (5, 6, 7):
        outer(j)
    round_robin(rows_da, *flows)
    kept.append(keep(own_dn, own_dn_out))
    kept[-1].start()
    for copy in kept:
        copy.wait()
    copies.finish()


def attend_back(half, chips, q, kv, do, log_sums, deltas, bias, dqkv, dk, dv):
    keys = 512 * (half + 1)
    k, v = kv[:keys, :64], kv[:keys, 64:]
    logs, delta = of_both(log_sums, half, chips), of_both(deltas, half, chips)
    for h in range(HEADS // N_CTX):
        lanes = slice(h * 64, h * 64 + 64)
        queries, grads = of_both(q, half, chips, lanes), of_both(do, half, chips, lanes)
        scores = contract(queries, k, ACROSS) + bias[: 128 * len(chips), :keys]
        probs = jnp.exp(scores - logs[:, h : h + 1])
        score_grad = probs * (contract(grads, v, ACROSS) - delta[:, h : h + 1])
        score_grad = score_grad.astype(BF)
        rows = contract(score_grad, k, PLAIN) * HEAD_DIM ** (-0.5)
        to_both(dqkv, half, chips, lanes, rows)
        dk[:keys, :] += contract(score_grad, queries, DOWNWARD)
        dv[:keys, :] += contract(probs.astype(BF), grads, DOWNWARD)


def end_kernel(
    da_in, part_y_in, g_gu_in, n1_in, w_qkv_in, w_out_in, own_dn,
    q, kv, o, log_sums, cos_of, sin_of, meta, places, h1, dh1, tokens,
    block_out, grad, ret_gu, ret_qkv, ret_out, ret_dn,
    da, part_y, g_gu, n1, w_qkv, w_out, do, deltas, dqkv, dqkv_low, dk, dv, bias,
    g_qkv, g_nat, g_out, own_gu, own_qkv, own_out, mid_out, mid_dn, *rest,
):
    ss, rs, ls = rest[-3:]
    scr_y, scr = rest[0:5], rest[5:10]
    scr_gu, scr_qkv, scr_out = rest[10:20], rest[20:30], rest[30:40]
    me = Place()
    copies, keep = Copies(ss, rs), keeper(ls)

    def load(src, dst):
        copy = keep(src, dst)
        copy.start()
        return copy

    load_y = load(part_y_in, part_y)
    load_out = load(w_out_in, w_out)
    load_da = load(da_in, da)
    load_gu = load(g_gu_in, g_gu)
    load_qkv = load(w_qkv_in, w_qkv)
    load_n1 = load(n1_in, n1)
    greet(ctx_peers(me) + yz_peers(me), me.spread_to(), me.spreads())
    load_y.wait()
    sums_y = CtxScatter(me, copies, part_y, *scr_y)
    for s in (2, 1, 3, 0):
        sums_y.give(s)
    turn_dn = hop(copies, keep, own_dn, mid_dn, me.turn_to(), me.turns())
    home_dn = hop(copies, keep, mid_dn, ret_dn, me.spread_from(), me.spreads())
    turn_dn[0]()
    load_out.wait()
    load_da.wait()
    load_gu.wait()

    def scatter(g, scratch, own, by_rows):
        return [
            dp_scatter(me, copies, g, h, by_rows, own, *scratch[h * 5 : h * 5 + 5]) for h in (0, 1)
        ]

    def steps(flows):
        for flow in flows:
            next(flow, None)

    f_gu = scatter(g_gu, scr_gu, own_gu, True)
    steps(f_gu)

    def attended_grad(i, carry):
        at = pl.ds(pl.multiple_of(i * 256, 256), 256)
        x = da[pl.ds(2 * i, 2)].reshape(256, D)
        grads = contract(x, w_out[...].reshape(Q_LOC, D), ACROSS).astype(BF)
        both = grads.astype(F32) * o[at, :].astype(F32)
        delta = [
            jnp.sum(both[:, h * 64 : h * 64 + 64], -1, keepdims=True)
            for h in range(HEADS // N_CTX)
        ]
        for ref, values in ((do, grads), (deltas, jnp.concatenate(delta, 1))):
            for half, rows_of in enumerate(split_halves(values)):
                ref[half_rows(half, i), :] = rows_of
        return carry

    lax.fori_loop(0, 4, attended_grad, 0)
    sums_y.merge(2)
    sums_y.merge(1)
    sums_y.merge(3)
    for i in (0, 1):
        cols = slice(1024 * i, 1024 * i + 1024)
        term = contract(o[...], da[:, :, cols].reshape(GROUP, 1024), DOWNWARD)
        g_nat[:, :, cols] = term.astype(BF).reshape(16, 16, 1024)

    def place(i, carry):
        g_out[lax.div(i, 4), lax.rem(i, 4)] = g_nat[block_at(i, me.c)]
        return carry

    lax.fori_loop(0, 16, place, 0)
    dk[...] = jnp.zeros_like(dk)
    dv[...] = jnp.zeros_like(dv)

    def to_indices(own, back):
        sent = [
            copies.send(own.at[lax.rem(me.c + s, 8)], back.at[me.c], me.on_ctx(s))
            for s in range(1, 8)
        ]
        mine = keep(own.at[me.c], back.at[me.c])
        mine.start()

        def wait():
            for copy in sent:
                copy.wait_recv()
            mine.wait()

        return wait

    def heads_of(half, *chips):
        mask_bias(bias, half, chips, meta, places)
        attend_back(half, chips, q, kv, do, log_sums, deltas, bias, dqkv, dk, dv)

    heads_of(1, 0, 1)
    steps(f_gu)
    f_out = scatter(g_out, scr_out, own_out, False)
    steps(f_out)
    turn_dn[1]()
    home_dn[0]()
    sums_y.relay_right()
    sums_y.relay_left()
    sums_y.merge(0)
    heads_of(0, 0, 1)
    sums_y.finish()

    def finish_y(i, carry):
        at = pl.ds(pl.multiple_of(i * 16, 16), 16)
        block_out[at, :] = (h1[at, :] + scattered(at, scr_y[0], scr_y[3], scr_y[4])).astype(BF)
        return carry

    lax.fori_loop(0, 8, finish_y, 0)
    heads_of(1, 2, 3)
    steps(f_gu)
    steps(f_out)
    heads_of(0, 2, 3)
    load_qkv.wait()
    dqkv[:, Q_LOC : Q_LOC + 64] = dk[...]
    dqkv[:, Q_LOC + 64 :] = dv[...]

    def turn_back(chip, carry):
        for half in (0, 1):
            at = half_rows(half, chip)
            cos_b, sin_b = cos_of[at, :], -sin_of[at, :]
            turned = [turn(dqkv[at, j * 128 : j * 128 + 128], cos_b, sin_b) for j in (0, 1)]
            turned.append(turn(dqkv[at, Q_LOC:], *keys_only(cos_b, sin_b)))
            turned = jnp.concatenate(turned, 1).astype(BF)
            for core in (0, 1):
                rows_of = turned[64 * core : 64 * core + 64]
                dqkv_low[group_rows(chip, core, half), :] = rows_of
        return carry

    lax.fori_loop(0, 4, turn_back, 0)
    part = part_y
    for s in (2, 1, 3, 0):
        copies.sent(sums_y.arriving[s])
    sums = CtxScatter(me, copies, part, *scr)

    def rows_of(s):
        at = pl.ds(pl.multiple_of(me.at_x(s) * 256, 256), 256)
        term = contract(dqkv_low[at, :], w_qkv[...].reshape(D, QKV_LOC), ACROSS).astype(BF)
        part[pl.ds(me.at_x(s) * 2, 2)] = term.reshape(2, 128, D)
        sums.give(s)

    rows_of(2)
    rows_of(1)
    sums.merge(2)
    rows_of(3)
    sums.merge(1)
    sums.merge(3)
    rows_of(0)
    steps(f_gu)
    gu_back = to_indices(own_gu, ret_gu)
    steps(f_out)
    load_n1.wait()

    def outer(j, carry):
        at = pl.ds(pl.multiple_of(256 * j, 256), 256)
        term = contract(n1[:, :, at].reshape(GROUP, 256), dqkv_low[...], DOWNWARD)
        where = (lax.div(j, 2), pl.ds(2 * lax.rem(j, 2), 2))
        g_qkv[where] = term.astype(BF).reshape(2, 8, 16, QKV_LOC)
        return carry

    lax.fori_loop(0, 8, outer, 0)
    f_qkv = scatter(g_qkv, scr_qkv, own_qkv, True)
    steps(f_qkv)
    sums.relay_right()
    sums.relay_left()
    sums.merge(0)
    steps(f_qkv)
    steps(f_out)
    turn_out = hop(copies, keep, own_out, mid_out, me.turn_to(), me.turns())
    home_out = hop(copies, keep, mid_out, ret_out, me.spread_from(), me.spreads())
    turn_out[0]()
    steps(f_qkv)
    turn_out[1]()
    home_out[0]()
    sums.finish()

    def finish(i, carry):
        at = pl.ds(pl.multiple_of(i * 16, 16), 16)
        x = tokens[at, :].astype(F32)
        scale = lax.rsqrt(jnp.mean(x * x, -1, keepdims=True) + EPSILON)
        u = scattered(at, scr[0], scr[3], scr[4])
        grad[at, :] = (
            dh1[at, :]
            + scale * u
            - x * (scale * scale * scale * jnp.mean(u * x, -1, keepdims=True))
        )
        return carry

    lax.fori_loop(0, 8, finish, 0)
    steps(f_qkv)
    steps(f_qkv)
    qkv_back = to_indices(own_qkv, ret_qkv)
    gu_back()
    home_dn[1]()
    home_out[1]()
    qkv_back()
    copies.finish()


def finish_kernel(
    ret_gu, ret_qkv, ret_out, ret_dn, block_in, grad_in, gain_attn, gain_mlp,
    w_query, w_key, w_value, w_gate, w_up,
    block_out, grad, d_gain_attn, d_query, d_key, d_value, d_out, d_gain_mlp, d_gate, d_up, d_down,
):
    block_out[...] = block_in[...]
    grad[...] = grad_in[...]
    d_out[...] = ret_out[...].astype(F32)
    for i in range(3):
        n = min(16, FF_PART - 16 * i)
        d_down[16 * i : 16 * i + n, :] = ret_dn[i].astype(F32)[:n]

    def as_row(values):
        i = lax.broadcasted_iota(jnp.int32, (16, 16), 0)
        j = lax.broadcasted_iota(jnp.int32, (16, 16), 1)
        return jnp.sum(jnp.where(i == j, values, 0.0), 0, keepdims=True)

    def give(out, weights, lanes, raw, gain):
        out[:, lanes] = raw * gain
        return jnp.sum(weights[:, lanes].astype(F32) * raw, 1, keepdims=True)

    gain, total = column(gain_attn), jnp.zeros((16, 1), F32)
    for i in range(8):
        lanes = slice(Q_LOC * i, Q_LOC * i + Q_LOC)
        total += give(d_query, w_query, lanes, ret_qkv[i, :, :Q_LOC].astype(F32), gain)
    for i in range(4):
        both = ret_qkv[2 * i, :, Q_LOC:].astype(F32) + ret_qkv[2 * i + 1, :, Q_LOC:].astype(F32)
        lanes = slice(64 * i, 64 * i + 64)
        total += give(d_key, w_key, lanes, both[:, :64], gain)
        total += give(d_value, w_value, lanes, both[:, 64:], gain)
    d_gain_attn[...] = as_row(total)
    gain, total = column(gain_mlp), jnp.zeros((16, 1), F32)
    for j, (out, weights) in enumerate(((d_gate, w_gate), (d_up, w_up))):
        placed = ret_gu[:, :, FF_LOC * j : FF_LOC * j + FF_LOC].reshape(128, FF_LOC)
        raw = contract(placed, spread(), ACROSS)
        for i in range(8):
            lanes = slice(FF_CUT * i, FF_CUT * i + FF_CUT)
            total += give(out, weights, lanes, raw[16 * i : 16 * i + 16], gain)
    d_gain_mlp[...] = as_row(total)


def call(kernel, number, ins, in_specs, outs, out_specs, scratch, n_copies, n_local):
    return pl.pallas_call(
        kernel,
        out_shape=[jax.ShapeDtypeStruct(*o) for o in outs],
        in_specs=in_specs,
        out_specs=out_specs,
        scratch_shapes=[
            *scratch,
            pltpu.SemaphoreType.DMA((n_copies,)),
            pltpu.SemaphoreType.DMA((n_copies,)),
            pltpu.SemaphoreType.DMA((n_local,)),
        ],
        compiler_params=pltpu.CompilerParams(
            collective_id=number, has_side_effects=True, vmem_limit_bytes=60 << 20
        ),
        name=kernel.__name__,
    )(*ins)


def per_device(
    tokens, cotangent, lengths, spans, gain_attn, w_query, w_key, w_value, w_out, gain_mlp,
    w_gate, w_up, w_down,
):
    pair = (2 * (np.arange(128) % 32)).astype(np.float32)
    inverse = np.power(np.float32(10000.0), -pair / np.float32(HEAD_DIM)).astype(np.float32)[None]
    gain_a, gain_m = gain_attn[None], gain_mlp[None]

    n1, wf_qkv, wf_out, wf_gu, wf_dn, cot_full, n2, h1, q, kv, o, log_sums, *tables = call(
        forward_kernel, 1,
        (lengths, spans.reshape(1, 16), jnp.asarray(inverse), gain_a, gain_m, w_query, w_key,
         w_value, w_out, w_gate, w_up, w_down, tokens, cotangent),
        [SM] * 2 + [VM] * 11 + [ANY],
        [((8, 128, D), BF), ((4, 4, 8, 16, QKV_LOC), BF), ((16, 16, D), BF),
         ((4, 4, 8, 16, 2 * FF_LOC), BF), ((4, 4, 3, 16, D), BF), ((8, 128, D), BF),
         ((8, 128, D), BF), ((128, D), F32), ((GROUP, Q_LOC), BF), ((GROUP, 128), BF),
         ((GROUP, Q_LOC), BF), ((GROUP, 4), F32), ((GROUP, 128), F32), ((GROUP, 128), F32),
         ((GROUP, 8), F32), ((1, GROUP), F32)],
        [ANY] * 7 + [VM] * 9,
        [pltpu.VMEM((128, D), BF), pltpu.VMEM((8, 16, QKV_LOC), BF), pltpu.VMEM((4, 16, D), BF),
         pltpu.VMEM((8, 16, 2 * FF_LOC), BF), pltpu.VMEM((128, FF_CUT), BF),
         pltpu.VMEM((8, 128, D), BF), pltpu.VMEM((4, 4, 8, 16, QKV_LOC), BF),
         pltpu.VMEM((4, 16, D), BF), pltpu.VMEM((4, 4, 16, D), BF), pltpu.VMEM((16, 16, D), BF),
         pltpu.VMEM((256, GROUP), F32),
         pltpu.VMEM((8, 128, D), BF), pltpu.VMEM((128, D), BF), *SCATTER_SCRATCH], 128, 16,
    )
    dh1, da, part_y, g_gu, own_dn = call(
        ffn_kernel, 2,
        (n2, cot_full, wf_gu, wf_dn, h1, cotangent), [ANY] * 4 + [VM] * 2,
        [((128, D), F32), ((8, 128, D), BF), ((8, 128, D), BF), ((4, 4, 8, 16, 2 * FF_LOC), BF),
         ((3, 16, D), BF)],
        [VM] + [ANY] * 4,
        [pltpu.VMEM((8, 128, D), BF), pltpu.VMEM((8, 128, D), BF),
         pltpu.VMEM((4, 4, 8, 16, 2 * FF_LOC), BF), pltpu.VMEM((16, 3, 16, D), BF),
         pltpu.VMEM((GROUP, FF_LOC), BF), pltpu.VMEM((GROUP, 2 * FF_LOC), BF),
         pltpu.VMEM((8, 128, D), BF), pltpu.VMEM((8, 128, D), BF),
         pltpu.VMEM((4, 4, 8, 16, 2 * FF_LOC), BF), pltpu.VMEM((16, 3, 16, D), BF),
         pltpu.VMEM((4, 4, 3, 16, D), BF), pltpu.VMEM((128, D), BF), pltpu.VMEM((3, 16, D), BF),
         *SCATTER_SCRATCH, *dp_scatter_scratch((3, 16, D), False)],
        64, 48,
    )

    block_low, grad, ret_gu, ret_qkv, ret_out, ret_dn = call(
        end_kernel, 3,
        (da, part_y, g_gu, n1, wf_qkv, wf_out, own_dn, q, kv, o, log_sums, *tables, h1, dh1, tokens),
        [ANY] * 7 + [VM] * 11,
        [((128, D), BF), ((128, D), F32), ((8, 16, 2 * FF_LOC), BF), ((8, 16, QKV_LOC), BF),
         ((16, D), BF), ((3, 16, D), BF)],
        [VM, VM, ANY, ANY, ANY, ANY],
        [pltpu.VMEM((8, 128, D), BF), pltpu.VMEM((8, 128, D), BF),
         pltpu.VMEM((4, 4, 8, 16, 2 * FF_LOC), BF), pltpu.VMEM((8, 128, D), BF),
         pltpu.VMEM((4, 4, 8, 16, QKV_LOC), BF), pltpu.VMEM((16, 16, D), BF),
         pltpu.VMEM((GROUP, Q_LOC), BF), pltpu.VMEM((GROUP, 4), F32),
         pltpu.VMEM((GROUP, QKV_LOC), F32),
         pltpu.VMEM((GROUP, QKV_LOC), BF), pltpu.VMEM((GROUP, 64), F32),
         pltpu.VMEM((GROUP, 64), F32), pltpu.VMEM((256, GROUP), F32),
         pltpu.VMEM((4, 4, 8, 16, QKV_LOC), BF),
         pltpu.VMEM((16, 16, D), BF), pltpu.VMEM((4, 4, 16, D), BF),
         pltpu.VMEM((8, 16, 2 * FF_LOC), BF), pltpu.VMEM((8, 16, QKV_LOC), BF),
         pltpu.VMEM((16, D), BF), pltpu.VMEM((16, D), BF), pltpu.VMEM((3, 16, D), BF),
         *SCATTER_SCRATCH, *SCATTER_SCRATCH, *dp_scatter_scratch((8, 16, 2 * FF_LOC), True),
         *dp_scatter_scratch((8, 16, QKV_LOC), True), *dp_scatter_scratch((16, D), False)],
        112, 32,
    )

    outs = [
        ((128, D), BF), ((128, D), F32), ((1, 16), F32), ((16, D), F32), ((16, 256), F32),
        ((16, 256), F32), ((16, D), F32), ((1, 16), F32), ((16, FF), F32), ((16, FF), F32),
        ((FF_PART, D), F32),
    ]
    outs = pl.pallas_call(
        finish_kernel,
        out_shape=[jax.ShapeDtypeStruct(*out) for out in outs],
        in_specs=[VM] * 13,
        out_specs=[VM] * 11,
        name="finish_kernel",
    )(ret_gu, ret_qkv, ret_out, ret_dn, block_low, grad, gain_a, gain_m, w_query, w_key, w_value,
      w_gate, w_up)
    return tuple(out.reshape(16) if out.shape == (1, 16) else out for out in outs)


def solution(mesh):
    flat = P(("dp", "ctx"), None)
    in_specs = (
        flat, flat, P("dp", None), P("dp", None, None), P(("dp", "ctx")), flat, flat, flat, flat,
        P(("dp", "ctx")), flat, flat, flat,
    )
    out_specs = (
        flat, flat, P(("dp", "ctx")), flat, flat, flat, flat, P(("dp", "ctx")), flat, flat, flat,
    )
    return jax.shard_map(
        per_device, mesh=mesh, in_specs=in_specs, out_specs=out_specs, check_vma=False
    )
```

```python
import jax
import jax.numpy as jnp
import numpy as np
from jax import lax
from jax.experimental import pallas as pl
from jax.experimental.pallas import tpu as pltpu
from jax.sharding import PartitionSpec as P

D = 2048
HEADS = 32
KV_HEADS = 4
HEAD_DIM = 64
FF = 5632
N_CTX = 8
N_DP = 16
ROWS = 128
GROUP = 1024
Q_LOC = 256
QKV_LOC = 384
FF_PART = 44
FF_PAD = 48
FF_LOC = N_DP * FF_PAD
FF_CUT = FF // N_CTX
EPSILON = 1e-05
NEG_LARGE = -1e30
MESH = pl.DeviceIdType.MESH
BF = jnp.bfloat16
F32 = jnp.float32
ANY = pl.BlockSpec(memory_space=pl.ANY)
VM = pl.BlockSpec(memory_space=pltpu.VMEM)
SM = pl.BlockSpec(memory_space=pltpu.SMEM)
ACROSS = (((1,), (1,)), ((), ()))
DOWNWARD = (((0,), (0,)), ((), ()))
PLAIN = (((1,), (0,)), ((), ()))


def contract(left_op, right_op, dims_pair):
    return lax.dot_general(left_op, right_op, dims_pair, preferred_element_type=F32)


class Place:
    def __init__(self):
        self.d = lax.axis_index("dp")
        self.c = lax.axis_index("ctx")
        self.z, self.y = lax.div(self.d, 4), lax.rem(self.d, 4)
        self.x, self.k = lax.div(self.c, 2), lax.rem(self.c, 2)

    def at_x(self, step):
        return lax.rem(self.x + step, 4)

    def on_x(self, step):
        return (self.d, self.at_x(step) * 2 + self.k)

    def sibling(self):
        return (self.d, self.x * 2 + 1 - self.k)

    def on_ctx(self, step):
        return (self.d, lax.rem(self.c + step, 8))

    def on_y(self, step):
        return (self.z * 4 + lax.rem(self.y + step, 4), self.c)

    def on_z(self, step):
        return (lax.rem(self.z + step, 4) * 4 + self.y, self.c)

    def spread_to(self):
        return (lax.rem(self.d + 2 * self.c, 16), self.c)

    def spread_from(self):
        return (lax.rem(self.d + 16 - 2 * self.c, 16), self.c)

    def spreads(self):
        return self.c != 0

    def turn_to(self):
        return (self.d, lax.rem(lax.div(self.d, 2) + 8 - self.c, 8))

    def turns(self):
        return self.turn_to()[1] != self.c


def block_at(position, index):
    return 8 * lax.rem(position, 2) + lax.rem(lax.div(position, 2) + 8 - index, 8)


class Copies:
    def __init__(self, send_sems, recv_sems):
        self.send_sems, self.recv_sems, self.used, self.started = send_sems, recv_sems, 0, []

    def make(self, src, dst, device):
        i = self.used
        self.used += 1
        return pltpu.make_async_remote_copy(
            src_ref=src,
            dst_ref=dst,
            send_sem=self.send_sems.at[i],
            recv_sem=self.recv_sems.at[i],
            device_id=device,
            device_id_type=MESH,
        )

    def send(self, src, dst, device):
        copy = self.make(src, dst, device)
        copy.start()
        self.started.append(copy)
        return copy

    def sent(self, copy):
        copy.wait_send()
        self.started = [other for other in self.started if other is not copy]

    def finish(self):
        for copy in self.started:
            copy.wait_send()


def greet(peers, extra=None, extra_on=None, meanwhile=lambda: None):
    barrier = pltpu.get_barrier_semaphore()
    for peer in peers:
        pl.semaphore_signal(barrier, 1, device_id=peer, device_id_type=MESH)
    count = len(peers)
    if extra is not None:

        @pl.when(extra_on)
        def _():
            pl.semaphore_signal(barrier, 1, device_id=extra, device_id_type=MESH)

        count = jnp.where(extra_on, count + 1, count)
    meanwhile()
    pl.semaphore_wait(barrier, count)


def hop(copies, keep, src, dst, device, far):
    sent, kept = copies.make(src, dst, device), keep(src, dst)

    def start():
        pl.when(far)(sent.start)
        pl.when(jnp.logical_not(far))(kept.start)

    def wait():
        pl.when(far)(sent.wait)
        pl.when(jnp.logical_not(far))(kept.wait)

    return start, wait


def keeper(sems):
    used = []

    def keep(src, dst):
        used.append(src)
        return pltpu.make_async_copy(src, dst, sems.at[len(used) - 1])

    return keep


def yz_peers(me):
    return [me.on_y(s) for s in (1, 2, 3)] + [me.on_z(s) for s in (1, 2, 3)]


def ctx_peers(me):
    return [me.on_ctx(s) for s in range(1, 8)]


def x_peers(me):
    return [me.on_x(1), me.on_x(3), me.sibling()]


def round_robin(*flows):
    flows = list(flows)
    while flows:
        flows = [f for f in flows if next(f, "end") != "end"]


class CtxGather:
    def __init__(self, me, copies, src, full, keep):
        self.me, self.copies, self.src, self.full = me, copies, src, full
        self.own, self.left, self.right, self.far_one = (
            me.at_x(s) * 2 + me.k for s in (0, 3, 1, 2)
        )
        self.to_right, self.to_left, self.to_sib = me.on_x(1), me.on_x(3), me.sibling()
        self.mine = keep(src, full.at[self.own])

    def pass_on(self, block, rows, device):
        at = self.full.at[block, rows]
        return self.copies.send(at, at, device)

    def start(self):
        top, low = pl.ds(0, 64), pl.ds(64, 64)
        src, home, send = self.src, self.full.at[self.own], self.copies.send
        self.r1 = send(src.at[top], home.at[top], self.to_right)
        self.l1 = send(src.at[low], home.at[low], self.to_left)
        self.s0 = send(src, home, self.to_sib)
        self.mine.start()

    def start_rest(self):
        top, low = pl.ds(0, 64), pl.ds(64, 64)
        src, home, send = self.src, self.full.at[self.own], self.copies.send
        self.r2 = send(src.at[low], home.at[low], self.to_right)
        self.l2 = send(src.at[top], home.at[top], self.to_left)

    def relay(self):
        self.r1.wait_recv()
        self.r3 = self.pass_on(self.left, pl.ds(0, 64), self.to_right)
        self.l1.wait_recv()
        self.l3 = self.pass_on(self.right, pl.ds(64, 64), self.to_left)

    def sides(self):
        self.r2.wait_recv()
        self.s1 = self.pass_on(self.left, pl.ds(0, 128), self.to_sib)
        self.l2.wait_recv()
        self.s2 = self.pass_on(self.right, pl.ds(0, 128), self.to_sib)

    def far(self):
        self.r3.wait_recv()
        self.s3 = self.pass_on(self.far_one, pl.ds(0, 64), self.to_sib)
        self.l3.wait_recv()
        self.s4 = self.pass_on(self.far_one, pl.ds(64, 64), self.to_sib)

    def wait_own(self):
        self.s0.wait_recv()
        self.mine.wait()

    def wait_sides(self):
        self.s1.wait_recv()
        self.s2.wait_recv()

    def wait_far(self):
        self.s3.wait_recv()
        self.s4.wait_recv()

    def settle(self):
        for copy in (self.r3, self.l3, self.s1, self.s2, self.s3, self.s4):
            self.copies.sent(copy)


def gather_steps(job):
    job.start()
    job.start_rest()
    yield
    job.relay()
    yield
    job.sides()
    yield
    job.far()
    yield
    job.wait_own()
    job.wait_sides()
    job.wait_far()


def ctx_gather(*args):
    return gather_steps(CtxGather(*args))


def add_rows(dst, rows, *terms):
    def step(i, carry):
        at = pl.ds(pl.multiple_of(i * 16, 16), 16)
        total = terms[0](at).astype(F32)
        for term in terms[1:]:
            total += term(at).astype(F32)
        dst[at, :] = total.astype(dst.dtype)
        return carry

    lax.fori_loop(0, rows // 16, step, 0)


class CtxScatter:
    def __init__(self, me, copies, part, pair, half_left, half_right, from_left, from_right):
        self.me, self.copies, self.part, self.pair = me, copies, part, pair
        self.half_left, self.half_right = half_left, half_right
        self.from_left, self.from_right = from_left, from_right
        self.to_right, self.to_left, self.to_sib = me.on_x(1), me.on_x(3), me.sibling()
        self.arriving = {}

    def give(self, s):
        block = self.me.at_x(s) * 2 + 1 - self.me.k
        self.arriving[s] = self.copies.send(self.part.at[block], self.pair.at[s], self.to_sib)

    def merge(self, s):
        top, low = pl.ds(0, 64), pl.ds(64, 64)
        self.arriving[s].wait_recv()
        block, pair, part = self.me.at_x(s) * 2 + self.me.k, self.pair, self.part
        add_rows(pair.at[s], 128, lambda at: part[block, at, :], lambda at: pair[s, at, :])
        send = self.copies.send
        if s == 2:
            self.a = send(pair.at[2, top], self.half_left, self.to_right)
            self.b = send(pair.at[2, low], self.half_right, self.to_left)
        if s == 1:
            self.r1 = send(pair.at[1, low], self.from_left.at[low], self.to_right)
        if s == 3:
            self.l1 = send(pair.at[3, top], self.from_right.at[top], self.to_left)

    def relay_right(self):
        half, pair = self.half_left, self.pair
        self.a.wait_recv()
        add_rows(half, 64, lambda at: half[at, :], lambda at: pair[1, at, :])
        self.r2 = self.copies.send(half, self.from_left.at[pl.ds(0, 64)], self.to_right)

    def relay_left(self):
        half, pair = self.half_right, self.pair
        self.b.wait_recv()
        add_rows(half, 64, lambda at: half[at, :], lambda at: pair.at[3, pl.ds(64, 64)][at, :])
        self.l2 = self.copies.send(half, self.from_right.at[pl.ds(64, 64)], self.to_left)

    def finish(self):
        for copy in (self.r1, self.l1, self.r2, self.l2):
            copy.wait_recv()

    def settle(self):
        for copy in (*self.arriving.values(), self.a, self.b, self.r1, self.l1, self.r2, self.l2):
            self.copies.sent(copy)


def ctx_scatter(*args):
    job = CtxScatter(*args)
    for s in (2, 1, 3, 0):
        job.give(s)
    yield
    for s in (2, 1, 3, 0):
        job.merge(s)
    yield
    job.relay_right()
    job.relay_left()
    yield
    job.finish()


SCATTER_SCRATCH = [
    pltpu.VMEM((4, 128, D), BF),
    pltpu.VMEM((64, D), BF),
    pltpu.VMEM((64, D), BF),
    pltpu.VMEM((128, D), BF),
    pltpu.VMEM((128, D), BF),
]


def scattered(at, pair, from_left, from_right):
    return (
        pair[0, at, :].astype(F32) + from_left[at, :].astype(F32) + from_right[at, :].astype(F32)
    )


def halves(ref, half, by_rows):
    shape = ref.shape
    if by_rows:
        n = shape[-3]
        return ref.at[(*(slice(None),) * (len(shape) - 3), pl.ds(half * (n // 2), n // 2))]
    columns = shape[-1]
    return ref.at[
        (*(slice(None),) * (len(shape) - 1), pl.ds(half * (columns // 2), columns // 2))
    ]


def dp_axes(me, half):
    z = (me.z, me.on_z)
    y = (me.y, me.on_y)
    return (y, z) if half else (z, y)


def dp_gather(me, copies, full, half, by_rows):
    view = halves(full, half, by_rows)
    (p2, dev2), (p1, dev1) = dp_axes(me, half)

    def group(i2, j1):
        return view.at[j1, i2] if half else view.at[i2, j1]

    own = group(p2, p1)
    first = [copies.send(own, own, dev1(s)) for s in (1, 3, 2)]
    yield
    for copy in first:
        copy.wait_recv()
    every, lo, hi = pl.ds(0, 4), pl.ds(0, 2), pl.ds(2, 2)
    mine = group(p2, every)
    up = copies.send(mine, mine, dev2(1))
    down = copies.send(mine, mine, dev2(3))
    yield
    up.wait_recv()
    passed = group(lax.rem(p2 + 3, 4), lo)
    up2 = copies.send(passed, passed, dev2(1))
    down.wait_recv()
    passed = group(lax.rem(p2 + 1, 4), hi)
    down2 = copies.send(passed, passed, dev2(3))
    yield
    up2.wait_recv()
    down2.wait_recv()
    yield
    for copy in (*first, up, down, up2, down2):
        copies.sent(copy)


def add_blocks(dst, *terms):
    lead = dst.shape[:-2]
    if not lead:
        total = terms[0][...].astype(F32)
        for term in terms[1:]:
            total += term[...].astype(F32)
        dst[...] = total.astype(dst.dtype)
        return

    def step(i, carry):
        at = (lax.div(i, lead[1]), lax.rem(i, lead[1])) if len(lead) == 2 else (i,)
        total = terms[0][at].astype(F32)
        for term in terms[1:]:
            total += term[at].astype(F32)
        dst[at] = total.astype(dst.dtype)
        return carry

    lax.fori_loop(0, lead[0] * (lead[1] if len(lead) == 2 else 1), step, 0)


def dp_scatter(
    me, copies, part, half, by_rows, out, pass_up, pass_down, from_up, from_down, last, sent_from=None
):
    view = halves(part, half, by_rows)
    sent_view = view if sent_from is None else halves(sent_from, half, by_rows)
    (p1, dev1), (p2, dev2) = dp_axes(me, half)

    def group(i1, j2, of=view):
        return of.at[j2, i1] if half else of.at[i1, j2]

    every, lo, hi = pl.ds(0, 4), pl.ds(0, 2), pl.ds(2, 2)
    nxt, far, prv = (lax.rem(p1 + s, 4) for s in (1, 2, 3))
    a = copies.send(group(far, lo, sent_view), pass_up, dev1(1))
    b = copies.send(group(far, hi, sent_view), pass_down, dev1(3))
    e1 = copies.send(group(nxt, hi, sent_view), from_up.at[hi], dev1(1))
    e2 = copies.send(group(prv, lo, sent_view), from_down.at[lo], dev1(3))
    yield
    a.wait_recv()
    add_blocks(pass_up, pass_up, group(nxt, lo))
    f1 = copies.send(pass_up, from_up.at[lo], dev1(1))
    b.wait_recv()
    add_blocks(pass_down, pass_down, group(prv, hi))
    f2 = copies.send(pass_down, from_down.at[hi], dev1(3))
    yield
    for copy in (e1, e2, f1, f2):
        copy.wait_recv()
    add_blocks(from_up, from_up, from_down, group(p1, every))
    sent = [
        copies.send(from_up.at[lax.rem(p2 + s, 4)], last.at[s - 1], dev2(s)) for s in (1, 2, 3)
    ]
    yield
    for copy in sent:
        copy.wait_recv()
    add_blocks(halves(out, half, by_rows), from_up.at[p2], last.at[0], last.at[1], last.at[2])


def dp_scatter_scratch(block, by_rows):
    block = (block[0] // 2, *block[1:]) if by_rows else (*block[:-1], block[-1] // 2)
    return [pltpu.VMEM((lead, *block), BF) for lead in (2, 2, 4, 4, 3)] * 2


def turn(values, cos_of, sin_of):
    lane = lax.broadcasted_iota(jnp.int32, values.shape, 1)
    other = jnp.where(
        lax.rem(lane, 64) < 32, pltpu.roll(values, 96, 1), pltpu.roll(values, 32, 1)
    )
    return values * cos_of + other * sin_of


def keys_only(cos_of, sin_of):
    lane = lax.broadcasted_iota(jnp.int32, cos_of.shape, 1)
    return jnp.where(lane < 64, cos_of, 1.0), jnp.where(lane < 64, sin_of, 0.0)


def split_halves(values):
    return (
        jnp.concatenate([values[0:64], values[128:192]], 0),
        jnp.concatenate([values[64:128], values[192:256]], 0),
    )


def half_rows(half, chip):
    return pl.ds(pl.multiple_of(half * 512 + chip * 128, 128), 128)


def of_both(ref, half, chips, lanes=slice(None)):
    pieces = [ref[half_rows(half, chip), lanes] for chip in chips]
    return jnp.concatenate(pieces, 0) if len(pieces) > 1 else pieces[0]


def to_both(ref, half, chips, lanes, values):
    for i, chip in enumerate(chips):
        ref[half_rows(half, chip), lanes] = values[128 * i : 128 * i + 128]


def group_rows(chip, core, half):
    return pl.ds(pl.multiple_of(chip * 256 + core * 128 + half * 64, 64), 64)


def lay_out(lengths, spans, inverse, meta, places, cos_of, sin_of):
    j = lax.broadcasted_iota(jnp.int32, (1, GROUP), 1)
    slot, packed = lax.div(j, 64), lax.rem(j, 64)
    for r in range(8):
        for half in range(2):
            packed = packed + jnp.where(slot == half * 8 + r, spans[0, 2 * r + half] * 64, 0)
    first, end = jnp.zeros_like(packed), 0
    for i in range(4):
        end = end + lengths[0, i]
        first = first + jnp.where(packed >= end, lengths[0, i], 0)
    places[...] = packed.astype(F32)
    row = lax.broadcasted_iota(jnp.int32, (8, GROUP), 0)
    meta[...] = jnp.transpose(
        jnp.where(row == 0, packed, jnp.where(row == 1, first, packed - first)).astype(F32)
    )

    def table(i, carry):
        at = pl.ds(pl.multiple_of(i * 128, 128), 128)
        angles = meta[at, 2:3] * inverse[...]
        lane = lax.broadcasted_iota(jnp.int32, angles.shape, 1)
        sines = jnp.sin(angles)
        cos_of[at, :] = jnp.cos(angles)
        sin_of[at, :] = jnp.where(lax.rem(lane, 64) < 32, -sines, sines)
        return carry

    lax.fori_loop(0, 8, table, 0)


def mask_bias(bias, half, chips, meta, places):
    keys = 512 * (half + 1)
    seen = places[:, :keys]
    here = of_both(meta, half, chips)
    allowed = (seen <= here[:, 0:1]) & (seen >= here[:, 1:2])
    bias[: 128 * len(chips), :keys] = jnp.where(allowed, 0.0, NEG_LARGE).astype(F32)


def attend(half, chips, q, kv, bias, o, log_sums):
    keys = 512 * (half + 1)
    k, v = kv[:keys, :64], kv[:keys, 64:]
    for h in range(HEADS // N_CTX):
        lanes = slice(h * 64, h * 64 + 64)
        scores = contract(of_both(q, half, chips, lanes), k, ACROSS) + bias[: 128 * len(chips), :keys]
        peak = jnp.max(scores, -1, keepdims=True)
        expo = jnp.exp(scores - peak)
        total = jnp.sum(expo, -1, keepdims=True)
        out = (contract(expo.astype(BF), v, PLAIN) / total).astype(BF)
        for i in range(2 * len(chips)):
            o[group_rows(chips[i // 2], i % 2, half), lanes] = out[64 * i : 64 * i + 64]
        to_both(log_sums, half, chips, slice(h, h + 1), peak + jnp.log(total))


def column(row):
    i = lax.broadcasted_iota(jnp.int32, (16, 16), 0)
    j = lax.broadcasted_iota(jnp.int32, (16, 16), 1)
    return jnp.sum(jnp.where(i == j, row[...].astype(F32), 0.0), 1, keepdims=True)


def spread():
    j = lax.broadcasted_iota(jnp.int32, (FF_CUT, FF_LOC), 0)
    to = lax.broadcasted_iota(jnp.int32, (FF_CUT, FF_LOC), 1)
    return jnp.where(FF_PAD * lax.div(j, FF_PART) + lax.rem(j, FF_PART) == to, 1.0, 0.0).astype(BF)


def front_kernel(
    lengths, spans, inverse, gain_attn, gain_mlp, w_query, w_key, w_value, w_out_own, w_gate, w_up,
    w_down, tokens, cot_own,
    n1_out, w_qkv_out, w_out_out, da_full, part_y, g_up, own_gate_out, own_dn_out,
    h1, dh1, q, kv, o, log_sums, cos_of, sin_of, meta, places,
    n1_own, qkv_src, od_src, gu_src, stack, n1, w_qkv, od_mid, w_out, bias, part,
    n2, cot_full, w_gu, w_dn, w_dn_here, hm, dgu, own_gate, own_dn, *rest,
):
    ss, rs, ls = rest[-3:]
    scr, scr_dn, scr_gate = rest[0:5], rest[5:15], rest[15:25]
    me = Place()
    w_od = w_dn_here.at[:, :, 0]

    def prepare():
        def norm(i, carry):
            at = pl.ds(pl.multiple_of(i * 16, 16), 16)
            x = tokens[at, :].astype(F32)
            scale = lax.rsqrt(jnp.mean(x * x, -1, keepdims=True) + EPSILON)
            n1_own[at, :] = (x * scale).astype(BF)
            return carry

        lax.fori_loop(0, 8, norm, 0)
        gain = column(gain_attn)
        for i in range(8):
            pair = slice(64 * (i // 2), 64 * (i // 2) + 64)
            scaled = w_query[:, Q_LOC * i : Q_LOC * i + Q_LOC].astype(F32) * gain
            qkv_src[i, :, :Q_LOC] = scaled.astype(BF)
            both = jnp.concatenate([w_key[:, pair], w_value[:, pair]], 1).astype(F32) * gain
            qkv_src[i, :, Q_LOC:] = both.astype(BF)
        od_src[0] = w_out_own[...]
        od_src[1] = w_down[0:16, :]
        od_src[2] = w_down[16:32, :]
        tail = jnp.concatenate([w_down[32:FF_PART, :].astype(F32), jnp.zeros((4, D), F32)], 0)
        od_src[3] = tail.astype(BF)
        gain = column(gain_mlp)
        for j, w in enumerate((w_gate, w_up)):
            for i in range(8):
                scaled = w[:, FF_CUT * i : FF_CUT * i + FF_CUT].astype(F32) * gain
                stack[16 * i : 16 * i + 16, :] = scaled.astype(BF)
            placed = contract(stack[...], spread(), PLAIN).astype(BF)
            gu_src[:, :, FF_LOC * j : FF_LOC * j + FF_LOC] = placed.reshape(8, 16, FF_LOC)

    greet(ctx_peers(me) + yz_peers(me), me.spread_from(), me.spreads(), prepare)
    copies = Copies(ss, rs)
    keep = keeper(ls)

    def to_indices(src, home):
        sent = [
            copies.send(src.at[lax.rem(me.c + s, 8)], home.at[me.c], me.on_ctx(s))
            for s in range(1, 8)
        ]
        mine = keep(src.at[me.c], home.at[me.c])
        mine.start()

        def wait():
            for copy in sent:
                copy.wait_recv()
            mine.wait()

        return wait

    qkv_there = to_indices(qkv_src, w_qkv.at[me.z, me.y])
    spread_start, spread_there = hop(
        copies, keep, od_src, od_mid, me.spread_to(), me.spreads()
    )
    turns = [
        hop(copies, keep, od_mid.at[0], w_od.at[me.z, me.y], me.turn_to(), me.turns()),
        hop(copies, keep, od_mid.at[pl.ds(1, 3)], w_dn.at[me.z, me.y], me.turn_to(), me.turns()),
    ]
    spread_start()
    gu_there = to_indices(gu_src, w_gu.at[me.z, me.y])
    rows = CtxGather(me, copies, n1_own, n1, keep)
    rows.start()

    def steps(flows):
        for flow in flows:
            next(flow, None)

    f_qkv = [dp_gather(me, copies, w_qkv, h, True) for h in (0, 1)]
    f_out = [dp_gather(me, copies, w_od, h, False) for h in (0, 1)]
    f_gu = [dp_gather(me, copies, w_gu, h, True) for h in (0, 1)]
    f_dn = [dp_gather(me, copies, w_dn, h, False) for h in (0, 1)]
    seeds = ctx_gather(me, copies, cot_own, cot_full, keep)
    qkv_there()
    steps(f_qkv)
    spread_there()
    for start, _ in turns:
        start()
    rows.start_rest()
    first_row_copies = (rows.r1, rows.l1, rows.s0, rows.r2, rows.l2)
    steps(f_qkv)
    gu_there()
    steps(f_qkv)
    rows.relay()
    turns[0][1]()
    steps(f_out)
    steps(f_gu)
    lay_out(lengths, spans, inverse, meta, places, cos_of, sin_of)
    turns[1][1]()
    steps(f_out)
    steps(f_dn)
    rows.sides()
    steps(f_qkv)
    rows.far()
    next(seeds)
    steps(f_out)
    steps(f_gu)
    rows.wait_own()
    rows.wait_sides()
    rows.wait_far()
    keeps = [keep(n1, n1_out), keep(w_qkv, w_qkv_out)]
    for copy in keeps:
        copy.start()

    def project(chip, carry):
        x = n1[pl.ds(2 * chip, 2)].reshape(256, D)
        qkv = contract(x, w_qkv[...].reshape(D, QKV_LOC), PLAIN)
        for half, rows_of in enumerate(split_halves(qkv)):
            at = half_rows(half, chip)
            cos_b, sin_b = cos_of[at, :], sin_of[at, :]
            for j in (0, 1):
                turned = turn(rows_of[:, j * 128 : j * 128 + 128], cos_b, sin_b)
                q[at, j * 128 : j * 128 + 128] = (turned * HEAD_DIM ** (-0.5)).astype(BF)
            kv[at, :] = turn(rows_of[:, Q_LOC:], *keys_only(cos_b, sin_b)).astype(BF)
        return carry

    lax.fori_loop(0, 4, project, 0)
    steps(f_out)
    steps(f_dn)

    def place(i, carry):
        w_out[block_at(i, me.c)] = w_od[lax.div(i, 4), lax.rem(i, 4)]
        return carry

    lax.fori_loop(0, 16, place, 0)
    keeps.append(keep(w_out, w_out_out))
    keeps[-1].start()
    sums = CtxScatter(me, copies, part, *scr)

    def heads_of(half, *steps_away):
        chips = [me.at_x(s) for s in steps_away]
        mask_bias(bias, half, chips, meta, places)
        attend(half, chips, q, kv, bias, o, log_sums)

    def out_of(s):
        at = pl.ds(pl.multiple_of(me.at_x(s) * 256, 256), 256)
        term = contract(o[at, :], w_out[...].reshape(Q_LOC, D), PLAIN).astype(BF)
        part[pl.ds(me.at_x(s) * 2, 2)] = term.reshape(2, 128, D)
        sums.give(s)

    heads_of(0, 2, 1)
    heads_of(1, 2, 1)
    next(seeds)
    out_of(2)
    out_of(1)
    heads_of(0, 3)
    sums.merge(2)
    sums.merge(1)
    next(seeds)
    heads_of(1, 3)
    out_of(3)
    steps(f_gu)
    heads_of(0, 0)
    sums.merge(3)
    sums.relay_right()
    sums.relay_left()
    next(seeds)
    heads_of(1, 0)
    out_of(0)
    sums.merge(0)
    steps(f_dn)
    sums.finish()
    sums.settle()
    own_norm = n1_own

    def norm(i, carry):
        at = pl.ds(pl.multiple_of(i * 16, 16), 16)
        hidden = tokens[at, :].astype(F32) + scattered(at, scr[0], scr[3], scr[4])
        scale = lax.rsqrt(jnp.mean(hidden * hidden, -1, keepdims=True) + EPSILON)
        h1[at, :] = hidden
        own_norm[at, :] = (hidden * scale).astype(BF)
        return carry

    for copy in first_row_copies:
        copies.sent(copy)
    lax.fori_loop(0, 8, norm, 0)
    normed = CtxGather(me, copies, own_norm, n2, keep)
    normed.start()
    normed.start_rest()
    steps(f_gu)
    steps(f_dn)
    next(seeds, None)

    steps(f_out)

    def place_down(i, carry):
        here = block_at(i, me.c)
        w_dn_here[lax.div(here, 4), lax.rem(here, 4)] = w_dn[lax.div(i, 4), lax.rem(i, 4)]
        return carry

    lax.fori_loop(0, 16, place_down, 0)
    sums = CtxScatter(me, copies, part, *scr)

    def two(s):
        return pl.ds(me.at_x(s) * 2, 2)

    def gate_up(s):
        at = pl.ds(pl.multiple_of(me.at_x(s) * 256, 256), 256)
        x = n2[two(s)].reshape(256, D)
        gate = contract(x, w_gu[..., :FF_LOC].reshape(D, FF_LOC), PLAIN)
        up = contract(x, w_gu[..., FF_LOC:].reshape(D, FF_LOC), PLAIN)
        sig = jax.nn.sigmoid(gate)
        silu = gate * sig
        hm[at, :] = (silu * up).astype(BF)
        inner = contract(
            cot_full[two(s)].reshape(256, D), w_dn_here[...].reshape(FF_LOC, D), ACROSS
        )
        dgu[at, :FF_LOC] = (inner * up * (sig + silu * (1.0 - sig))).astype(BF)
        dgu[at, FF_LOC:] = (inner * silu).astype(BF)
        term = contract(dgu[at, :], w_gu[...].reshape(D, 2 * FF_LOC), ACROSS).astype(BF)
        part[two(s)] = term.reshape(2, 128, D)
        sums.give(s)

    normed.wait_own()
    gate_up(0)
    normed.relay()
    normed.sides()
    normed.wait_sides()
    gate_up(1)
    normed.far()
    gate_up(3)
    sums.merge(1)
    sums.merge(3)
    normed.wait_far()
    gate_up(2)
    for copy in keeps:
        copy.wait()
    rows.settle()
    steps(f_gu)
    steps(f_dn)
    part_out = n1

    def outer(j, carry):
        at = pl.ds(pl.multiple_of(256 * j, 256), 256)
        term = contract(n2[:, :, at].reshape(GROUP, 256), dgu[...], DOWNWARD)
        where = (lax.div(j, 2), pl.ds(2 * lax.rem(j, 2), 2))
        w_gu[where] = term.astype(BF).reshape(2, 8, 16, 2 * FF_LOC)
        return carry

    lax.fori_loop(0, 4, outer, 0)
    sums.merge(2)
    lax.fori_loop(4, 8, outer, 0)
    gate_columns, up_columns = (
        w_gu.at[:, :, :, :, pl.ds(FF_LOC * j, FF_LOC)] for j in (0, 1)
    )
    f_gate = [
        dp_scatter(me, copies, gate_columns, h, True, own_gate, *scr_gate[h * 5 : h * 5 + 5])
        for h in (0, 1)
    ]
    steps(f_gate)
    kept = [keep(up_columns, g_up)]
    kept[0].start()

    def down(i, carry):
        at = pl.ds(pl.multiple_of(i * 256, 256), 256)
        y = contract(hm[at, :], w_dn_here[...].reshape(FF_LOC, D), PLAIN).astype(BF)
        part_out[pl.ds(2 * i, 2)] = y.reshape(2, 128, D)
        return carry

    lax.fori_loop(0, 4, down, 0)
    kept.append(keep(part_out, part_y))
    kept[-1].start()
    for j in (0, 1):
        for i in (0, 1):
            cols = slice(1024 * i, 1024 * i + 1024)
            term = contract(
                hm[:, 384 * j : 384 * j + 384], cot_full[:, :, cols].reshape(GROUP, 1024), DOWNWARD
            )
            w_dn_here[2 * j : 2 * j + 2, :, :, :, cols] = term.astype(BF).reshape(2, 4, 3, 16, 1024)

    def place_back(i, carry):
        here = block_at(i, me.c)
        w_dn[lax.div(i, 4), lax.rem(i, 4)] = w_dn_here[lax.div(here, 4), lax.rem(here, 4)]
        return carry

    lax.fori_loop(0, 16, place_back, 0)
    flows = [
        dp_scatter(me, copies, w_dn, h, False, own_dn, *scr_dn[h * 5 : h * 5 + 5]) for h in (0, 1)
    ]
    steps(flows)

    sums.relay_right()
    sums.relay_left()
    sums.merge(0)
    steps(f_gate)
    sums.finish()
    da = own_norm
    copies.sent(normed.s0)
    for copy in (normed.r1, normed.r2, normed.l1, normed.l2):
        copies.sent(copy)

    def norm_back(i, carry):
        at = pl.ds(pl.multiple_of(i * 16, 16), 16)
        hidden = h1[at, :]
        scale = lax.rsqrt(jnp.mean(hidden * hidden, -1, keepdims=True) + EPSILON)
        u = scattered(at, scr[0], scr[3], scr[4])
        grad = (
            cot_own[at, :].astype(F32)
            + scale * u
            - hidden * (scale * scale * scale * jnp.mean(u * hidden, -1, keepdims=True))
        )
        dh1[at, :] = grad
        da[at, :] = grad.astype(BF)
        return carry

    lax.fori_loop(0, 8, norm_back, 0)
    rows_da = ctx_gather(me, copies, da, da_full, keep)
    next(rows_da)
    steps(flows)
    steps(f_gate)
    next(rows_da)
    steps(flows)
    next(rows_da)
    steps(f_gate)
    steps(flows)
    next(rows_da)
    kept.append(keep(own_gate, own_gate_out))
    kept[-1].start()
    kept.append(keep(own_dn, own_dn_out))
    kept[-1].start()
    next(rows_da, None)
    for copy in kept:
        copy.wait()
    copies.finish()


def attend_back(half, chips, q, kv, do, log_sums, deltas, bias, dqkv, dk, dv):
    keys = 512 * (half + 1)
    k, v = kv[:keys, :64], kv[:keys, 64:]
    logs, delta = of_both(log_sums, half, chips), of_both(deltas, half, chips)
    for h in range(HEADS // N_CTX):
        lanes = slice(h * 64, h * 64 + 64)
        queries, grads = of_both(q, half, chips, lanes), of_both(do, half, chips, lanes)
        scores = contract(queries, k, ACROSS) + bias[: 128 * len(chips), :keys]
        probs = jnp.exp(scores - logs[:, h : h + 1])
        score_grad = probs * (contract(grads, v, ACROSS) - delta[:, h : h + 1])
        score_grad = score_grad.astype(BF)
        rows = contract(score_grad, k, PLAIN) * HEAD_DIM ** (-0.5)
        to_both(dqkv, half, chips, lanes, rows)
        dk[:keys, :] += contract(score_grad, queries, DOWNWARD)
        dv[:keys, :] += contract(probs.astype(BF), grads, DOWNWARD)


def end_kernel(
    da_in, part_y_in, g_up_in, n1_in, w_qkv_in, w_out_in, own_gate, own_dn,
    q, kv, o, log_sums, cos_of, sin_of, meta, places, h1, dh1, tokens,
    block_out, grad, ret_gate, ret_up, ret_qkv, ret_out, ret_dn,
    da, part_y, g_up, n1, w_qkv, w_out, do, deltas, dqkv, dqkv_low, dk, dv, bias,
    g_qkv, g_nat, g_out, own_up, own_qkv, own_out, mid_out, mid_dn, *rest,
):
    ss, rs, ls = rest[-3:]
    scr_y, scr = rest[0:5], rest[5:10]
    scr_up, scr_qkv, scr_out = rest[10:20], rest[20:30], rest[30:40]
    me = Place()
    copies, keep = Copies(ss, rs), keeper(ls)

    def load(src, dst):
        copy = keep(src, dst)
        copy.start()
        return copy

    load_y = load(part_y_in, part_y)
    load_out = load(w_out_in, w_out)
    load_da = load(da_in, da)
    load_up = load(g_up_in, g_up)
    load_qkv = load(w_qkv_in, w_qkv)
    load_n1 = load(n1_in, n1)
    greet(ctx_peers(me) + yz_peers(me), me.spread_to(), me.spreads())
    def steps(flows):
        for flow in flows:
            next(flow, None)


    def scatter(g, scratch, own, by_rows, sent_from=None):
        return [
            dp_scatter(me, copies, g, h, by_rows, own, *scratch[h * 5 : h * 5 + 5], sent_from)
            for h in (0, 1)
        ]

    def to_indices(own, back):
        sent = [
            copies.send(own.at[lax.rem(me.c + s, 8)], back.at[me.c], me.on_ctx(s))
            for s in range(1, 8)
        ]
        mine = keep(own.at[me.c], back.at[me.c])
        mine.start()

        def wait():
            for copy in sent:
                copy.wait_recv()
            mine.wait()

        return wait

    f_up = scatter(g_up, scr_up, own_up, True, g_up_in)
    steps(f_up)
    gate_back = to_indices(own_gate, ret_gate)
    load_y.wait()
    sums_y = CtxScatter(me, copies, part_y, *scr_y)
    for s in (2, 1, 3, 0):
        sums_y.give(s)
    turn_dn = hop(copies, keep, own_dn, mid_dn, me.turn_to(), me.turns())
    home_dn = hop(copies, keep, mid_dn, ret_dn, me.spread_from(), me.spreads())
    turn_dn[0]()
    load_out.wait()
    load_da.wait()
    load_up.wait()

    def attended_grad(i, carry):
        at = pl.ds(pl.multiple_of(i * 256, 256), 256)
        x = da[pl.ds(2 * i, 2)].reshape(256, D)
        grads = contract(x, w_out[...].reshape(Q_LOC, D), ACROSS).astype(BF)
        both = grads.astype(F32) * o[at, :].astype(F32)
        delta = [
            jnp.sum(both[:, h * 64 : h * 64 + 64], -1, keepdims=True)
            for h in range(HEADS // N_CTX)
        ]
        for ref, values in ((do, grads), (deltas, jnp.concatenate(delta, 1))):
            for half, rows_of in enumerate(split_halves(values)):
                ref[half_rows(half, i), :] = rows_of
        return carry

    lax.fori_loop(0, 4, attended_grad, 0)

    def out_grads():
        for i in (0, 1):
            cols = slice(1024 * i, 1024 * i + 1024)
            term = contract(o[...], da[:, :, cols].reshape(GROUP, 1024), DOWNWARD)
            g_nat[:, :, cols] = term.astype(BF).reshape(16, 16, 1024)

        def place(i, carry):
            g_out[lax.div(i, 4), lax.rem(i, 4)] = g_nat[block_at(i, me.c)]
            return carry

        lax.fori_loop(0, 16, place, 0)

    dk[...] = jnp.zeros_like(dk)
    dv[...] = jnp.zeros_like(dv)

    def heads_of(half, *chips):
        mask_bias(bias, half, chips, meta, places)
        attend_back(half, chips, q, kv, do, log_sums, deltas, bias, dqkv, dk, dv)

    heads_of(1, 0, 1)
    sums_y.merge(2)
    sums_y.merge(1)
    sums_y.merge(3)
    steps(f_up)
    heads_of(0, 0, 1)
    out_grads()
    f_out = scatter(g_out, scr_out, own_out, False)
    steps(f_out)
    turn_dn[1]()
    home_dn[0]()
    sums_y.relay_right()
    sums_y.relay_left()
    sums_y.merge(0)
    heads_of(1, 2, 3)
    steps(f_up)
    steps(f_out)
    heads_of(0, 2, 3)
    load_qkv.wait()
    dqkv[:, Q_LOC : Q_LOC + 64] = dk[...]
    dqkv[:, Q_LOC + 64 :] = dv[...]

    def turn_back(chip, carry):
        for half in (0, 1):
            at = half_rows(half, chip)
            cos_b, sin_b = cos_of[at, :], -sin_of[at, :]
            turned = [turn(dqkv[at, j * 128 : j * 128 + 128], cos_b, sin_b) for j in (0, 1)]
            turned.append(turn(dqkv[at, Q_LOC:], *keys_only(cos_b, sin_b)))
            turned = jnp.concatenate(turned, 1).astype(BF)
            for core in (0, 1):
                rows_of = turned[64 * core : 64 * core + 64]
                dqkv_low[group_rows(chip, core, half), :] = rows_of
        return carry

    lax.fori_loop(0, 4, turn_back, 0)
    load_n1.wait()

    def outer(j, carry):
        at = pl.ds(pl.multiple_of(256 * j, 256), 256)
        term = contract(n1[:, :, at].reshape(GROUP, 256), dqkv_low[...], DOWNWARD)
        where = (lax.div(j, 2), pl.ds(2 * lax.rem(j, 2), 2))
        g_qkv[where] = term.astype(BF).reshape(2, 8, 16, QKV_LOC)
        return carry

    lax.fori_loop(0, 8, outer, 0)
    f_qkv = scatter(g_qkv, scr_qkv, own_qkv, True)
    steps(f_qkv)
    part = part_y
    for s in (2, 1, 3, 0):
        copies.sent(sums_y.arriving[s])
    sums = CtxScatter(me, copies, part, *scr)

    def rows_of(s):
        at = pl.ds(pl.multiple_of(me.at_x(s) * 256, 256), 256)
        term = contract(dqkv_low[at, :], w_qkv[...].reshape(D, QKV_LOC), ACROSS).astype(BF)
        part[pl.ds(me.at_x(s) * 2, 2)] = term.reshape(2, 128, D)
        sums.give(s)

    rows_of(2)
    rows_of(1)
    sums.merge(2)
    rows_of(3)
    sums.merge(1)
    sums.merge(3)
    rows_of(0)
    steps(f_qkv)
    steps(f_up)
    up_back = to_indices(own_up, ret_up)
    steps(f_out)
    sums_y.finish()

    def finish_y(i, carry):
        at = pl.ds(pl.multiple_of(i * 16, 16), 16)
        block_out[at, :] = (h1[at, :] + scattered(at, scr_y[0], scr_y[3], scr_y[4])).astype(BF)
        return carry

    lax.fori_loop(0, 8, finish_y, 0)
    steps(f_qkv)
    sums.relay_right()
    sums.relay_left()
    sums.merge(0)
    steps(f_out)
    turn_out = hop(copies, keep, own_out, mid_out, me.turn_to(), me.turns())
    home_out = hop(copies, keep, mid_out, ret_out, me.spread_from(), me.spreads())
    turn_out[0]()
    steps(f_qkv)
    qkv_back = to_indices(own_qkv, ret_qkv)
    turn_out[1]()
    home_out[0]()
    sums.finish()

    def finish(i, carry):
        at = pl.ds(pl.multiple_of(i * 16, 16), 16)
        x = tokens[at, :].astype(F32)
        scale = lax.rsqrt(jnp.mean(x * x, -1, keepdims=True) + EPSILON)
        u = scattered(at, scr[0], scr[3], scr[4])
        grad[at, :] = (
            dh1[at, :]
            + scale * u
            - x * (scale * scale * scale * jnp.mean(u * x, -1, keepdims=True))
        )
        return carry

    lax.fori_loop(0, 8, finish, 0)
    gate_back()
    up_back()
    home_dn[1]()
    home_out[1]()
    qkv_back()
    copies.finish()


def finish_kernel(
    ret_gate, ret_up, ret_qkv, ret_out, ret_dn, block_in, grad_in, gain_attn, gain_mlp,
    w_query, w_key, w_value, w_gate, w_up,
    block_out, grad, d_gain_attn, d_query, d_key, d_value, d_out, d_gain_mlp, d_gate, d_up, d_down,
):
    block_out[...] = block_in[...]
    grad[...] = grad_in[...]
    d_out[...] = ret_out[...].astype(F32)
    for i in range(3):
        n = min(16, FF_PART - 16 * i)
        d_down[16 * i : 16 * i + n, :] = ret_dn[i].astype(F32)[:n]

    def as_row(values):
        i = lax.broadcasted_iota(jnp.int32, (16, 16), 0)
        j = lax.broadcasted_iota(jnp.int32, (16, 16), 1)
        return jnp.sum(jnp.where(i == j, values, 0.0), 0, keepdims=True)

    def give(out, weights, lanes, raw, gain):
        out[:, lanes] = raw * gain
        return jnp.sum(weights[:, lanes].astype(F32) * raw, 1, keepdims=True)

    gain, total = column(gain_attn), jnp.zeros((16, 1), F32)
    for i in range(8):
        lanes = slice(Q_LOC * i, Q_LOC * i + Q_LOC)
        total += give(d_query, w_query, lanes, ret_qkv[i, :, :Q_LOC].astype(F32), gain)
    for i in range(4):
        both = ret_qkv[2 * i, :, Q_LOC:].astype(F32) + ret_qkv[2 * i + 1, :, Q_LOC:].astype(F32)
        lanes = slice(64 * i, 64 * i + 64)
        total += give(d_key, w_key, lanes, both[:, :64], gain)
        total += give(d_value, w_value, lanes, both[:, 64:], gain)
    d_gain_attn[...] = as_row(total)
    gain, total = column(gain_mlp), jnp.zeros((16, 1), F32)
    for out, weights, back in ((d_gate, w_gate, ret_gate), (d_up, w_up, ret_up)):
        raw = contract(back[...].reshape(128, FF_LOC), spread(), ACROSS)
        for i in range(8):
            lanes = slice(FF_CUT * i, FF_CUT * i + FF_CUT)
            total += give(out, weights, lanes, raw[16 * i : 16 * i + 16], gain)
    d_gain_mlp[...] = as_row(total)


def call(kernel, number, ins, in_specs, outs, out_specs, scratch, n_copies, n_local):
    return pl.pallas_call(
        kernel,
        out_shape=[jax.ShapeDtypeStruct(*o) for o in outs],
        in_specs=in_specs,
        out_specs=out_specs,
        scratch_shapes=[
            *scratch,
            pltpu.SemaphoreType.DMA((n_copies,)),
            pltpu.SemaphoreType.DMA((n_copies,)),
            pltpu.SemaphoreType.DMA((n_local,)),
        ],
        compiler_params=pltpu.CompilerParams(
            collective_id=number, has_side_effects=True, vmem_limit_bytes=62 << 20
        ),
        name=kernel.__name__,
    )(*ins)


def per_device(
    tokens, cotangent, lengths, spans, gain_attn, w_query, w_key, w_value, w_out, gain_mlp,
    w_gate, w_up, w_down,
):
    pair = (2 * (np.arange(128) % 32)).astype(np.float32)
    inverse = np.power(np.float32(10000.0), -pair / np.float32(HEAD_DIM)).astype(np.float32)[None]
    gain_a, gain_m = gain_attn[None], gain_mlp[None]

    n1, wf_qkv, wf_out, da, part_y, g_up, *owned, h1, dh1, q, kv, o, log_sums, cos_of, sin_of, meta, places = call(
        front_kernel, 1,
        (lengths, spans.reshape(1, 16), jnp.asarray(inverse), gain_a, gain_m, w_query, w_key,
         w_value, w_out, w_gate, w_up, w_down, tokens, cotangent),
        [SM] * 2 + [VM] * 12,
        [((8, 128, D), BF), ((4, 4, 8, 16, QKV_LOC), BF), ((16, 16, D), BF), ((8, 128, D), BF),
         ((8, 128, D), BF), ((4, 4, 8, 16, FF_LOC), BF), ((8, 16, FF_LOC), BF), ((3, 16, D), BF),
         ((128, D), F32), ((128, D), F32), ((GROUP, Q_LOC), BF), ((GROUP, 128), BF),
         ((GROUP, Q_LOC), BF), ((GROUP, 4), F32), ((GROUP, 128), F32), ((GROUP, 128), F32),
         ((GROUP, 8), F32), ((1, GROUP), F32)],
        [ANY] * 8 + [VM] * 10,
        [pltpu.VMEM((128, D), BF), pltpu.VMEM((8, 16, QKV_LOC), BF), pltpu.VMEM((4, 16, D), BF),
         pltpu.VMEM((8, 16, 2 * FF_LOC), BF), pltpu.VMEM((128, FF_CUT), BF),
         pltpu.VMEM((8, 128, D), BF), pltpu.VMEM((4, 4, 8, 16, QKV_LOC), BF),
         pltpu.VMEM((4, 16, D), BF), pltpu.VMEM((16, 16, D), BF), pltpu.VMEM((256, GROUP), F32),
         pltpu.VMEM((8, 128, D), BF),
         pltpu.VMEM((8, 128, D), BF), pltpu.VMEM((8, 128, D), BF),
         pltpu.VMEM((4, 4, 8, 16, 2 * FF_LOC), BF), pltpu.VMEM((4, 4, 3, 16, D), BF),
         pltpu.VMEM((4, 4, 3, 16, D), BF), pltpu.VMEM((GROUP, FF_LOC), BF),
         pltpu.VMEM((GROUP, 2 * FF_LOC), BF), pltpu.VMEM((8, 16, FF_LOC), BF),
         pltpu.VMEM((3, 16, D), BF), *SCATTER_SCRATCH, *dp_scatter_scratch((3, 16, D), False),
         *dp_scatter_scratch((8, 16, FF_LOC), True)], 192, 32,
    )

    block_low, grad, ret_gate, ret_up, ret_qkv, ret_out, ret_dn = call(
        end_kernel, 3,
        (da, part_y, g_up, n1, wf_qkv, wf_out, *owned, q, kv, o, log_sums, cos_of, sin_of, meta,
         places, h1, dh1, tokens),
        [ANY] * 8 + [VM] * 11,
        [((128, D), BF), ((128, D), F32), ((8, 16, FF_LOC), BF), ((8, 16, FF_LOC), BF),
         ((8, 16, QKV_LOC), BF), ((16, D), BF), ((3, 16, D), BF)],
        [VM, VM] + [ANY] * 5,
        [pltpu.VMEM((8, 128, D), BF), pltpu.VMEM((8, 128, D), BF),
         pltpu.VMEM((4, 4, 8, 16, FF_LOC), BF), pltpu.VMEM((8, 128, D), BF),
         pltpu.VMEM((4, 4, 8, 16, QKV_LOC), BF), pltpu.VMEM((16, 16, D), BF),
         pltpu.VMEM((GROUP, Q_LOC), BF), pltpu.VMEM((GROUP, 4), F32),
         pltpu.VMEM((GROUP, QKV_LOC), F32),
         pltpu.VMEM((GROUP, QKV_LOC), BF), pltpu.VMEM((GROUP, 64), F32),
         pltpu.VMEM((GROUP, 64), F32), pltpu.VMEM((256, GROUP), F32),
         pltpu.VMEM((4, 4, 8, 16, QKV_LOC), BF),
         pltpu.VMEM((16, 16, D), BF), pltpu.VMEM((4, 4, 16, D), BF),
         pltpu.VMEM((8, 16, FF_LOC), BF), pltpu.VMEM((8, 16, QKV_LOC), BF),
         pltpu.VMEM((16, D), BF), pltpu.VMEM((16, D), BF), pltpu.VMEM((3, 16, D), BF),
         *SCATTER_SCRATCH, *SCATTER_SCRATCH, *dp_scatter_scratch((8, 16, FF_LOC), True),
         *dp_scatter_scratch((8, 16, QKV_LOC), True), *dp_scatter_scratch((16, D), False)],
        112, 32,
    )

    outs = [
        ((128, D), BF), ((128, D), F32), ((1, 16), F32), ((16, D), F32), ((16, 256), F32),
        ((16, 256), F32), ((16, D), F32), ((1, 16), F32), ((16, FF), F32), ((16, FF), F32),
        ((FF_PART, D), F32),
    ]
    outs = pl.pallas_call(
        finish_kernel,
        out_shape=[jax.ShapeDtypeStruct(*out) for out in outs],
        in_specs=[VM] * 14,
        out_specs=[VM] * 11,
        name="finish_kernel",
    )(ret_gate, ret_up, ret_qkv, ret_out, ret_dn, block_low, grad, gain_a, gain_m, w_query, w_key, w_value,
      w_gate, w_up)
    return tuple(out.reshape(16) if out.shape == (1, 16) else out for out in outs)


def solution(mesh):
    flat = P(("dp", "ctx"), None)
    in_specs = (
        flat, flat, P("dp", None), P("dp", None, None), P(("dp", "ctx")), flat, flat, flat, flat,
        P(("dp", "ctx")), flat, flat, flat,
    )
    out_specs = (
        flat, flat, P(("dp", "ctx")), flat, flat, flat, flat, P(("dp", "ctx")), flat, flat, flat,
    )
    return jax.shard_map(
        per_device, mesh=mesh, in_specs=in_specs, out_specs=out_specs, check_vma=False
    )
```

```python
import jax
import jax.numpy as jnp
import numpy as np
from jax import lax
from jax.experimental import pallas as pl
from jax.experimental.pallas import tpu as pltpu
from jax.sharding import PartitionSpec as P

D = 2048
HEADS = 32
KV_HEADS = 4
HEAD_DIM = 64
FF = 5632
N_CTX = 8
N_DP = 16
ROWS = 128
GROUP = 1024
Q_LOC = 256
QKV_LOC = 384
FF_PART = 44
FF_PAD = 48
FF_LOC = N_DP * FF_PAD
FF_CUT = FF // N_CTX
EPSILON = 1e-05
NEG_LARGE = -1e30
MESH = pl.DeviceIdType.MESH
BF = jnp.bfloat16
F32 = jnp.float32
ANY = pl.BlockSpec(memory_space=pl.ANY)
VM = pl.BlockSpec(memory_space=pltpu.VMEM)
SM = pl.BlockSpec(memory_space=pltpu.SMEM)
ACROSS = (((1,), (1,)), ((), ()))
DOWNWARD = (((0,), (0,)), ((), ()))
PLAIN = (((1,), (0,)), ((), ()))


def contract(left_op, right_op, dims_pair):
    return lax.dot_general(left_op, right_op, dims_pair, preferred_element_type=F32)


class Place:
    def __init__(self):
        self.d = lax.axis_index("dp")
        self.c = lax.axis_index("ctx")
        self.z, self.y = lax.div(self.d, 4), lax.rem(self.d, 4)
        self.x, self.k = lax.div(self.c, 2), lax.rem(self.c, 2)

    def at_x(self, step):
        return lax.rem(self.x + step, 4)

    def on_x(self, step):
        return (self.d, self.at_x(step) * 2 + self.k)

    def sibling(self):
        return (self.d, self.x * 2 + 1 - self.k)

    def on_ctx(self, step):
        return (self.d, lax.rem(self.c + step, 8))

    def on_y(self, step):
        return (self.z * 4 + lax.rem(self.y + step, 4), self.c)

    def on_z(self, step):
        return (lax.rem(self.z + step, 4) * 4 + self.y, self.c)

    def spread_to(self):
        return (lax.rem(self.d + 2 * self.c, 16), self.c)

    def spread_from(self):
        return (lax.rem(self.d + 16 - 2 * self.c, 16), self.c)

    def spreads(self):
        return self.c != 0

    def turn_to(self):
        return (self.d, lax.rem(lax.div(self.d, 2) + 8 - self.c, 8))

    def turns(self):
        return self.turn_to()[1] != self.c


def block_at(position, index):
    return 8 * lax.rem(position, 2) + lax.rem(lax.div(position, 2) + 8 - index, 8)


class Copies:
    def __init__(self, send_sems, recv_sems):
        self.send_sems, self.recv_sems, self.used, self.started = send_sems, recv_sems, 0, []

    def make(self, src, dst, device):
        i = self.used
        self.used += 1
        return pltpu.make_async_remote_copy(
            src_ref=src,
            dst_ref=dst,
            send_sem=self.send_sems.at[i],
            recv_sem=self.recv_sems.at[i],
            device_id=device,
            device_id_type=MESH,
        )

    def send(self, src, dst, device):
        copy = self.make(src, dst, device)
        copy.start()
        self.started.append(copy)
        return copy

    def sent(self, copy):
        copy.wait_send()
        self.started = [other for other in self.started if other is not copy]

    def finish(self):
        for copy in self.started:
            copy.wait_send()


def greet(peers, extra=None, extra_on=None, meanwhile=lambda: None):
    barrier = pltpu.get_barrier_semaphore()
    for peer in peers:
        pl.semaphore_signal(barrier, 1, device_id=peer, device_id_type=MESH)
    count = len(peers)
    if extra is not None:

        @pl.when(extra_on)
        def _():
            pl.semaphore_signal(barrier, 1, device_id=extra, device_id_type=MESH)

        count = jnp.where(extra_on, count + 1, count)
    meanwhile()
    pl.semaphore_wait(barrier, count)


def hop(copies, keep, src, dst, device, far):
    sent, kept = copies.make(src, dst, device), keep(src, dst)

    def start():
        pl.when(far)(sent.start)
        pl.when(jnp.logical_not(far))(kept.start)

    def wait():
        pl.when(far)(sent.wait)
        pl.when(jnp.logical_not(far))(kept.wait)

    return start, wait


def keeper(sems):
    used = []

    def keep(src, dst):
        used.append(src)
        return pltpu.make_async_copy(src, dst, sems.at[len(used) - 1])

    return keep


def yz_peers(me):
    return [me.on_y(s) for s in (1, 2, 3)] + [me.on_z(s) for s in (1, 2, 3)]


def ctx_peers(me):
    return [me.on_ctx(s) for s in range(1, 8)]


def x_peers(me):
    return [me.on_x(1), me.on_x(3), me.sibling()]


def round_robin(*flows):
    flows = list(flows)
    while flows:
        flows = [f for f in flows if next(f, "end") != "end"]


class CtxGather:
    def __init__(self, me, copies, src, full, keep):
        self.me, self.copies, self.src, self.full = me, copies, src, full
        self.own, self.left, self.right, self.far_one = (
            me.at_x(s) * 2 + me.k for s in (0, 3, 1, 2)
        )
        self.to_right, self.to_left, self.to_sib = me.on_x(1), me.on_x(3), me.sibling()
        self.mine = keep(src, full.at[self.own])

    def pass_on(self, block, rows, device):
        at = self.full.at[block, rows]
        return self.copies.send(at, at, device)

    def start(self):
        top, low = pl.ds(0, 64), pl.ds(64, 64)
        src, home, send = self.src, self.full.at[self.own], self.copies.send
        self.r1 = send(src.at[top], home.at[top], self.to_right)
        self.l1 = send(src.at[low], home.at[low], self.to_left)
        self.s0 = send(src, home, self.to_sib)
        self.mine.start()

    def start_rest(self):
        top, low = pl.ds(0, 64), pl.ds(64, 64)
        src, home, send = self.src, self.full.at[self.own], self.copies.send
        self.r2 = send(src.at[low], home.at[low], self.to_right)
        self.l2 = send(src.at[top], home.at[top], self.to_left)

    def relay(self):
        self.r1.wait_recv()
        self.r3 = self.pass_on(self.left, pl.ds(0, 64), self.to_right)
        self.l1.wait_recv()
        self.l3 = self.pass_on(self.right, pl.ds(64, 64), self.to_left)

    def sides(self):
        self.r2.wait_recv()
        self.s1 = self.pass_on(self.left, pl.ds(0, 128), self.to_sib)
        self.l2.wait_recv()
        self.s2 = self.pass_on(self.right, pl.ds(0, 128), self.to_sib)

    def far(self):
        self.r3.wait_recv()
        self.s3 = self.pass_on(self.far_one, pl.ds(0, 64), self.to_sib)
        self.l3.wait_recv()
        self.s4 = self.pass_on(self.far_one, pl.ds(64, 64), self.to_sib)

    def wait_own(self):
        self.s0.wait_recv()
        self.mine.wait()

    def wait_sides(self):
        self.s1.wait_recv()
        self.s2.wait_recv()

    def wait_far(self):
        self.s3.wait_recv()
        self.s4.wait_recv()

    def settle(self):
        for copy in (self.r3, self.l3, self.s1, self.s2, self.s3, self.s4):
            self.copies.sent(copy)


def gather_steps(job):
    job.start()
    job.start_rest()
    yield
    job.relay()
    yield
    job.sides()
    yield
    job.far()
    yield
    job.wait_own()
    job.wait_sides()
    job.wait_far()


def ctx_gather(*args):
    return gather_steps(CtxGather(*args))


def add_rows(dst, rows, *terms):
    def step(i, carry):
        at = pl.ds(pl.multiple_of(i * 16, 16), 16)
        total = terms[0](at).astype(F32)
        for term in terms[1:]:
            total += term(at).astype(F32)
        dst[at, :] = total.astype(dst.dtype)
        return carry

    lax.fori_loop(0, rows // 16, step, 0)


class CtxScatter:
    def __init__(self, me, copies, part, scratch, direct=False):
        self.me, self.copies, self.part, self.direct = me, copies, part, direct
        self.pair, self.half_left, self.half_right, self.from_left, self.from_right = scratch
        self.to_right, self.to_left, self.to_sib = me.on_x(1), me.on_x(3), me.sibling()
        self.arriving, self.sends = {}, []

    def send(self, src, dst, device):
        copy = self.copies.send(src, dst, device)
        self.sends.append(copy)
        return copy

    def give(self, s):
        block = self.me.at_x(s) * 2 + 1 - self.me.k
        self.arriving[s] = self.send(self.part.at[block], self.pair.at[s], self.to_sib)

    def merge(self, s):
        top, low, whole = pl.ds(0, 64), pl.ds(64, 64), pl.ds(0, 128)
        self.arriving[s].wait_recv()
        block, pair, part = self.me.at_x(s) * 2 + self.me.k, self.pair, self.part
        add_rows(pair.at[s], 128, lambda at: part[block, at, :], lambda at: pair[s, at, :])
        if s == 2:
            one, other = (self.me.on_x(2),) * 2 if self.direct else (self.to_right, self.to_left)
            self.a = self.send(pair.at[2, top], self.half_left, one)
            self.b = self.send(pair.at[2, low], self.half_right, other)
        if s == 1:
            rows = whole if self.direct else low
            self.r1 = self.send(pair.at[1, rows], self.from_left.at[rows], self.to_right)
        if s == 3:
            rows = whole if self.direct else top
            self.l1 = self.send(pair.at[3, rows], self.from_right.at[rows], self.to_left)

    def relay_right(self):
        half, pair = self.half_left, self.pair
        self.a.wait_recv()
        add_rows(half, 64, lambda at: half[at, :], lambda at: pair[1, at, :])
        self.r2 = self.send(half, self.from_left.at[pl.ds(0, 64)], self.to_right)

    def relay_left(self):
        half, pair = self.half_right, self.pair
        self.b.wait_recv()
        add_rows(half, 64, lambda at: half[at, :], lambda at: pair.at[3, pl.ds(64, 64)][at, :])
        self.l2 = self.send(half, self.from_right.at[pl.ds(64, 64)], self.to_left)

    def finish(self):
        last = (self.a, self.b) if self.direct else (self.r2, self.l2)
        for copy in (self.r1, self.l1, *last):
            copy.wait_recv()

    def settle(self):
        for copy in self.sends:
            self.copies.sent(copy)

    def rows(self, half, i):
        at = pl.ds(pl.multiple_of(64 * half + i * 16, 16), 16)
        refs = [self.pair.at[0], self.from_left, self.from_right]
        total = sum(ref[at, :].astype(F32) for ref in refs)
        if self.direct:
            away = (self.half_right if half else self.half_left)
            total += away[pl.ds(pl.multiple_of(i * 16, 16), 16), :].astype(F32)
        return at, total

    def each_rows(self, use):
        for half in (0, 1):

            def step(i, carry, half=half):
                use(*self.rows(half, i))
                return carry

            lax.fori_loop(0, 4, step, 0)


SCATTER_SCRATCH = [
    pltpu.VMEM((4, 128, D), BF),
    pltpu.VMEM((64, D), BF),
    pltpu.VMEM((64, D), BF),
    pltpu.VMEM((128, D), BF),
    pltpu.VMEM((128, D), BF),
]


def halves(ref, half, by_rows):
    shape = ref.shape
    if by_rows:
        n = shape[-3]
        return ref.at[(*(slice(None),) * (len(shape) - 3), pl.ds(half * (n // 2), n // 2))]
    columns = shape[-1]
    return ref.at[
        (*(slice(None),) * (len(shape) - 1), pl.ds(half * (columns // 2), columns // 2))
    ]


def dp_axes(me, half):
    z = (me.z, me.on_z)
    y = (me.y, me.on_y)
    return (y, z) if half else (z, y)


def dp_gather(me, copies, full, half, by_rows):
    view = halves(full, half, by_rows)
    (p2, dev2), (p1, dev1) = dp_axes(me, half)

    def group(i2, j1):
        return view.at[j1, i2] if half else view.at[i2, j1]

    own = group(p2, p1)
    first = [copies.send(own, own, dev1(s)) for s in (1, 3, 2)]
    yield
    for copy in first:
        copy.wait_recv()
    every, lo, hi = pl.ds(0, 4), pl.ds(0, 2), pl.ds(2, 2)
    mine = group(p2, every)
    up = copies.send(mine, mine, dev2(1))
    down = copies.send(mine, mine, dev2(3))
    yield
    up.wait_recv()
    passed = group(lax.rem(p2 + 3, 4), lo)
    up2 = copies.send(passed, passed, dev2(1))
    down.wait_recv()
    passed = group(lax.rem(p2 + 1, 4), hi)
    down2 = copies.send(passed, passed, dev2(3))
    yield
    up2.wait_recv()
    down2.wait_recv()
    yield
    for copy in (*first, up, down, up2, down2):
        copies.sent(copy)


def add_blocks(dst, *terms):
    lead = dst.shape[:-2]
    if not lead:
        total = terms[0][...].astype(F32)
        for term in terms[1:]:
            total += term[...].astype(F32)
        dst[...] = total.astype(dst.dtype)
        return

    def step(i, carry):
        at = (lax.div(i, lead[1]), lax.rem(i, lead[1])) if len(lead) == 2 else (i,)
        total = terms[0][at].astype(F32)
        for term in terms[1:]:
            total += term[at].astype(F32)
        dst[at] = total.astype(dst.dtype)
        return carry

    lax.fori_loop(0, lead[0] * (lead[1] if len(lead) == 2 else 1), step, 0)


def dp_scatter(
    me, copies, part, half, by_rows, out, pass_up, pass_down, from_up, from_down, last, sent_from=None
):
    view = halves(part, half, by_rows)
    sent_view = view if sent_from is None else halves(sent_from, half, by_rows)
    (p1, dev1), (p2, dev2) = dp_axes(me, half)

    def group(i1, j2, of=view):
        return of.at[j2, i1] if half else of.at[i1, j2]

    every, lo, hi = pl.ds(0, 4), pl.ds(0, 2), pl.ds(2, 2)
    nxt, far, prv = (lax.rem(p1 + s, 4) for s in (1, 2, 3))
    a = copies.send(group(far, lo, sent_view), pass_up, dev1(1))
    b = copies.send(group(far, hi, sent_view), pass_down, dev1(3))
    e1 = copies.send(group(nxt, hi, sent_view), from_up.at[hi], dev1(1))
    e2 = copies.send(group(prv, lo, sent_view), from_down.at[lo], dev1(3))
    yield
    a.wait_recv()
    add_blocks(pass_up, pass_up, group(nxt, lo))
    f1 = copies.send(pass_up, from_up.at[lo], dev1(1))
    b.wait_recv()
    add_blocks(pass_down, pass_down, group(prv, hi))
    f2 = copies.send(pass_down, from_down.at[hi], dev1(3))
    yield
    for copy in (e1, e2, f1, f2):
        copy.wait_recv()
    add_blocks(from_up, from_up, from_down, group(p1, every))
    sent = [
        copies.send(from_up.at[lax.rem(p2 + s, 4)], last.at[s - 1], dev2(s)) for s in (1, 2, 3)
    ]
    yield
    for copy in sent:
        copy.wait_recv()
    add_blocks(halves(out, half, by_rows), from_up.at[p2], last.at[0], last.at[1], last.at[2])


def dp_scatter_scratch(block, by_rows):
    block = (block[0] // 2, *block[1:]) if by_rows else (*block[:-1], block[-1] // 2)
    return [pltpu.VMEM((lead, *block), BF) for lead in (2, 2, 4, 4, 3)] * 2


def turn(values, cos_of, sin_of):
    lane = lax.broadcasted_iota(jnp.int32, values.shape, 1)
    other = jnp.where(
        lax.rem(lane, 64) < 32, pltpu.roll(values, 96, 1), pltpu.roll(values, 32, 1)
    )
    return values * cos_of + other * sin_of


def keys_only(cos_of, sin_of):
    lane = lax.broadcasted_iota(jnp.int32, cos_of.shape, 1)
    return jnp.where(lane < 64, cos_of, 1.0), jnp.where(lane < 64, sin_of, 0.0)


def split_halves(values):
    return (
        jnp.concatenate([values[0:64], values[128:192]], 0),
        jnp.concatenate([values[64:128], values[192:256]], 0),
    )


def half_rows(half, chip):
    return pl.ds(pl.multiple_of(half * 512 + chip * 128, 128), 128)


def of_both(ref, half, chips, lanes=slice(None)):
    pieces = [ref[half_rows(half, chip), lanes] for chip in chips]
    return jnp.concatenate(pieces, 0) if len(pieces) > 1 else pieces[0]


def to_both(ref, half, chips, lanes, values):
    for i, chip in enumerate(chips):
        ref[half_rows(half, chip), lanes] = values[128 * i : 128 * i + 128]


def group_rows(chip, core, half):
    return pl.ds(pl.multiple_of(chip * 256 + core * 128 + half * 64, 64), 64)


def lay_out(lengths, spans, inverse, meta, places, cos_of, sin_of):
    j = lax.broadcasted_iota(jnp.int32, (1, GROUP), 1)
    slot, packed = lax.div(j, 64), lax.rem(j, 64)
    for r in range(8):
        for half in range(2):
            packed = packed + jnp.where(slot == half * 8 + r, spans[0, 2 * r + half] * 64, 0)
    first, end = jnp.zeros_like(packed), 0
    for i in range(4):
        end = end + lengths[0, i]
        first = first + jnp.where(packed >= end, lengths[0, i], 0)
    places[...] = packed.astype(F32)
    row = lax.broadcasted_iota(jnp.int32, (8, GROUP), 0)
    meta[...] = jnp.transpose(
        jnp.where(row == 0, packed, jnp.where(row == 1, first, packed - first)).astype(F32)
    )

    def table(i, carry):
        at = pl.ds(pl.multiple_of(i * 128, 128), 128)
        angles = meta[at, 2:3] * inverse[...]
        lane = lax.broadcasted_iota(jnp.int32, angles.shape, 1)
        sines = jnp.sin(angles)
        cos_of[at, :] = jnp.cos(angles)
        sin_of[at, :] = jnp.where(lax.rem(lane, 64) < 32, -sines, sines)
        return carry

    lax.fori_loop(0, 8, table, 0)


def mask_bias(bias, half, chips, meta, places):
    keys = 512 * (half + 1)
    seen = places[:, :keys]
    here = of_both(meta, half, chips)
    allowed = (seen <= here[:, 0:1]) & (seen >= here[:, 1:2])
    bias[: 128 * len(chips), :keys] = jnp.where(allowed, 0.0, NEG_LARGE).astype(F32)


def attend(half, chips, q, kv, bias, o, log_sums):
    keys = 512 * (half + 1)
    k, v = kv[:keys, :64], kv[:keys, 64:]
    for h in range(HEADS // N_CTX):
        lanes = slice(h * 64, h * 64 + 64)
        scores = contract(of_both(q, half, chips, lanes), k, ACROSS) + bias[: 128 * len(chips), :keys]
        peak = jnp.max(scores, -1, keepdims=True)
        expo = jnp.exp(scores - peak)
        total = jnp.sum(expo, -1, keepdims=True)
        out = (contract(expo.astype(BF), v, PLAIN) / total).astype(BF)
        for i in range(2 * len(chips)):
            o[group_rows(chips[i // 2], i % 2, half), lanes] = out[64 * i : 64 * i + 64]
        to_both(log_sums, half, chips, slice(h, h + 1), peak + jnp.log(total))


def column(row):
    i = lax.broadcasted_iota(jnp.int32, (16, 16), 0)
    j = lax.broadcasted_iota(jnp.int32, (16, 16), 1)
    return jnp.sum(jnp.where(i == j, row[...].astype(F32), 0.0), 1, keepdims=True)


def spread():
    j = lax.broadcasted_iota(jnp.int32, (FF_CUT, FF_LOC), 0)
    to = lax.broadcasted_iota(jnp.int32, (FF_CUT, FF_LOC), 1)
    return jnp.where(FF_PAD * lax.div(j, FF_PART) + lax.rem(j, FF_PART) == to, 1.0, 0.0).astype(BF)


def front_kernel(
    lengths, spans, inverse, gain_attn, gain_mlp, w_query, w_key, w_value, w_out_own, w_gate, w_up,
    w_down, tokens, cot_own,
    n1_out, w_qkv_out, w_out_out, da_full, part_y, g_up, own_gate_out, own_dn_out,
    h1_out, dh1_out, q_out, kv_out, o_out, log_sums_out, cos_out, sin_out, meta_out, places_out,
    h1, dh1, q, kv, o, log_sums, cos_of, sin_of, meta, places,
    n1_own, qkv_src, od_src, gu_src, stack, n1, w_qkv, od_mid, w_out, bias, part,
    n2, cot_full, w_gu, w_dn, w_dn_here, hm, dgu, own_gate, own_dn, *rest,
):
    ss, rs, ls = rest[-3:]
    scr, scr_dn, scr_gate = rest[0:5], rest[5:15], rest[15:25]
    me = Place()
    w_od = w_dn_here.at[:, :, 0]

    def prepare():
        def norm(i, carry):
            at = pl.ds(pl.multiple_of(i * 16, 16), 16)
            x = tokens[at, :].astype(F32)
            scale = lax.rsqrt(jnp.mean(x * x, -1, keepdims=True) + EPSILON)
            n1_own[at, :] = (x * scale).astype(BF)
            return carry

        lax.fori_loop(0, 8, norm, 0)
        gain = column(gain_attn)
        for i in range(8):
            pair = slice(64 * (i // 2), 64 * (i // 2) + 64)
            scaled = w_query[:, Q_LOC * i : Q_LOC * i + Q_LOC].astype(F32) * gain
            qkv_src[i, :, :Q_LOC] = scaled.astype(BF)
            both = jnp.concatenate([w_key[:, pair], w_value[:, pair]], 1).astype(F32) * gain
            qkv_src[i, :, Q_LOC:] = both.astype(BF)
        od_src[0] = w_out_own[...]
        od_src[1] = w_down[0:16, :]
        od_src[2] = w_down[16:32, :]
        tail = jnp.concatenate([w_down[32:FF_PART, :].astype(F32), jnp.zeros((4, D), F32)], 0)
        od_src[3] = tail.astype(BF)
        gain = column(gain_mlp)
        for j, w in enumerate((w_gate, w_up)):
            for i in range(8):
                scaled = w[:, FF_CUT * i : FF_CUT * i + FF_CUT].astype(F32) * gain
                stack[16 * i : 16 * i + 16, :] = scaled.astype(BF)
            placed = contract(stack[...], spread(), PLAIN).astype(BF)
            gu_src[:, :, FF_LOC * j : FF_LOC * j + FF_LOC] = placed.reshape(8, 16, FF_LOC)

    greet(ctx_peers(me) + yz_peers(me), me.spread_from(), me.spreads(), prepare)
    copies = Copies(ss, rs)
    keep = keeper(ls)

    def to_indices(src, home):
        sent = [
            copies.send(src.at[lax.rem(me.c + s, 8)], home.at[me.c], me.on_ctx(s))
            for s in range(1, 8)
        ]
        mine = keep(src.at[me.c], home.at[me.c])
        mine.start()

        def wait():
            for copy in sent:
                copy.wait_recv()
            mine.wait()

        return wait

    qkv_there = to_indices(qkv_src, w_qkv.at[me.z, me.y])
    spread_start, spread_there = hop(
        copies, keep, od_src, od_mid, me.spread_to(), me.spreads()
    )
    turns = [
        hop(copies, keep, od_mid.at[0], w_od.at[me.z, me.y], me.turn_to(), me.turns()),
        hop(copies, keep, od_mid.at[pl.ds(1, 3)], w_dn.at[me.z, me.y], me.turn_to(), me.turns()),
    ]
    spread_start()
    gu_there = to_indices(gu_src, w_gu.at[me.z, me.y])
    rows = CtxGather(me, copies, n1_own, n1, keep)
    rows.start()

    def steps(flows):
        for flow in flows:
            next(flow, None)

    f_qkv = [dp_gather(me, copies, w_qkv, h, True) for h in (0, 1)]
    f_out = [dp_gather(me, copies, w_od, h, False) for h in (0, 1)]
    f_gu = [dp_gather(me, copies, w_gu, h, True) for h in (0, 1)]
    f_dn = [dp_gather(me, copies, w_dn, h, False) for h in (0, 1)]
    seeds = ctx_gather(me, copies, cot_own, cot_full, keep)
    qkv_there()
    steps(f_qkv)
    spread_there()
    for start, _ in turns:
        start()
    rows.start_rest()
    first_row_copies = (rows.r1, rows.l1, rows.s0, rows.r2, rows.l2)
    steps(f_qkv)
    gu_there()
    steps(f_qkv)
    rows.relay()
    turns[0][1]()
    steps(f_out)
    steps(f_gu)
    lay_out(lengths, spans, inverse, meta, places, cos_of, sin_of)
    turns[1][1]()
    steps(f_out)
    steps(f_dn)
    rows.sides()
    steps(f_qkv)
    rows.far()
    next(seeds)
    steps(f_out)
    steps(f_gu)
    rows.wait_own()
    rows.wait_sides()
    rows.wait_far()
    keeps = [keep(n1, n1_out), keep(w_qkv, w_qkv_out)]
    for copy in keeps:
        copy.start()
    kept = []

    def leave(*pairs):
        for src, dst in pairs:
            kept.append(keep(src, dst))
            kept[-1].start()


    def project(chip, carry):
        x = n1[pl.ds(2 * chip, 2)].reshape(256, D)
        qkv = contract(x, w_qkv[...].reshape(D, QKV_LOC), PLAIN)
        for half, rows_of in enumerate(split_halves(qkv)):
            at = half_rows(half, chip)
            cos_b, sin_b = cos_of[at, :], sin_of[at, :]
            for j in (0, 1):
                turned = turn(rows_of[:, j * 128 : j * 128 + 128], cos_b, sin_b)
                q[at, j * 128 : j * 128 + 128] = (turned * HEAD_DIM ** (-0.5)).astype(BF)
            kv[at, :] = turn(rows_of[:, Q_LOC:], *keys_only(cos_b, sin_b)).astype(BF)
        return carry

    lax.fori_loop(0, 4, project, 0)
    leave((q, q_out), (kv, kv_out), (cos_of, cos_out), (sin_of, sin_out))
    leave((meta, meta_out), (places, places_out))
    steps(f_out)
    steps(f_dn)

    def place(i, carry):
        w_out[block_at(i, me.c)] = w_od[lax.div(i, 4), lax.rem(i, 4)]
        return carry

    lax.fori_loop(0, 16, place, 0)
    keeps.append(keep(w_out, w_out_out))
    keeps[-1].start()
    sums = CtxScatter(me, copies, part, scr)

    def heads_of(half, *steps_away):
        chips = [me.at_x(s) for s in steps_away]
        mask_bias(bias, half, chips, meta, places)
        attend(half, chips, q, kv, bias, o, log_sums)

    def out_of(s):
        at = pl.ds(pl.multiple_of(me.at_x(s) * 256, 256), 256)
        term = contract(o[at, :], w_out[...].reshape(Q_LOC, D), PLAIN).astype(BF)
        part[pl.ds(me.at_x(s) * 2, 2)] = term.reshape(2, 128, D)
        sums.give(s)

    heads_of(0, 2, 1)
    heads_of(1, 2, 1)
    next(seeds)
    out_of(2)
    out_of(1)
    heads_of(0, 3)
    sums.merge(2)
    sums.merge(1)
    next(seeds)
    heads_of(1, 3)
    out_of(3)
    steps(f_gu)
    heads_of(0, 0)
    sums.merge(3)
    sums.relay_right()
    sums.relay_left()
    next(seeds)
    heads_of(1, 0)
    out_of(0)
    sums.merge(0)
    steps(f_dn)
    sums.finish()
    sums.settle()
    leave((o, o_out), (log_sums, log_sums_out))
    own_norm = n1_own

    def norm(at, branch):
        hidden = tokens[at, :].astype(F32) + branch
        scale = lax.rsqrt(jnp.mean(hidden * hidden, -1, keepdims=True) + EPSILON)
        h1[at, :] = hidden
        own_norm[at, :] = (hidden * scale).astype(BF)

    for copy in first_row_copies:
        copies.sent(copy)
    sums.each_rows(norm)
    normed = CtxGather(me, copies, own_norm, n2, keep)
    normed.start()
    normed.start_rest()
    leave((h1, h1_out))
    steps(f_gu)
    steps(f_dn)
    next(seeds, None)

    steps(f_out)

    def place_down(i, carry):
        here = block_at(i, me.c)
        w_dn_here[lax.div(here, 4), lax.rem(here, 4)] = w_dn[lax.div(i, 4), lax.rem(i, 4)]
        return carry

    lax.fori_loop(0, 16, place_down, 0)
    sums = CtxScatter(me, copies, part, scr, direct=True)

    def two(s):
        return pl.ds(me.at_x(s) * 2, 2)

    def gate_up(s):
        at = pl.ds(pl.multiple_of(me.at_x(s) * 256, 256), 256)
        x = n2[two(s)].reshape(256, D)
        gate = contract(x, w_gu[..., :FF_LOC].reshape(D, FF_LOC), PLAIN)
        up = contract(x, w_gu[..., FF_LOC:].reshape(D, FF_LOC), PLAIN)
        sig = jax.nn.sigmoid(gate)
        silu = gate * sig
        hm[at, :] = (silu * up).astype(BF)
        inner = contract(
            cot_full[two(s)].reshape(256, D), w_dn_here[...].reshape(FF_LOC, D), ACROSS
        )
        dgu[at, :FF_LOC] = (inner * up * (sig + silu * (1.0 - sig))).astype(BF)
        dgu[at, FF_LOC:] = (inner * silu).astype(BF)
        term = contract(dgu[at, :], w_gu[...].reshape(D, 2 * FF_LOC), ACROSS).astype(BF)
        part[two(s)] = term.reshape(2, 128, D)
        sums.give(s)

    normed.wait_own()
    gate_up(0)
    normed.relay()
    normed.sides()
    normed.wait_sides()
    gate_up(1)
    normed.far()
    gate_up(3)
    sums.merge(1)
    sums.merge(3)
    normed.wait_far()
    gate_up(2)
    for copy in keeps:
        copy.wait()
    rows.settle()
    steps(f_gu)
    steps(f_dn)
    part_out = n1

    def outer(j, carry):
        at = pl.ds(pl.multiple_of(256 * j, 256), 256)
        term = contract(n2[:, :, at].reshape(GROUP, 256), dgu[...], DOWNWARD)
        where = (lax.div(j, 2), pl.ds(2 * lax.rem(j, 2), 2))
        w_gu[where] = term.astype(BF).reshape(2, 8, 16, 2 * FF_LOC)
        return carry

    lax.fori_loop(0, 4, outer, 0)
    sums.merge(2)
    lax.fori_loop(4, 8, outer, 0)
    gate_columns, up_columns = (
        w_gu.at[:, :, :, :, pl.ds(FF_LOC * j, FF_LOC)] for j in (0, 1)
    )
    f_gate = [
        dp_scatter(me, copies, gate_columns, h, True, own_gate, *scr_gate[h * 5 : h * 5 + 5])
        for h in (0, 1)
    ]
    steps(f_gate)
    leave((up_columns, g_up))

    def down(i, carry):
        at = pl.ds(pl.multiple_of(i * 256, 256), 256)
        y = contract(hm[at, :], w_dn_here[...].reshape(FF_LOC, D), PLAIN).astype(BF)
        part_out[pl.ds(2 * i, 2)] = y.reshape(2, 128, D)
        return carry

    lax.fori_loop(0, 4, down, 0)
    leave((part_out, part_y))
    for j in (0, 1):
        for i in (0, 1):
            cols = slice(1024 * i, 1024 * i + 1024)
            term = contract(
                hm[:, 384 * j : 384 * j + 384], cot_full[:, :, cols].reshape(GROUP, 1024), DOWNWARD
            )
            w_dn_here[2 * j : 2 * j + 2, :, :, :, cols] = term.astype(BF).reshape(2, 4, 3, 16, 1024)

    def place_back(i, carry):
        here = block_at(i, me.c)
        w_dn[lax.div(i, 4), lax.rem(i, 4)] = w_dn_here[lax.div(here, 4), lax.rem(here, 4)]
        return carry

    lax.fori_loop(0, 16, place_back, 0)
    flows = [
        dp_scatter(me, copies, w_dn, h, False, own_dn, *scr_dn[h * 5 : h * 5 + 5]) for h in (0, 1)
    ]
    steps(flows)

    sums.merge(0)
    steps(f_gate)
    sums.finish()
    da = own_norm
    copies.sent(normed.s0)
    for copy in (normed.r1, normed.r2, normed.l1, normed.l2):
        copies.sent(copy)

    def norm_back(at, u):
        hidden = h1[at, :]
        scale = lax.rsqrt(jnp.mean(hidden * hidden, -1, keepdims=True) + EPSILON)
        grad = (
            cot_own[at, :].astype(F32)
            + scale * u
            - hidden * (scale * scale * scale * jnp.mean(u * hidden, -1, keepdims=True))
        )
        dh1[at, :] = grad
        da[at, :] = grad.astype(BF)

    sums.each_rows(norm_back)
    rows_da = ctx_gather(me, copies, da, da_full, keep)
    next(rows_da)
    leave((dh1, dh1_out))
    steps(flows)
    next(rows_da)
    steps(f_gate)
    next(rows_da)
    steps(flows)
    next(rows_da)
    steps(f_gate)
    steps(flows)
    leave((own_gate, own_gate_out), (own_dn, own_dn_out))
    next(rows_da, None)
    for copy in kept:
        copy.wait()
    copies.finish()


def attend_back(half, chips, q, kv, do, log_sums, deltas, bias, dqkv, dk, dv):
    keys = 512 * (half + 1)
    k, v = kv[:keys, :64], kv[:keys, 64:]
    logs, delta = of_both(log_sums, half, chips), of_both(deltas, half, chips)
    for h in range(HEADS // N_CTX):
        lanes = slice(h * 64, h * 64 + 64)
        queries, grads = of_both(q, half, chips, lanes), of_both(do, half, chips, lanes)
        scores = contract(queries, k, ACROSS) + bias[: 128 * len(chips), :keys]
        probs = jnp.exp(scores - logs[:, h : h + 1])
        score_grad = probs * (contract(grads, v, ACROSS) - delta[:, h : h + 1])
        score_grad = score_grad.astype(BF)
        rows = contract(score_grad, k, PLAIN) * HEAD_DIM ** (-0.5)
        to_both(dqkv, half, chips, lanes, rows)
        dk[:keys, :] += contract(score_grad, queries, DOWNWARD)
        dv[:keys, :] += contract(probs.astype(BF), grads, DOWNWARD)


def end_kernel(
    da_in, part_y_in, g_up_in, n1_in, w_qkv_in, w_out_in, own_gate, own_dn,
    q_in, kv_in, o_in, log_sums_in, cos_in, sin_in, meta_in, places_in, h1_in, dh1_in, tokens,
    block_out, grad, ret_gate, ret_up, ret_qkv, ret_out, ret_dn,
    q, kv, o, log_sums, cos_of, sin_of, meta, places, h1, dh1, da, part_y, g_up, n1, w_qkv, w_out, do, deltas, dqkv, dqkv_low, dk, dv, bias,
    g_qkv, g_nat, g_out, own_up, own_qkv, own_out, mid_out, mid_dn, *rest,
):
    ss, rs, ls = rest[-3:]
    scr_y, scr = rest[0:5], rest[5:10]
    scr_up, scr_qkv, scr_out = rest[10:20], rest[20:30], rest[30:40]
    me = Place()
    copies, keep = Copies(ss, rs), keeper(ls)

    def load(src, dst):
        copy = keep(src, dst)
        copy.start()
        return copy

    load_y = load(part_y_in, part_y)
    load_out = load(w_out_in, w_out)
    load_da = load(da_in, da)
    load_rows = [
        load(src, dst)
        for src, dst in ((o_in, o), (q_in, q), (kv_in, kv), (log_sums_in, log_sums), (meta_in, meta), (places_in, places))
    ]
    load_up = load(g_up_in, g_up)
    load_last = [
        load(src, dst)
        for src, dst in ((cos_in, cos_of), (sin_in, sin_of), (h1_in, h1), (dh1_in, dh1))
    ]
    load_qkv = load(w_qkv_in, w_qkv)
    load_n1 = load(n1_in, n1)
    greet(ctx_peers(me) + yz_peers(me), me.spread_to(), me.spreads())
    def steps(flows):
        for flow in flows:
            next(flow, None)


    def scatter(g, scratch, own, by_rows, sent_from=None):
        return [
            dp_scatter(me, copies, g, h, by_rows, own, *scratch[h * 5 : h * 5 + 5], sent_from)
            for h in (0, 1)
        ]

    def to_indices(own, back):
        sent = [
            copies.send(own.at[lax.rem(me.c + s, 8)], back.at[me.c], me.on_ctx(s))
            for s in range(1, 8)
        ]
        mine = keep(own.at[me.c], back.at[me.c])
        mine.start()

        def wait():
            for copy in sent:
                copy.wait_recv()
            mine.wait()

        return wait

    f_up = scatter(g_up, scr_up, own_up, True, g_up_in)
    steps(f_up)
    gate_back = to_indices(own_gate, ret_gate)
    load_y.wait()
    sums_y = CtxScatter(me, copies, part_y, scr_y)
    for s in (2, 1, 3, 0):
        sums_y.give(s)
    turn_dn = hop(copies, keep, own_dn, mid_dn, me.turn_to(), me.turns())
    home_dn = hop(copies, keep, mid_dn, ret_dn, me.spread_from(), me.spreads())
    turn_dn[0]()
    load_out.wait()
    load_da.wait()
    for copy in load_rows:
        copy.wait()

    def attended_grad(i, carry):
        at = pl.ds(pl.multiple_of(i * 256, 256), 256)
        x = da[pl.ds(2 * i, 2)].reshape(256, D)
        grads = contract(x, w_out[...].reshape(Q_LOC, D), ACROSS).astype(BF)
        both = grads.astype(F32) * o[at, :].astype(F32)
        delta = [
            jnp.sum(both[:, h * 64 : h * 64 + 64], -1, keepdims=True)
            for h in range(HEADS // N_CTX)
        ]
        for ref, values in ((do, grads), (deltas, jnp.concatenate(delta, 1))):
            for half, rows_of in enumerate(split_halves(values)):
                ref[half_rows(half, i), :] = rows_of
        return carry

    lax.fori_loop(0, 4, attended_grad, 0)

    def out_grads():
        for i in (0, 1):
            cols = slice(1024 * i, 1024 * i + 1024)
            term = contract(o[...], da[:, :, cols].reshape(GROUP, 1024), DOWNWARD)
            g_nat[:, :, cols] = term.astype(BF).reshape(16, 16, 1024)

        def place(i, carry):
            g_out[lax.div(i, 4), lax.rem(i, 4)] = g_nat[block_at(i, me.c)]
            return carry

        lax.fori_loop(0, 16, place, 0)

    dk[...] = jnp.zeros_like(dk)
    dv[...] = jnp.zeros_like(dv)

    def heads_of(half, *chips):
        mask_bias(bias, half, chips, meta, places)
        attend_back(half, chips, q, kv, do, log_sums, deltas, bias, dqkv, dk, dv)

    heads_of(1, 0, 1)
    sums_y.merge(2)
    sums_y.merge(1)
    sums_y.merge(3)
    load_up.wait()
    steps(f_up)
    heads_of(0, 0, 1)
    out_grads()
    f_out = scatter(g_out, scr_out, own_out, False)
    steps(f_out)
    turn_dn[1]()
    home_dn[0]()
    sums_y.relay_right()
    sums_y.relay_left()
    sums_y.merge(0)
    heads_of(1, 2, 3)
    steps(f_up)
    steps(f_out)
    heads_of(0, 2, 3)
    load_qkv.wait()
    for copy in load_last:
        copy.wait()
    dqkv[:, Q_LOC : Q_LOC + 64] = dk[...]
    dqkv[:, Q_LOC + 64 :] = dv[...]

    def turn_back(chip, carry):
        for half in (0, 1):
            at = half_rows(half, chip)
            cos_b, sin_b = cos_of[at, :], -sin_of[at, :]
            turned = [turn(dqkv[at, j * 128 : j * 128 + 128], cos_b, sin_b) for j in (0, 1)]
            turned.append(turn(dqkv[at, Q_LOC:], *keys_only(cos_b, sin_b)))
            turned = jnp.concatenate(turned, 1).astype(BF)
            for core in (0, 1):
                rows_of = turned[64 * core : 64 * core + 64]
                dqkv_low[group_rows(chip, core, half), :] = rows_of
        return carry

    lax.fori_loop(0, 4, turn_back, 0)
    load_n1.wait()

    def outer(j, carry):
        at = pl.ds(pl.multiple_of(256 * j, 256), 256)
        term = contract(n1[:, :, at].reshape(GROUP, 256), dqkv_low[...], DOWNWARD)
        where = (lax.div(j, 2), pl.ds(2 * lax.rem(j, 2), 2))
        g_qkv[where] = term.astype(BF).reshape(2, 8, 16, QKV_LOC)
        return carry

    lax.fori_loop(0, 8, outer, 0)
    f_qkv = scatter(g_qkv, scr_qkv, own_qkv, True)
    steps(f_qkv)
    part = part_y
    for s in (2, 1, 3, 0):
        copies.sent(sums_y.arriving[s])
    sums = CtxScatter(me, copies, part, scr)

    def rows_of(s):
        at = pl.ds(pl.multiple_of(me.at_x(s) * 256, 256), 256)
        term = contract(dqkv_low[at, :], w_qkv[...].reshape(D, QKV_LOC), ACROSS).astype(BF)
        part[pl.ds(me.at_x(s) * 2, 2)] = term.reshape(2, 128, D)
        sums.give(s)

    rows_of(2)
    rows_of(1)
    sums.merge(2)
    rows_of(3)
    sums.merge(1)
    sums.merge(3)
    rows_of(0)
    steps(f_qkv)
    steps(f_up)
    up_back = to_indices(own_up, ret_up)
    steps(f_out)
    sums_y.finish()

    def finish_y(at, y):
        block_out[at, :] = (h1[at, :] + y).astype(BF)

    sums_y.each_rows(finish_y)
    steps(f_qkv)
    sums.relay_right()
    sums.relay_left()
    sums.merge(0)
    steps(f_out)
    turn_out = hop(copies, keep, own_out, mid_out, me.turn_to(), me.turns())
    home_out = hop(copies, keep, mid_out, ret_out, me.spread_from(), me.spreads())
    turn_out[0]()
    steps(f_qkv)
    qkv_back = to_indices(own_qkv, ret_qkv)
    turn_out[1]()
    home_out[0]()
    sums.finish()

    def finish(at, u):
        x = tokens[at, :].astype(F32)
        scale = lax.rsqrt(jnp.mean(x * x, -1, keepdims=True) + EPSILON)
        grad[at, :] = (
            dh1[at, :]
            + scale * u
            - x * (scale * scale * scale * jnp.mean(u * x, -1, keepdims=True))
        )

    sums.each_rows(finish)
    gate_back()
    up_back()
    home_dn[1]()
    home_out[1]()
    qkv_back()
    copies.finish()


def finish_kernel(
    ret_gate, ret_up, ret_qkv, ret_out, ret_dn, block_in, grad_in, gain_attn, gain_mlp,
    w_query, w_key, w_value, w_gate, w_up,
    block_out, grad, d_gain_attn, d_query, d_key, d_value, d_out, d_gain_mlp, d_gate, d_up, d_down,
):
    block_out[...] = block_in[...]
    grad[...] = grad_in[...]
    d_out[...] = ret_out[...].astype(F32)
    for i in range(3):
        n = min(16, FF_PART - 16 * i)
        d_down[16 * i : 16 * i + n, :] = ret_dn[i].astype(F32)[:n]

    def as_row(values):
        i = lax.broadcasted_iota(jnp.int32, (16, 16), 0)
        j = lax.broadcasted_iota(jnp.int32, (16, 16), 1)
        return jnp.sum(jnp.where(i == j, values, 0.0), 0, keepdims=True)

    def give(out, weights, lanes, raw, gain):
        out[:, lanes] = raw * gain
        return jnp.sum(weights[:, lanes].astype(F32) * raw, 1, keepdims=True)

    gain, total = column(gain_attn), jnp.zeros((16, 1), F32)
    for i in range(8):
        lanes = slice(Q_LOC * i, Q_LOC * i + Q_LOC)
        total += give(d_query, w_query, lanes, ret_qkv[i, :, :Q_LOC].astype(F32), gain)
    for i in range(4):
        both = ret_qkv[2 * i, :, Q_LOC:].astype(F32) + ret_qkv[2 * i + 1, :, Q_LOC:].astype(F32)
        lanes = slice(64 * i, 64 * i + 64)
        total += give(d_key, w_key, lanes, both[:, :64], gain)
        total += give(d_value, w_value, lanes, both[:, 64:], gain)
    d_gain_attn[...] = as_row(total)
    gain, total = column(gain_mlp), jnp.zeros((16, 1), F32)
    for out, weights, back in ((d_gate, w_gate, ret_gate), (d_up, w_up, ret_up)):
        raw = contract(back[...].reshape(128, FF_LOC), spread(), ACROSS)
        for i in range(8):
            lanes = slice(FF_CUT * i, FF_CUT * i + FF_CUT)
            total += give(out, weights, lanes, raw[16 * i : 16 * i + 16], gain)
    d_gain_mlp[...] = as_row(total)


def call(kernel, number, ins, in_specs, outs, out_specs, scratch, n_copies, n_local):
    return pl.pallas_call(
        kernel,
        out_shape=[jax.ShapeDtypeStruct(*o) for o in outs],
        in_specs=in_specs,
        out_specs=out_specs,
        scratch_shapes=[
            *scratch,
            pltpu.SemaphoreType.DMA((n_copies,)),
            pltpu.SemaphoreType.DMA((n_copies,)),
            pltpu.SemaphoreType.DMA((n_local,)),
        ],
        compiler_params=pltpu.CompilerParams(
            collective_id=number, has_side_effects=True, vmem_limit_bytes=62 << 20
        ),
        name=kernel.__name__,
    )(*ins)


def per_device(
    tokens, cotangent, lengths, spans, gain_attn, w_query, w_key, w_value, w_out, gain_mlp,
    w_gate, w_up, w_down,
):
    pair = (2 * (np.arange(128) % 32)).astype(np.float32)
    inverse = np.power(np.float32(10000.0), -pair / np.float32(HEAD_DIM)).astype(np.float32)[None]
    gain_a, gain_m = gain_attn[None], gain_mlp[None]
    rows = [
        ((128, D), F32), ((128, D), F32), ((GROUP, Q_LOC), BF), ((GROUP, 128), BF),
        ((GROUP, Q_LOC), BF), ((GROUP, 4), F32), ((GROUP, 128), F32), ((GROUP, 128), F32),
        ((GROUP, 8), F32), ((1, GROUP), F32),
    ]

    n1, wf_qkv, wf_out, da, part_y, g_up, *owned, h1, dh1, q, kv, o, log_sums, cos_of, sin_of, meta, places = call(
        front_kernel, 1,
        (lengths, spans.reshape(1, 16), jnp.asarray(inverse), gain_a, gain_m, w_query, w_key,
         w_value, w_out, w_gate, w_up, w_down, tokens, cotangent),
        [SM] * 2 + [VM] * 12,
        [((8, 128, D), BF), ((4, 4, 8, 16, QKV_LOC), BF), ((16, 16, D), BF), ((8, 128, D), BF),
         ((8, 128, D), BF), ((4, 4, 8, 16, FF_LOC), BF), ((8, 16, FF_LOC), BF), ((3, 16, D), BF),
         *rows],
        [ANY] * 18,
        [*(pltpu.VMEM(*row) for row in rows), pltpu.VMEM((128, D), BF), pltpu.VMEM((8, 16, QKV_LOC), BF), pltpu.VMEM((4, 16, D), BF),
         pltpu.VMEM((8, 16, 2 * FF_LOC), BF), pltpu.VMEM((128, FF_CUT), BF),
         pltpu.VMEM((8, 128, D), BF), pltpu.VMEM((4, 4, 8, 16, QKV_LOC), BF),
         pltpu.VMEM((4, 16, D), BF), pltpu.VMEM((16, 16, D), BF), pltpu.VMEM((256, GROUP), F32),
         pltpu.VMEM((8, 128, D), BF),
         pltpu.VMEM((8, 128, D), BF), pltpu.VMEM((8, 128, D), BF),
         pltpu.VMEM((4, 4, 8, 16, 2 * FF_LOC), BF), pltpu.VMEM((4, 4, 3, 16, D), BF),
         pltpu.VMEM((4, 4, 3, 16, D), BF), pltpu.VMEM((GROUP, FF_LOC), BF),
         pltpu.VMEM((GROUP, 2 * FF_LOC), BF), pltpu.VMEM((8, 16, FF_LOC), BF),
         pltpu.VMEM((3, 16, D), BF), *SCATTER_SCRATCH, *dp_scatter_scratch((3, 16, D), False),
         *dp_scatter_scratch((8, 16, FF_LOC), True)], 192, 32,
    )

    block_low, grad, ret_gate, ret_up, ret_qkv, ret_out, ret_dn = call(
        end_kernel, 3,
        (da, part_y, g_up, n1, wf_qkv, wf_out, *owned, q, kv, o, log_sums, cos_of, sin_of, meta,
         places, h1, dh1, tokens),
        [ANY] * 18 + [VM],
        [((128, D), BF), ((128, D), F32), ((8, 16, FF_LOC), BF), ((8, 16, FF_LOC), BF),
         ((8, 16, QKV_LOC), BF), ((16, D), BF), ((3, 16, D), BF)],
        [VM, VM] + [ANY] * 5,
        [*(pltpu.VMEM(*row) for row in rows[2:] + rows[:2]), pltpu.VMEM((8, 128, D), BF), pltpu.VMEM((8, 128, D), BF),
         pltpu.VMEM((4, 4, 8, 16, FF_LOC), BF), pltpu.VMEM((8, 128, D), BF),
         pltpu.VMEM((4, 4, 8, 16, QKV_LOC), BF), pltpu.VMEM((16, 16, D), BF),
         pltpu.VMEM((GROUP, Q_LOC), BF), pltpu.VMEM((GROUP, 4), F32),
         pltpu.VMEM((GROUP, QKV_LOC), F32),
         pltpu.VMEM((GROUP, QKV_LOC), BF), pltpu.VMEM((GROUP, 64), F32),
         pltpu.VMEM((GROUP, 64), F32), pltpu.VMEM((256, GROUP), F32),
         pltpu.VMEM((4, 4, 8, 16, QKV_LOC), BF),
         pltpu.VMEM((16, 16, D), BF), pltpu.VMEM((4, 4, 16, D), BF),
         pltpu.VMEM((8, 16, FF_LOC), BF), pltpu.VMEM((8, 16, QKV_LOC), BF),
         pltpu.VMEM((16, D), BF), pltpu.VMEM((16, D), BF), pltpu.VMEM((3, 16, D), BF),
         *SCATTER_SCRATCH, *SCATTER_SCRATCH, *dp_scatter_scratch((8, 16, FF_LOC), True),
         *dp_scatter_scratch((8, 16, QKV_LOC), True), *dp_scatter_scratch((16, D), False)],
        112, 40,
    )

    outs = [
        ((128, D), BF), ((128, D), F32), ((1, 16), F32), ((16, D), F32), ((16, 256), F32),
        ((16, 256), F32), ((16, D), F32), ((1, 16), F32), ((16, FF), F32), ((16, FF), F32),
        ((FF_PART, D), F32),
    ]
    outs = pl.pallas_call(
        finish_kernel,
        out_shape=[jax.ShapeDtypeStruct(*out) for out in outs],
        in_specs=[VM] * 14,
        out_specs=[VM] * 11,
        name="finish_kernel",
    )(ret_gate, ret_up, ret_qkv, ret_out, ret_dn, block_low, grad, gain_a, gain_m, w_query, w_key, w_value,
      w_gate, w_up)
    return tuple(out.reshape(16) if out.shape == (1, 16) else out for out in outs)


def solution(mesh):
    flat = P(("dp", "ctx"), None)
    in_specs = (
        flat, flat, P("dp", None), P("dp", None, None), P(("dp", "ctx")), flat, flat, flat, flat,
        P(("dp", "ctx")), flat, flat, flat,
    )
    out_specs = (
        flat, flat, P(("dp", "ctx")), flat, flat, flat, flat, P(("dp", "ctx")), flat, flat, flat,
    )
    return jax.shard_map(
        per_device, mesh=mesh, in_specs=in_specs, out_specs=out_specs, check_vma=False
    )
```

```python
import jax
import jax.numpy as jnp
import numpy as np
from jax import lax
from jax.experimental import pallas as pl
from jax.experimental.pallas import tpu as pltpu
from jax.sharding import PartitionSpec as P

D = 2048
HEADS = 32
KV_HEADS = 4
HEAD_DIM = 64
FF = 5632
N_CTX = 8
N_DP = 16
ROWS = 128
GROUP = 1024
Q_LOC = 256
QKV_LOC = 384
FF_PART = 44
FF_PAD = 48
FF_LOC = N_DP * FF_PAD
FF_CUT = FF // N_CTX
EPSILON = 1e-05
NEG_LARGE = -1e30
MESH = pl.DeviceIdType.MESH
BF = jnp.bfloat16
F32 = jnp.float32
ANY = pl.BlockSpec(memory_space=pl.ANY)
VM = pl.BlockSpec(memory_space=pltpu.VMEM)
SM = pl.BlockSpec(memory_space=pltpu.SMEM)
ACROSS = (((1,), (1,)), ((), ()))
DOWNWARD = (((0,), (0,)), ((), ()))
PLAIN = (((1,), (0,)), ((), ()))


def contract(left_op, right_op, dims_pair):
    return lax.dot_general(left_op, right_op, dims_pair, preferred_element_type=F32)


class Place:
    def __init__(self):
        self.d = lax.axis_index("dp")
        self.c = lax.axis_index("ctx")
        self.z, self.y = lax.div(self.d, 4), lax.rem(self.d, 4)
        self.x, self.k = lax.div(self.c, 2), lax.rem(self.c, 2)

    def at_x(self, step):
        return lax.rem(self.x + step, 4)

    def on_x(self, step):
        return (self.d, self.at_x(step) * 2 + self.k)

    def sibling(self):
        return (self.d, self.x * 2 + 1 - self.k)

    def on_ctx(self, step):
        return (self.d, lax.rem(self.c + step, 8))

    def on_y(self, step):
        return (self.z * 4 + lax.rem(self.y + step, 4), self.c)

    def on_z(self, step):
        return (lax.rem(self.z + step, 4) * 4 + self.y, self.c)

    def spread_to(self):
        return (lax.rem(self.d + 2 * self.c, 16), self.c)

    def spread_from(self):
        return (lax.rem(self.d + 16 - 2 * self.c, 16), self.c)

    def spreads(self):
        return self.c != 0

    def turn_to(self):
        return (self.d, lax.rem(lax.div(self.d, 2) + 8 - self.c, 8))

    def turns(self):
        return self.turn_to()[1] != self.c


def block_at(position, index):
    return 8 * lax.rem(position, 2) + lax.rem(lax.div(position, 2) + 8 - index, 8)


class Copies:
    def __init__(self, send_sems, recv_sems):
        self.send_sems, self.recv_sems, self.used, self.started = send_sems, recv_sems, 0, []

    def make(self, src, dst, device):
        i = self.used
        self.used += 1
        return pltpu.make_async_remote_copy(
            src_ref=src,
            dst_ref=dst,
            send_sem=self.send_sems.at[i],
            recv_sem=self.recv_sems.at[i],
            device_id=device,
            device_id_type=MESH,
        )

    def send(self, src, dst, device):
        copy = self.make(src, dst, device)
        copy.start()
        self.started.append(copy)
        return copy

    def sent(self, copy):
        copy.wait_send()
        self.started = [other for other in self.started if other is not copy]

    def finish(self):
        for copy in self.started:
            copy.wait_send()


def greet(peers, extra=None, extra_on=None, meanwhile=lambda: None):
    barrier = pltpu.get_barrier_semaphore()
    for peer in peers:
        pl.semaphore_signal(barrier, 1, device_id=peer, device_id_type=MESH)
    count = len(peers)
    if extra is not None:

        @pl.when(extra_on)
        def _():
            pl.semaphore_signal(barrier, 1, device_id=extra, device_id_type=MESH)

        count = jnp.where(extra_on, count + 1, count)
    meanwhile()
    pl.semaphore_wait(barrier, count)


def hop(copies, keep, src, dst, device, far):
    sent, kept = copies.make(src, dst, device), keep(src, dst)

    def start():
        pl.when(far)(sent.start)
        pl.when(jnp.logical_not(far))(kept.start)

    def wait():
        pl.when(far)(sent.wait)
        pl.when(jnp.logical_not(far))(kept.wait)

    return start, wait


def keeper(sems):
    used = []

    def keep(src, dst):
        used.append(src)
        return pltpu.make_async_copy(src, dst, sems.at[len(used) - 1])

    return keep


def yz_peers(me):
    return [me.on_y(s) for s in (1, 2, 3)] + [me.on_z(s) for s in (1, 2, 3)]


def ctx_peers(me):
    return [me.on_ctx(s) for s in range(1, 8)]


def x_peers(me):
    return [me.on_x(1), me.on_x(3), me.sibling()]


def round_robin(*flows):
    flows = list(flows)
    while flows:
        flows = [f for f in flows if next(f, "end") != "end"]


class CtxGather:
    def __init__(self, me, copies, src, full, keep):
        self.me, self.copies, self.src, self.full = me, copies, src, full
        self.own, self.left, self.right, self.far_one = (
            me.at_x(s) * 2 + me.k for s in (0, 3, 1, 2)
        )
        self.to_right, self.to_left, self.to_sib = me.on_x(1), me.on_x(3), me.sibling()
        self.mine = keep(src, full.at[self.own])

    def pass_on(self, block, rows, device):
        at = self.full.at[block, rows]
        return self.copies.send(at, at, device)

    def start(self):
        top, low = pl.ds(0, 64), pl.ds(64, 64)
        src, home, send = self.src, self.full.at[self.own], self.copies.send
        self.r1 = send(src.at[top], home.at[top], self.to_right)
        self.l1 = send(src.at[low], home.at[low], self.to_left)
        self.s0 = send(src, home, self.to_sib)
        self.mine.start()

    def start_rest(self):
        top, low = pl.ds(0, 64), pl.ds(64, 64)
        src, home, send = self.src, self.full.at[self.own], self.copies.send
        self.r2 = send(src.at[low], home.at[low], self.to_right)
        self.l2 = send(src.at[top], home.at[top], self.to_left)

    def relay(self):
        self.r1.wait_recv()
        self.r3 = self.pass_on(self.left, pl.ds(0, 64), self.to_right)
        self.l1.wait_recv()
        self.l3 = self.pass_on(self.right, pl.ds(64, 64), self.to_left)

    def sides(self):
        self.r2.wait_recv()
        self.s1 = self.pass_on(self.left, pl.ds(0, 128), self.to_sib)
        self.l2.wait_recv()
        self.s2 = self.pass_on(self.right, pl.ds(0, 128), self.to_sib)

    def far(self):
        self.r3.wait_recv()
        self.s3 = self.pass_on(self.far_one, pl.ds(0, 64), self.to_sib)
        self.l3.wait_recv()
        self.s4 = self.pass_on(self.far_one, pl.ds(64, 64), self.to_sib)

    def wait_own(self):
        self.s0.wait_recv()
        self.mine.wait()

    def wait_sides(self):
        self.s1.wait_recv()
        self.s2.wait_recv()

    def wait_far(self):
        self.s3.wait_recv()
        self.s4.wait_recv()

    def settle(self):
        for copy in (self.r3, self.l3, self.s1, self.s2, self.s3, self.s4):
            self.copies.sent(copy)


def gather_steps(job):
    job.start()
    job.start_rest()
    yield
    job.relay()
    yield
    job.sides()
    yield
    job.far()
    yield
    job.wait_own()
    job.wait_sides()
    job.wait_far()


def ctx_gather(*args):
    return gather_steps(CtxGather(*args))


def add_rows(dst, rows, *terms):
    def step(i, carry):
        at = pl.ds(pl.multiple_of(i * 16, 16), 16)
        total = terms[0](at).astype(F32)
        for term in terms[1:]:
            total += term(at).astype(F32)
        dst[at, :] = total.astype(dst.dtype)
        return carry

    lax.fori_loop(0, rows // 16, step, 0)


class CtxScatter:
    def __init__(self, me, copies, part, scratch, direct=False):
        self.me, self.copies, self.part, self.direct = me, copies, part, direct
        self.pair, self.half_left, self.half_right, self.from_left, self.from_right = scratch
        self.to_right, self.to_left, self.to_sib = me.on_x(1), me.on_x(3), me.sibling()
        self.arriving, self.sends = {}, []

    def send(self, src, dst, device):
        copy = self.copies.send(src, dst, device)
        self.sends.append(copy)
        return copy

    def give(self, s):
        block = self.me.at_x(s) * 2 + 1 - self.me.k
        self.arriving[s] = self.send(self.part.at[block], self.pair.at[s], self.to_sib)

    def merge(self, s):
        top, low, whole = pl.ds(0, 64), pl.ds(64, 64), pl.ds(0, 128)
        self.arriving[s].wait_recv()
        block, pair, part = self.me.at_x(s) * 2 + self.me.k, self.pair, self.part
        add_rows(pair.at[s], 128, lambda at: part[block, at, :], lambda at: pair[s, at, :])
        if s == 2:
            one, other = (self.me.on_x(2),) * 2 if self.direct else (self.to_right, self.to_left)
            self.a = self.send(pair.at[2, top], self.half_left, one)
            self.b = self.send(pair.at[2, low], self.half_right, other)
        if s == 1:
            rows = whole if self.direct else low
            self.r1 = self.send(pair.at[1, rows], self.from_left.at[rows], self.to_right)
        if s == 3:
            rows = whole if self.direct else top
            self.l1 = self.send(pair.at[3, rows], self.from_right.at[rows], self.to_left)

    def relay_right(self):
        half, pair = self.half_left, self.pair
        self.a.wait_recv()
        add_rows(half, 64, lambda at: half[at, :], lambda at: pair[1, at, :])
        self.r2 = self.send(half, self.from_left.at[pl.ds(0, 64)], self.to_right)

    def relay_left(self):
        half, pair = self.half_right, self.pair
        self.b.wait_recv()
        add_rows(half, 64, lambda at: half[at, :], lambda at: pair.at[3, pl.ds(64, 64)][at, :])
        self.l2 = self.send(half, self.from_right.at[pl.ds(64, 64)], self.to_left)

    def finish(self):
        last = (self.a, self.b) if self.direct else (self.r2, self.l2)
        for copy in (self.r1, self.l1, *last):
            copy.wait_recv()

    def settle(self):
        for copy in self.sends:
            self.copies.sent(copy)

    def rows(self, half, i):
        at = pl.ds(pl.multiple_of(64 * half + i * 16, 16), 16)
        refs = [self.pair.at[0], self.from_left, self.from_right]
        total = sum(ref[at, :].astype(F32) for ref in refs)
        if self.direct:
            away = (self.half_right if half else self.half_left)
            total += away[pl.ds(pl.multiple_of(i * 16, 16), 16), :].astype(F32)
        return at, total

    def each_rows(self, use):
        for half in (0, 1):

            def step(i, carry, half=half):
                use(*self.rows(half, i))
                return carry

            lax.fori_loop(0, 4, step, 0)


SCATTER_SCRATCH = [
    pltpu.VMEM((4, 128, D), BF),
    pltpu.VMEM((64, D), BF),
    pltpu.VMEM((64, D), BF),
    pltpu.VMEM((128, D), BF),
    pltpu.VMEM((128, D), BF),
]


def halves(ref, half, by_rows):
    shape = ref.shape
    if by_rows:
        n = shape[-3]
        return ref.at[(*(slice(None),) * (len(shape) - 3), pl.ds(half * (n // 2), n // 2))]
    columns = shape[-1]
    return ref.at[
        (*(slice(None),) * (len(shape) - 1), pl.ds(half * (columns // 2), columns // 2))
    ]


def dp_axes(me, half):
    z = (me.z, me.on_z)
    y = (me.y, me.on_y)
    return (y, z) if half else (z, y)


def dp_gather(me, copies, full, half, by_rows):
    view = halves(full, half, by_rows)
    (p2, dev2), (p1, dev1) = dp_axes(me, half)

    def group(i2, j1):
        return view.at[j1, i2] if half else view.at[i2, j1]

    own = group(p2, p1)
    first = [copies.send(own, own, dev1(s)) for s in (1, 3, 2)]
    yield
    for copy in first:
        copy.wait_recv()
    every, lo, hi = pl.ds(0, 4), pl.ds(0, 2), pl.ds(2, 2)
    mine = group(p2, every)
    up = copies.send(mine, mine, dev2(1))
    down = copies.send(mine, mine, dev2(3))
    yield
    up.wait_recv()
    passed = group(lax.rem(p2 + 3, 4), lo)
    up2 = copies.send(passed, passed, dev2(1))
    down.wait_recv()
    passed = group(lax.rem(p2 + 1, 4), hi)
    down2 = copies.send(passed, passed, dev2(3))
    yield
    up2.wait_recv()
    down2.wait_recv()
    yield
    for copy in (*first, up, down, up2, down2):
        copies.sent(copy)


def add_blocks(dst, *terms):
    lead = dst.shape[:-2]
    if not lead:
        total = terms[0][...].astype(F32)
        for term in terms[1:]:
            total += term[...].astype(F32)
        dst[...] = total.astype(dst.dtype)
        return

    def step(i, carry):
        at = (lax.div(i, lead[1]), lax.rem(i, lead[1])) if len(lead) == 2 else (i,)
        total = terms[0][at].astype(F32)
        for term in terms[1:]:
            total += term[at].astype(F32)
        dst[at] = total.astype(dst.dtype)
        return carry

    lax.fori_loop(0, lead[0] * (lead[1] if len(lead) == 2 else 1), step, 0)


def dp_scatter(
    me, copies, part, half, by_rows, out, pass_up, pass_down, from_up, from_down, last, sent_from=None
):
    view = halves(part, half, by_rows)
    sent_view = view if sent_from is None else halves(sent_from, half, by_rows)
    (p1, dev1), (p2, dev2) = dp_axes(me, half)

    def group(i1, j2, of=view):
        return of.at[j2, i1] if half else of.at[i1, j2]

    every, lo, hi = pl.ds(0, 4), pl.ds(0, 2), pl.ds(2, 2)
    nxt, far, prv = (lax.rem(p1 + s, 4) for s in (1, 2, 3))
    a = copies.send(group(far, lo, sent_view), pass_up, dev1(1))
    b = copies.send(group(far, hi, sent_view), pass_down, dev1(3))
    e1 = copies.send(group(nxt, hi, sent_view), from_up.at[hi], dev1(1))
    e2 = copies.send(group(prv, lo, sent_view), from_down.at[lo], dev1(3))
    yield
    a.wait_recv()
    add_blocks(pass_up, pass_up, group(nxt, lo))
    f1 = copies.send(pass_up, from_up.at[lo], dev1(1))
    b.wait_recv()
    add_blocks(pass_down, pass_down, group(prv, hi))
    f2 = copies.send(pass_down, from_down.at[hi], dev1(3))
    yield
    for copy in (e1, e2, f1, f2):
        copy.wait_recv()
    add_blocks(from_up, from_up, from_down, group(p1, every))
    sent = [
        copies.send(from_up.at[lax.rem(p2 + s, 4)], last.at[s - 1], dev2(s)) for s in (1, 2, 3)
    ]
    yield
    for copy in sent:
        copy.wait_recv()
    add_blocks(halves(out, half, by_rows), from_up.at[p2], last.at[0], last.at[1], last.at[2])


def dp_scatter_scratch(block, by_rows):
    block = (block[0] // 2, *block[1:]) if by_rows else (*block[:-1], block[-1] // 2)
    return [pltpu.VMEM((lead, *block), BF) for lead in (2, 2, 4, 4, 3)] * 2


def turn(values, cos_of, sin_of):
    lane = lax.broadcasted_iota(jnp.int32, values.shape, 1)
    other = jnp.where(
        lax.rem(lane, 64) < 32, pltpu.roll(values, 96, 1), pltpu.roll(values, 32, 1)
    )
    return values * cos_of + other * sin_of


def keys_only(cos_of, sin_of):
    lane = lax.broadcasted_iota(jnp.int32, cos_of.shape, 1)
    return jnp.where(lane < 64, cos_of, 1.0), jnp.where(lane < 64, sin_of, 0.0)


def split_halves(values):
    return (
        jnp.concatenate([values[0:64], values[128:192]], 0),
        jnp.concatenate([values[64:128], values[192:256]], 0),
    )


def half_rows(half, chip):
    return pl.ds(pl.multiple_of(half * 512 + chip * 128, 128), 128)


def of_both(ref, half, chips, lanes=slice(None)):
    pieces = [ref[half_rows(half, chip), lanes] for chip in chips]
    return jnp.concatenate(pieces, 0) if len(pieces) > 1 else pieces[0]


def to_both(ref, half, chips, lanes, values):
    for i, chip in enumerate(chips):
        ref[half_rows(half, chip), lanes] = values[128 * i : 128 * i + 128]


def group_rows(chip, core, half):
    return pl.ds(pl.multiple_of(chip * 256 + core * 128 + half * 64, 64), 64)


def lay_out(lengths, spans, inverse, meta, places, cos_of, sin_of):
    j = lax.broadcasted_iota(jnp.int32, (1, GROUP), 1)
    slot, packed = lax.div(j, 64), lax.rem(j, 64)
    for r in range(8):
        for half in range(2):
            packed = packed + jnp.where(slot == half * 8 + r, spans[0, 2 * r + half] * 64, 0)
    first, end = jnp.zeros_like(packed), 0
    for i in range(4):
        end = end + lengths[0, i]
        first = first + jnp.where(packed >= end, lengths[0, i], 0)
    places[...] = packed.astype(F32)
    row = lax.broadcasted_iota(jnp.int32, (8, GROUP), 0)
    meta[...] = jnp.transpose(
        jnp.where(row == 0, packed, jnp.where(row == 1, first, packed - first)).astype(F32)
    )

    def table(i, carry):
        at = pl.ds(pl.multiple_of(i * 128, 128), 128)
        angles = meta[at, 2:3] * inverse[...]
        lane = lax.broadcasted_iota(jnp.int32, angles.shape, 1)
        sines = jnp.sin(angles)
        cos_of[at, :] = jnp.cos(angles)
        sin_of[at, :] = jnp.where(lax.rem(lane, 64) < 32, -sines, sines)
        return carry

    lax.fori_loop(0, 8, table, 0)


def mask_bias(bias, half, chips, meta, places):
    keys = 512 * (half + 1)
    seen = places[:, :keys]
    here = of_both(meta, half, chips)
    allowed = (seen <= here[:, 0:1]) & (seen >= here[:, 1:2])
    bias[: 128 * len(chips), :keys] = jnp.where(allowed, 0.0, NEG_LARGE).astype(F32)


def attend(half, chips, q, kv, bias, o, log_sums):
    keys = 512 * (half + 1)
    k, v = kv[:keys, :64], kv[:keys, 64:]
    for h in range(HEADS // N_CTX):
        lanes = slice(h * 64, h * 64 + 64)
        scores = contract(of_both(q, half, chips, lanes), k, ACROSS) + bias[: 128 * len(chips), :keys]
        peak = jnp.max(scores, -1, keepdims=True)
        expo = jnp.exp(scores - peak)
        total = jnp.sum(expo, -1, keepdims=True)
        out = (contract(expo.astype(BF), v, PLAIN) / total).astype(BF)
        for i in range(2 * len(chips)):
            o[group_rows(chips[i // 2], i % 2, half), lanes] = out[64 * i : 64 * i + 64]
        to_both(log_sums, half, chips, slice(h, h + 1), peak + jnp.log(total))


def column(row):
    i = lax.broadcasted_iota(jnp.int32, (16, 16), 0)
    j = lax.broadcasted_iota(jnp.int32, (16, 16), 1)
    return jnp.sum(jnp.where(i == j, row[...].astype(F32), 0.0), 1, keepdims=True)


def spread():
    j = lax.broadcasted_iota(jnp.int32, (FF_CUT, FF_LOC), 0)
    to = lax.broadcasted_iota(jnp.int32, (FF_CUT, FF_LOC), 1)
    return jnp.where(FF_PAD * lax.div(j, FF_PART) + lax.rem(j, FF_PART) == to, 1.0, 0.0).astype(BF)


def front_kernel(
    lengths, spans, inverse, gain_attn, gain_mlp, w_query, w_key, w_value, w_out_own, w_gate, w_up,
    w_down, tokens, cot_own,
    n1_out, w_qkv_out, w_out_out, da_full, part_y, g_up, own_gate_out, own_dn_out,
    h1_out, dh1_out, q_out, kv_out, o_out, log_sums_out, cos_out, sin_out, meta_out, places_out,
    h1, dh1, q, kv, o, log_sums, cos_of, sin_of, meta, places,
    n1_own, qkv_src, od_src, gu_src, stack, n1, w_qkv, od_mid, w_out, bias, part,
    n2, cot_full, w_gu, w_dn, w_dn_here, hm, dgu, own_gate, own_dn, *rest,
):
    ss, rs, ls = rest[-3:]
    scr, scr_dn, scr_gate = rest[0:5], rest[5:15], rest[15:25]
    me = Place()
    w_od = w_dn_here.at[:, :, 0]

    def prepare():
        def norm(i, carry):
            at = pl.ds(pl.multiple_of(i * 16, 16), 16)
            x = tokens[at, :].astype(F32)
            scale = lax.rsqrt(jnp.mean(x * x, -1, keepdims=True) + EPSILON)
            n1_own[at, :] = (x * scale).astype(BF)
            return carry

        lax.fori_loop(0, 8, norm, 0)
        gain = column(gain_attn)
        for i in range(8):
            pair = slice(64 * (i // 2), 64 * (i // 2) + 64)
            scaled = w_query[:, Q_LOC * i : Q_LOC * i + Q_LOC].astype(F32) * gain
            qkv_src[i, :, :Q_LOC] = scaled.astype(BF)
            both = jnp.concatenate([w_key[:, pair], w_value[:, pair]], 1).astype(F32) * gain
            qkv_src[i, :, Q_LOC:] = both.astype(BF)
        od_src[0] = w_out_own[...]
        od_src[1] = w_down[0:16, :]
        od_src[2] = w_down[16:32, :]
        tail = jnp.concatenate([w_down[32:FF_PART, :].astype(F32), jnp.zeros((4, D), F32)], 0)
        od_src[3] = tail.astype(BF)

    greet(ctx_peers(me) + yz_peers(me), me.spread_from(), me.spreads(), prepare)
    copies = Copies(ss, rs)
    keep = keeper(ls)

    def to_indices(src, home):
        sent = [
            copies.send(src.at[lax.rem(me.c + s, 8)], home.at[me.c], me.on_ctx(s))
            for s in range(1, 8)
        ]
        mine = keep(src.at[me.c], home.at[me.c])
        mine.start()

        def wait():
            for copy in sent:
                copy.wait_recv()
            mine.wait()

        return wait

    qkv_there = to_indices(qkv_src, w_qkv.at[me.z, me.y])
    spread_start, spread_there = hop(
        copies, keep, od_src, od_mid, me.spread_to(), me.spreads()
    )
    turns = [
        hop(copies, keep, od_mid.at[0], w_od.at[me.z, me.y], me.turn_to(), me.turns()),
        hop(copies, keep, od_mid.at[pl.ds(1, 3)], w_dn.at[me.z, me.y], me.turn_to(), me.turns()),
    ]
    spread_start()
    rows = CtxGather(me, copies, n1_own, n1, keep)
    rows.start()
    gain = column(gain_mlp)
    for j, w in enumerate((w_gate, w_up)):
        for i in range(8):
            scaled = w[:, FF_CUT * i : FF_CUT * i + FF_CUT].astype(F32) * gain
            stack[16 * i : 16 * i + 16, :] = scaled.astype(BF)
        placed = contract(stack[...], spread(), PLAIN).astype(BF)
        gu_src[:, :, FF_LOC * j : FF_LOC * j + FF_LOC] = placed.reshape(8, 16, FF_LOC)
    gu_there = to_indices(gu_src, w_gu.at[me.z, me.y])

    def steps(flows):
        for flow in flows:
            next(flow, None)

    f_qkv = [dp_gather(me, copies, w_qkv, h, True) for h in (0, 1)]
    f_out = [dp_gather(me, copies, w_od, h, False) for h in (0, 1)]
    f_gu = [dp_gather(me, copies, w_gu, h, True) for h in (0, 1)]
    f_dn = [dp_gather(me, copies, w_dn, h, False) for h in (0, 1)]
    seeds = ctx_gather(me, copies, cot_own, cot_full, keep)
    qkv_there()
    steps(f_qkv)
    spread_there()
    for start, _ in turns:
        start()
    rows.start_rest()
    first_row_copies = (rows.r1, rows.l1, rows.s0, rows.r2, rows.l2)
    steps(f_qkv)
    gu_there()
    steps(f_qkv)
    rows.relay()
    turns[0][1]()
    steps(f_out)
    steps(f_gu)
    lay_out(lengths, spans, inverse, meta, places, cos_of, sin_of)
    turns[1][1]()
    steps(f_out)
    steps(f_dn)
    rows.sides()
    steps(f_qkv)
    rows.far()
    next(seeds)
    steps(f_out)
    steps(f_gu)
    rows.wait_own()
    rows.wait_sides()
    rows.wait_far()
    keeps = [keep(n1, n1_out), keep(w_qkv, w_qkv_out)]
    for copy in keeps:
        copy.start()
    kept = []

    def leave(*pairs):
        for src, dst in pairs:
            kept.append(keep(src, dst))
            kept[-1].start()


    def project(chip, carry):
        x = n1[pl.ds(2 * chip, 2)].reshape(256, D)
        qkv = contract(x, w_qkv[...].reshape(D, QKV_LOC), PLAIN)
        for half, rows_of in enumerate(split_halves(qkv)):
            at = half_rows(half, chip)
            cos_b, sin_b = cos_of[at, :], sin_of[at, :]
            for j in (0, 1):
                turned = turn(rows_of[:, j * 128 : j * 128 + 128], cos_b, sin_b)
                q[at, j * 128 : j * 128 + 128] = (turned * HEAD_DIM ** (-0.5)).astype(BF)
            kv[at, :] = turn(rows_of[:, Q_LOC:], *keys_only(cos_b, sin_b)).astype(BF)
        return carry

    lax.fori_loop(0, 4, project, 0)
    leave((q, q_out), (kv, kv_out), (cos_of, cos_out), (sin_of, sin_out))
    leave((meta, meta_out), (places, places_out))
    steps(f_out)
    steps(f_dn)

    def place(i, carry):
        w_out[block_at(i, me.c)] = w_od[lax.div(i, 4), lax.rem(i, 4)]
        return carry

    lax.fori_loop(0, 16, place, 0)
    keeps.append(keep(w_out, w_out_out))
    keeps[-1].start()
    sums = CtxScatter(me, copies, part, scr)

    def heads_of(half, *steps_away):
        chips = [me.at_x(s) for s in steps_away]
        mask_bias(bias, half, chips, meta, places)
        attend(half, chips, q, kv, bias, o, log_sums)

    def out_of(s):
        at = pl.ds(pl.multiple_of(me.at_x(s) * 256, 256), 256)
        term = contract(o[at, :], w_out[...].reshape(Q_LOC, D), PLAIN).astype(BF)
        part[pl.ds(me.at_x(s) * 2, 2)] = term.reshape(2, 128, D)
        sums.give(s)

    heads_of(0, 2, 1)
    heads_of(1, 2, 1)
    next(seeds)
    out_of(2)
    out_of(1)
    heads_of(0, 3)
    sums.merge(2)
    sums.merge(1)
    next(seeds)
    heads_of(1, 3)
    out_of(3)
    steps(f_gu)
    heads_of(0, 0)
    sums.merge(3)
    sums.relay_right()
    sums.relay_left()
    next(seeds)
    heads_of(1, 0)
    out_of(0)
    sums.merge(0)
    steps(f_dn)
    sums.finish()
    sums.settle()
    leave((o, o_out), (log_sums, log_sums_out))
    own_norm = n1_own

    def norm(at, branch):
        hidden = tokens[at, :].astype(F32) + branch
        scale = lax.rsqrt(jnp.mean(hidden * hidden, -1, keepdims=True) + EPSILON)
        h1[at, :] = hidden
        own_norm[at, :] = (hidden * scale).astype(BF)

    for copy in first_row_copies:
        copies.sent(copy)
    sums.each_rows(norm)
    normed = CtxGather(me, copies, own_norm, n2, keep)
    normed.start()
    normed.start_rest()
    leave((h1, h1_out))
    steps(f_gu)
    steps(f_dn)
    next(seeds, None)

    steps(f_out)

    def place_down(i, carry):
        here = block_at(i, me.c)
        w_dn_here[lax.div(here, 4), lax.rem(here, 4)] = w_dn[lax.div(i, 4), lax.rem(i, 4)]
        return carry

    lax.fori_loop(0, 16, place_down, 0)
    sums = CtxScatter(me, copies, part, scr, direct=True)

    def two(s):
        return pl.ds(me.at_x(s) * 2, 2)

    def gate_up(s):
        at = pl.ds(pl.multiple_of(me.at_x(s) * 256, 256), 256)
        x = n2[two(s)].reshape(256, D)
        gate = contract(x, w_gu[..., :FF_LOC].reshape(D, FF_LOC), PLAIN)
        up = contract(x, w_gu[..., FF_LOC:].reshape(D, FF_LOC), PLAIN)
        sig = jax.nn.sigmoid(gate)
        silu = gate * sig
        hm[at, :] = (silu * up).astype(BF)
        inner = contract(
            cot_full[two(s)].reshape(256, D), w_dn_here[...].reshape(FF_LOC, D), ACROSS
        )
        dgu[at, :FF_LOC] = (inner * up * (sig + silu * (1.0 - sig))).astype(BF)
        dgu[at, FF_LOC:] = (inner * silu).astype(BF)
        term = contract(dgu[at, :], w_gu[...].reshape(D, 2 * FF_LOC), ACROSS).astype(BF)
        part[two(s)] = term.reshape(2, 128, D)
        sums.give(s)

    normed.wait_own()
    gate_up(0)
    normed.relay()
    normed.sides()
    normed.wait_sides()
    gate_up(1)
    normed.far()
    gate_up(3)
    sums.merge(1)
    sums.merge(3)
    normed.wait_far()
    gate_up(2)
    for copy in keeps:
        copy.wait()
    rows.settle()
    steps(f_gu)
    steps(f_dn)
    part_out = n1

    def outer(j, carry):
        at = pl.ds(pl.multiple_of(256 * j, 256), 256)
        term = contract(n2[:, :, at].reshape(GROUP, 256), dgu[...], DOWNWARD)
        where = (lax.div(j, 2), pl.ds(2 * lax.rem(j, 2), 2))
        w_gu[where] = term.astype(BF).reshape(2, 8, 16, 2 * FF_LOC)
        return carry

    lax.fori_loop(0, 4, outer, 0)
    sums.merge(2)
    lax.fori_loop(4, 8, outer, 0)
    gate_columns, up_columns = (
        w_gu.at[:, :, :, :, pl.ds(FF_LOC * j, FF_LOC)] for j in (0, 1)
    )
    f_gate = [
        dp_scatter(me, copies, gate_columns, h, True, own_gate, *scr_gate[h * 5 : h * 5 + 5])
        for h in (0, 1)
    ]
    steps(f_gate)
    leave((up_columns, g_up))

    def down(i, carry):
        at = pl.ds(pl.multiple_of(i * 256, 256), 256)
        y = contract(hm[at, :], w_dn_here[...].reshape(FF_LOC, D), PLAIN).astype(BF)
        part_out[pl.ds(2 * i, 2)] = y.reshape(2, 128, D)
        return carry

    lax.fori_loop(0, 4, down, 0)
    leave((part_out, part_y))
    for j in (0, 1):
        for i in (0, 1):
            cols = slice(1024 * i, 1024 * i + 1024)
            term = contract(
                hm[:, 384 * j : 384 * j + 384], cot_full[:, :, cols].reshape(GROUP, 1024), DOWNWARD
            )
            w_dn_here[2 * j : 2 * j + 2, :, :, :, cols] = term.astype(BF).reshape(2, 4, 3, 16, 1024)

    def place_back(i, carry):
        here = block_at(i, me.c)
        w_dn[lax.div(i, 4), lax.rem(i, 4)] = w_dn_here[lax.div(here, 4), lax.rem(here, 4)]
        return carry

    lax.fori_loop(0, 16, place_back, 0)
    flows = [
        dp_scatter(me, copies, w_dn, h, False, own_dn, *scr_dn[h * 5 : h * 5 + 5]) for h in (0, 1)
    ]
    steps(flows)

    sums.merge(0)
    steps(f_gate)
    sums.finish()
    da = own_norm
    copies.sent(normed.s0)
    for copy in (normed.r1, normed.r2, normed.l1, normed.l2):
        copies.sent(copy)

    def norm_back(at, u):
        hidden = h1[at, :]
        scale = lax.rsqrt(jnp.mean(hidden * hidden, -1, keepdims=True) + EPSILON)
        grad = (
            cot_own[at, :].astype(F32)
            + scale * u
            - hidden * (scale * scale * scale * jnp.mean(u * hidden, -1, keepdims=True))
        )
        dh1[at, :] = grad
        da[at, :] = grad.astype(BF)

    sums.each_rows(norm_back)
    rows_da = ctx_gather(me, copies, da, da_full, keep)
    next(rows_da)
    leave((dh1, dh1_out))
    steps(flows)
    next(rows_da)
    steps(f_gate)
    next(rows_da)
    steps(flows)
    next(rows_da)
    steps(f_gate)
    steps(flows)
    leave((own_gate, own_gate_out), (own_dn, own_dn_out))
    next(rows_da, None)
    for copy in kept:
        copy.wait()
    copies.finish()


def attend_back(half, chips, q, kv, do, log_sums, deltas, bias, dqkv, dk, dv):
    keys = 512 * (half + 1)
    k, v = kv[:keys, :64], kv[:keys, 64:]
    logs, delta = of_both(log_sums, half, chips), of_both(deltas, half, chips)
    for h in range(HEADS // N_CTX):
        lanes = slice(h * 64, h * 64 + 64)
        queries, grads = of_both(q, half, chips, lanes), of_both(do, half, chips, lanes)
        scores = contract(queries, k, ACROSS) + bias[: 128 * len(chips), :keys]
        probs = jnp.exp(scores - logs[:, h : h + 1])
        score_grad = probs * (contract(grads, v, ACROSS) - delta[:, h : h + 1])
        score_grad = score_grad.astype(BF)
        rows = contract(score_grad, k, PLAIN) * HEAD_DIM ** (-0.5)
        to_both(dqkv, half, chips, lanes, rows)
        dk[:keys, :] += contract(score_grad, queries, DOWNWARD)
        dv[:keys, :] += contract(probs.astype(BF), grads, DOWNWARD)


def end_kernel(
    da_in, part_y_in, g_up_in, n1_in, w_qkv_in, w_out_in, own_gate, own_dn,
    q_in, kv_in, o_in, log_sums_in, cos_in, sin_in, meta_in, places_in, h1_in, dh1_in, tokens,
    block_out, grad, ret_gate, ret_up, ret_qkv, ret_out, ret_dn,
    q, kv, o, log_sums, cos_of, sin_of, meta, places, h1, dh1, da, part_y, g_up, n1, w_qkv, w_out, do, deltas, dqkv, dqkv_low, dk, dv, bias,
    g_qkv, g_nat, g_out, own_up, own_qkv, own_out, mid_out, mid_dn, *rest,
):
    ss, rs, ls = rest[-3:]
    scr_y, scr = rest[0:5], rest[5:10]
    scr_up, scr_qkv, scr_out = rest[10:20], rest[20:30], rest[30:40]
    me = Place()
    copies, keep = Copies(ss, rs), keeper(ls)

    def load(src, dst):
        copy = keep(src, dst)
        copy.start()
        return copy

    load_y = load(part_y_in, part_y)
    load_out = load(w_out_in, w_out)
    load_da = load(da_in, da)
    load_rows = [
        load(src, dst)
        for src, dst in ((o_in, o), (q_in, q), (kv_in, kv), (log_sums_in, log_sums), (meta_in, meta), (places_in, places))
    ]
    load_up = load(g_up_in, g_up)
    load_last = [
        load(src, dst)
        for src, dst in ((cos_in, cos_of), (sin_in, sin_of), (h1_in, h1), (dh1_in, dh1))
    ]
    load_qkv = load(w_qkv_in, w_qkv)
    load_n1 = load(n1_in, n1)
    greet(ctx_peers(me) + yz_peers(me), me.spread_to(), me.spreads())
    def steps(flows):
        for flow in flows:
            next(flow, None)


    def scatter(g, scratch, own, by_rows, sent_from=None):
        return [
            dp_scatter(me, copies, g, h, by_rows, own, *scratch[h * 5 : h * 5 + 5], sent_from)
            for h in (0, 1)
        ]

    def to_indices(own, back):
        sent = [
            copies.send(own.at[lax.rem(me.c + s, 8)], back.at[me.c], me.on_ctx(s))
            for s in range(1, 8)
        ]
        mine = keep(own.at[me.c], back.at[me.c])
        mine.start()

        def wait():
            for copy in sent:
                copy.wait_recv()
            mine.wait()

        return wait

    f_up = scatter(g_up, scr_up, own_up, True, g_up_in)
    steps(f_up)
    gate_back = to_indices(own_gate, ret_gate)
    load_y.wait()
    sums_y = CtxScatter(me, copies, part_y, scr_y)
    for s in (2, 1, 3, 0):
        sums_y.give(s)
    turn_dn = hop(copies, keep, own_dn, mid_dn, me.turn_to(), me.turns())
    home_dn = hop(copies, keep, mid_dn, ret_dn, me.spread_from(), me.spreads())
    turn_dn[0]()
    load_out.wait()
    load_da.wait()
    for copy in load_rows:
        copy.wait()

    def attended_grad(i, carry):
        at = pl.ds(pl.multiple_of(i * 256, 256), 256)
        x = da[pl.ds(2 * i, 2)].reshape(256, D)
        grads = contract(x, w_out[...].reshape(Q_LOC, D), ACROSS).astype(BF)
        both = grads.astype(F32) * o[at, :].astype(F32)
        delta = [
            jnp.sum(both[:, h * 64 : h * 64 + 64], -1, keepdims=True)
            for h in range(HEADS // N_CTX)
        ]
        for ref, values in ((do, grads), (deltas, jnp.concatenate(delta, 1))):
            for half, rows_of in enumerate(split_halves(values)):
                ref[half_rows(half, i), :] = rows_of
        return carry

    lax.fori_loop(0, 4, attended_grad, 0)

    def out_grads():
        for i in (0, 1):
            cols = slice(1024 * i, 1024 * i + 1024)
            term = contract(o[...], da[:, :, cols].reshape(GROUP, 1024), DOWNWARD)
            g_nat[:, :, cols] = term.astype(BF).reshape(16, 16, 1024)

        def place(i, carry):
            g_out[lax.div(i, 4), lax.rem(i, 4)] = g_nat[block_at(i, me.c)]
            return carry

        lax.fori_loop(0, 16, place, 0)

    dk[...] = jnp.zeros_like(dk)
    dv[...] = jnp.zeros_like(dv)

    def heads_of(half, *chips):
        mask_bias(bias, half, chips, meta, places)
        attend_back(half, chips, q, kv, do, log_sums, deltas, bias, dqkv, dk, dv)

    heads_of(1, 0, 1)
    sums_y.merge(2)
    sums_y.merge(1)
    sums_y.merge(3)
    load_up.wait()
    steps(f_up)
    heads_of(0, 0, 1)
    out_grads()
    f_out = scatter(g_out, scr_out, own_out, False)
    steps(f_out)
    turn_dn[1]()
    home_dn[0]()
    sums_y.relay_right()
    sums_y.relay_left()
    sums_y.merge(0)
    heads_of(1, 2, 3)
    steps(f_up)
    steps(f_out)
    heads_of(0, 2, 3)
    load_qkv.wait()
    for copy in load_last:
        copy.wait()
    dqkv[:, Q_LOC : Q_LOC + 64] = dk[...]
    dqkv[:, Q_LOC + 64 :] = dv[...]

    def turn_back(chip, carry):
        for half in (0, 1):
            at = half_rows(half, chip)
            cos_b, sin_b = cos_of[at, :], -sin_of[at, :]
            turned = [turn(dqkv[at, j * 128 : j * 128 + 128], cos_b, sin_b) for j in (0, 1)]
            turned.append(turn(dqkv[at, Q_LOC:], *keys_only(cos_b, sin_b)))
            turned = jnp.concatenate(turned, 1).astype(BF)
            for core in (0, 1):
                rows_of = turned[64 * core : 64 * core + 64]
                dqkv_low[group_rows(chip, core, half), :] = rows_of
        return carry

    lax.fori_loop(0, 4, turn_back, 0)
    load_n1.wait()

    def outer(j, carry):
        at = pl.ds(pl.multiple_of(256 * j, 256), 256)
        term = contract(n1[:, :, at].reshape(GROUP, 256), dqkv_low[...], DOWNWARD)
        where = (lax.div(j, 2), pl.ds(2 * lax.rem(j, 2), 2))
        g_qkv[where] = term.astype(BF).reshape(2, 8, 16, QKV_LOC)
        return carry

    lax.fori_loop(0, 8, outer, 0)
    f_qkv = scatter(g_qkv, scr_qkv, own_qkv, True)
    steps(f_qkv)
    part = part_y
    for s in (2, 1, 3, 0):
        copies.sent(sums_y.arriving[s])
    sums = CtxScatter(me, copies, part, scr)

    def rows_of(s):
        at = pl.ds(pl.multiple_of(me.at_x(s) * 256, 256), 256)
        term = contract(dqkv_low[at, :], w_qkv[...].reshape(D, QKV_LOC), ACROSS).astype(BF)
        part[pl.ds(me.at_x(s) * 2, 2)] = term.reshape(2, 128, D)
        sums.give(s)

    rows_of(2)
    rows_of(1)
    sums.merge(2)
    rows_of(3)
    sums.merge(1)
    sums.merge(3)
    rows_of(0)
    steps(f_qkv)
    steps(f_up)
    up_back = to_indices(own_up, ret_up)
    steps(f_out)
    sums_y.finish()

    def finish_y(at, y):
        block_out[at, :] = (h1[at, :] + y).astype(BF)

    sums_y.each_rows(finish_y)
    steps(f_qkv)
    sums.relay_right()
    sums.relay_left()
    sums.merge(0)
    steps(f_out)
    turn_out = hop(copies, keep, own_out, mid_out, me.turn_to(), me.turns())
    home_out = hop(copies, keep, mid_out, ret_out, me.spread_from(), me.spreads())
    turn_out[0]()
    steps(f_qkv)
    qkv_back = to_indices(own_qkv, ret_qkv)
    turn_out[1]()
    home_out[0]()
    sums.finish()

    def finish(at, u):
        x = tokens[at, :].astype(F32)
        scale = lax.rsqrt(jnp.mean(x * x, -1, keepdims=True) + EPSILON)
        grad[at, :] = (
            dh1[at, :]
            + scale * u
            - x * (scale * scale * scale * jnp.mean(u * x, -1, keepdims=True))
        )

    sums.each_rows(finish)
    gate_back()
    up_back()
    home_dn[1]()
    home_out[1]()
    qkv_back()
    copies.finish()


def finish_kernel(
    ret_gate, ret_up, ret_qkv, ret_out, ret_dn, block_in, grad_in, gain_attn, gain_mlp,
    w_query, w_key, w_value, w_gate, w_up,
    block_out, grad, d_gain_attn, d_query, d_key, d_value, d_out, d_gain_mlp, d_gate, d_up, d_down,
):
    block_out[...] = block_in[...]
    grad[...] = grad_in[...]
    d_out[...] = ret_out[...].astype(F32)
    for i in range(3):
        n = min(16, FF_PART - 16 * i)
        d_down[16 * i : 16 * i + n, :] = ret_dn[i].astype(F32)[:n]

    def as_row(values):
        i = lax.broadcasted_iota(jnp.int32, (16, 16), 0)
        j = lax.broadcasted_iota(jnp.int32, (16, 16), 1)
        return jnp.sum(jnp.where(i == j, values, 0.0), 0, keepdims=True)

    def give(out, weights, lanes, raw, gain):
        out[:, lanes] = raw * gain
        return jnp.sum(weights[:, lanes].astype(F32) * raw, 1, keepdims=True)

    gain, total = column(gain_attn), jnp.zeros((16, 1), F32)
    for i in range(8):
        lanes = slice(Q_LOC * i, Q_LOC * i + Q_LOC)
        total += give(d_query, w_query, lanes, ret_qkv[i, :, :Q_LOC].astype(F32), gain)
    for i in range(4):
        both = ret_qkv[2 * i, :, Q_LOC:].astype(F32) + ret_qkv[2 * i + 1, :, Q_LOC:].astype(F32)
        lanes = slice(64 * i, 64 * i + 64)
        total += give(d_key, w_key, lanes, both[:, :64], gain)
        total += give(d_value, w_value, lanes, both[:, 64:], gain)
    d_gain_attn[...] = as_row(total)
    gain, total = column(gain_mlp), jnp.zeros((16, 1), F32)
    for out, weights, back in ((d_gate, w_gate, ret_gate), (d_up, w_up, ret_up)):
        raw = contract(back[...].reshape(128, FF_LOC), spread(), ACROSS)
        for i in range(8):
            lanes = slice(FF_CUT * i, FF_CUT * i + FF_CUT)
            total += give(out, weights, lanes, raw[16 * i : 16 * i + 16], gain)
    d_gain_mlp[...] = as_row(total)


def call(kernel, number, ins, in_specs, outs, out_specs, scratch, n_copies, n_local):
    return pl.pallas_call(
        kernel,
        out_shape=[jax.ShapeDtypeStruct(*o) for o in outs],
        in_specs=in_specs,
        out_specs=out_specs,
        scratch_shapes=[
            *scratch,
            pltpu.SemaphoreType.DMA((n_copies,)),
            pltpu.SemaphoreType.DMA((n_copies,)),
            pltpu.SemaphoreType.DMA((n_local,)),
        ],
        compiler_params=pltpu.CompilerParams(
            collective_id=number, has_side_effects=True, vmem_limit_bytes=62 << 20
        ),
        name=kernel.__name__,
    )(*ins)


def per_device(
    tokens, cotangent, lengths, spans, gain_attn, w_query, w_key, w_value, w_out, gain_mlp,
    w_gate, w_up, w_down,
):
    pair = (2 * (np.arange(128) % 32)).astype(np.float32)
    inverse = np.power(np.float32(10000.0), -pair / np.float32(HEAD_DIM)).astype(np.float32)[None]
    gain_a, gain_m = gain_attn[None], gain_mlp[None]
    rows = [
        ((128, D), F32), ((128, D), F32), ((GROUP, Q_LOC), BF), ((GROUP, 128), BF),
        ((GROUP, Q_LOC), BF), ((GROUP, 4), F32), ((GROUP, 128), F32), ((GROUP, 128), F32),
        ((GROUP, 8), F32), ((1, GROUP), F32),
    ]

    n1, wf_qkv, wf_out, da, part_y, g_up, *owned, h1, dh1, q, kv, o, log_sums, cos_of, sin_of, meta, places = call(
        front_kernel, 1,
        (lengths, spans.reshape(1, 16), jnp.asarray(inverse), gain_a, gain_m, w_query, w_key,
         w_value, w_out, w_gate, w_up, w_down, tokens, cotangent),
        [SM] * 2 + [VM] * 12,
        [((8, 128, D), BF), ((4, 4, 8, 16, QKV_LOC), BF), ((16, 16, D), BF), ((8, 128, D), BF),
         ((8, 128, D), BF), ((4, 4, 8, 16, FF_LOC), BF), ((8, 16, FF_LOC), BF), ((3, 16, D), BF),
         *rows],
        [ANY] * 18,
        [*(pltpu.VMEM(*row) for row in rows), pltpu.VMEM((128, D), BF), pltpu.VMEM((8, 16, QKV_LOC), BF), pltpu.VMEM((4, 16, D), BF),
         pltpu.VMEM((8, 16, 2 * FF_LOC), BF), pltpu.VMEM((128, FF_CUT), BF),
         pltpu.VMEM((8, 128, D), BF), pltpu.VMEM((4, 4, 8, 16, QKV_LOC), BF),
         pltpu.VMEM((4, 16, D), BF), pltpu.VMEM((16, 16, D), BF), pltpu.VMEM((256, GROUP), F32),
         pltpu.VMEM((8, 128, D), BF),
         pltpu.VMEM((8, 128, D), BF), pltpu.VMEM((8, 128, D), BF),
         pltpu.VMEM((4, 4, 8, 16, 2 * FF_LOC), BF), pltpu.VMEM((4, 4, 3, 16, D), BF),
         pltpu.VMEM((4, 4, 3, 16, D), BF), pltpu.VMEM((GROUP, FF_LOC), BF),
         pltpu.VMEM((GROUP, 2 * FF_LOC), BF), pltpu.VMEM((8, 16, FF_LOC), BF),
         pltpu.VMEM((3, 16, D), BF), *SCATTER_SCRATCH, *dp_scatter_scratch((3, 16, D), False),
         *dp_scatter_scratch((8, 16, FF_LOC), True)], 192, 32,
    )

    block_low, grad, ret_gate, ret_up, ret_qkv, ret_out, ret_dn = call(
        end_kernel, 3,
        (da, part_y, g_up, n1, wf_qkv, wf_out, *owned, q, kv, o, log_sums, cos_of, sin_of, meta,
         places, h1, dh1, tokens),
        [ANY] * 18 + [VM],
        [((128, D), BF), ((128, D), F32), ((8, 16, FF_LOC), BF), ((8, 16, FF_LOC), BF),
         ((8, 16, QKV_LOC), BF), ((16, D), BF), ((3, 16, D), BF)],
        [VM, VM] + [ANY] * 5,
        [*(pltpu.VMEM(*row) for row in rows[2:] + rows[:2]), pltpu.VMEM((8, 128, D), BF), pltpu.VMEM((8, 128, D), BF),
         pltpu.VMEM((4, 4, 8, 16, FF_LOC), BF), pltpu.VMEM((8, 128, D), BF),
         pltpu.VMEM((4, 4, 8, 16, QKV_LOC), BF), pltpu.VMEM((16, 16, D), BF),
         pltpu.VMEM((GROUP, Q_LOC), BF), pltpu.VMEM((GROUP, 4), F32),
         pltpu.VMEM((GROUP, QKV_LOC), F32),
         pltpu.VMEM((GROUP, QKV_LOC), BF), pltpu.VMEM((GROUP, 64), F32),
         pltpu.VMEM((GROUP, 64), F32), pltpu.VMEM((256, GROUP), F32),
         pltpu.VMEM((4, 4, 8, 16, QKV_LOC), BF),
         pltpu.VMEM((16, 16, D), BF), pltpu.VMEM((4, 4, 16, D), BF),
         pltpu.VMEM((8, 16, FF_LOC), BF), pltpu.VMEM((8, 16, QKV_LOC), BF),
         pltpu.VMEM((16, D), BF), pltpu.VMEM((16, D), BF), pltpu.VMEM((3, 16, D), BF),
         *SCATTER_SCRATCH, *SCATTER_SCRATCH, *dp_scatter_scratch((8, 16, FF_LOC), True),
         *dp_scatter_scratch((8, 16, QKV_LOC), True), *dp_scatter_scratch((16, D), False)],
        112, 40,
    )

    outs = [
        ((128, D), BF), ((128, D), F32), ((1, 16), F32), ((16, D), F32), ((16, 256), F32),
        ((16, 256), F32), ((16, D), F32), ((1, 16), F32), ((16, FF), F32), ((16, FF), F32),
        ((FF_PART, D), F32),
    ]
    outs = pl.pallas_call(
        finish_kernel,
        out_shape=[jax.ShapeDtypeStruct(*out) for out in outs],
        in_specs=[VM] * 14,
        out_specs=[VM] * 11,
        name="finish_kernel",
    )(ret_gate, ret_up, ret_qkv, ret_out, ret_dn, block_low, grad, gain_a, gain_m, w_query, w_key, w_value,
      w_gate, w_up)
    return tuple(out.reshape(16) if out.shape == (1, 16) else out for out in outs)


def solution(mesh):
    flat = P(("dp", "ctx"), None)
    in_specs = (
        flat, flat, P("dp", None), P("dp", None, None), P(("dp", "ctx")), flat, flat, flat, flat,
        P(("dp", "ctx")), flat, flat, flat,
    )
    out_specs = (
        flat, flat, P(("dp", "ctx")), flat, flat, flat, flat, P(("dp", "ctx")), flat, flat, flat,
    )
    return jax.shard_map(
        per_device, mesh=mesh, in_specs=in_specs, out_specs=out_specs, check_vma=False
    )
```
